32 devices in a mesh: dp: 8 (over z, x), seq: 4 (over y, core).
Axes of the slice: x: 2, y: 2, z: 4, core: 2. Of those that a mesh axis runs over, the one named last changes fastest.
Arguments:
- tokens: bfloat16 [8192, 768], P(('dp', 'seq')), may hold values from -6 to 6
- cotangent: bfloat16 [8192, 768], P(('dp', 'seq')), may hold values from -6 to 6
- lengths: int32 [8, 15], P('dp'), may hold values from 1 to 1010, as said below
- input_weight: bfloat16 [768, 2304], replicated, may hold values from -0.21875 to 0.21875
- output_weight: bfloat16 [768, 768], replicated, may hold values from -3.5 to 3.5
- gate_weight: bfloat16 [768, 3072], replicated, may hold values from -0.21875 to 0.21875
- up_weight: bfloat16 [768, 3072], replicated, may hold values from -0.21875 to 0.21875
- down_weight: bfloat16 [3072, 768], replicated, may hold values from -0.109375 to 0.109375
- gain_one: float32 [768], replicated, may hold values from 0.5 to 1.5
- bias_one: float32 [768], replicated, may hold values from -3 to 3
- gain_two: float32 [768], replicated, may hold values from 0.5 to 1.5
- bias_two: float32 [768], replicated, may hold values from -3 to 3
Outputs:
- output: bfloat16 [8192, 768], P(('dp', 'seq'))
- grad_tokens: bfloat16 [8192, 768], P(('dp', 'seq'))
- grad_input_weight: float32 [768, 2304], P('dp', 'seq')
- grad_output_weight: float32 [768, 768], P('dp', 'seq')
- grad_gate_weight: float32 [768, 3072], P('dp', 'seq')
- grad_up_weight: float32 [768, 3072], P('dp', 'seq')
- grad_down_weight: float32 [3072, 768], P('dp', 'seq')
- grad_gain_one: float32 [768], replicated
- grad_bias_one: float32 [768], replicated
- grad_gain_two: float32 [768], replicated
- grad_bias_two: float32 [768], replicated
The draws below stay inside these ranges and needn't reach their ends.
Inputs may be any that keep to these rules, and one draw needn't show every extreme that they name: Each window's 15 lengths sum to 1024. The first (15 - 1) / 2 and the last (15 - 1) / 2 of them each add up to fewer than 256 tokens.
All inputs are finite; a program needn't handle non-finite values.
Results may differ from the reference program's by a relative error of at most 0.024.
Values may be sent and summed in bfloat16 or wider, within the bound.
No kernel may reach another device: no remote copies, remote signals or barrier semaphores. Data moves between devices by JAX's collectives and lax.ppermute only.
A program may use at most 192 MiB of HBM per device.

```python
import math
import jax
import jax.numpy as jnp
from jax import lax

D = 768
HEADS = 12
HEAD = 64
FF = 3072
DOCS = 15
WIN = 1024
ROWS = 256
TOKENS = 8192
N_DP = 8


def draw_lengths(key, part):
    key = jax.random.fold_in(key, 11)
    side = (DOCS - 1) // 2
    longest = max(1, (ROWS - 1) // side)
    first_key, second_key = jax.random.split(key)
    first = jax.random.randint(first_key, (N_DP, DOCS - 1), 1, longest + 1)
    second = jax.random.randint(second_key, (N_DP, DOCS - 1), 1, longest + 1)
    short = jnp.minimum(first, second).astype(jnp.int32)
    window_index = jnp.arange(N_DP, dtype=jnp.int32)[:, None]
    short = jnp.where(window_index == 0, 1, short).astype(jnp.int32)
    middle = (WIN - jnp.sum(short, axis=1, keepdims=True)).astype(jnp.int32)
    return jnp.concatenate([short[:, :side], middle, short[:, side:]], axis=1).astype(jnp.int32)


def raised(drawn, own_key, source, target, shards_of, factor):
    owner, partner = [(jnp.arange(drawn.shape[dim]) // (drawn.shape[dim] // shards_of)).reshape([-1 if axis == dim else 1 for axis in range(drawn.ndim)]) for dim in (source, target)]
    chosen = jax.random.permutation(own_key, shards_of)[partner]
    strong = (owner == chosen) | (owner == (partner + shards_of // 2) % shards_of)
    return jnp.where(strong, factor * drawn, drawn)


def steps_of(key, shape, pieces, least, high):
    def one(dim, shards_of):
        heights = jax.random.uniform(jax.random.fold_in(jax.random.fold_in(key, 6), dim), (shards_of,), jnp.float32, least / len(pieces), high / len(pieces))
        return jnp.repeat(jnp.exp(heights), shape[dim] // shards_of).reshape((-1,) + (1,) * (len(shape) - dim - 1))

    loudness = one(*pieces[0])
    for cut in pieces[1:]:
        loudness = loudness * one(*cut)
    return loudness


def noise(own_key, dims, width, reach, pieces=(), kind=jnp.bfloat16):
    entries = width * jax.random.normal(own_key, dims, jnp.float32)
    if pieces:
        entries = entries * steps_of(own_key, dims, pieces, -0.22, 0.18)
    return jnp.clip(entries, -reach, reach).astype(kind)


def gaussian_with(rng, extent, deviation, reach, shards, heavy, kind=jnp.bfloat16):
    array = deviation * jax.random.normal(rng, extent, jnp.float32)
    if shards:
        array = array * steps_of(rng, extent, shards, -0.22, 0.18)
    return jnp.clip(raised(array, jax.random.fold_in(rng, 3), *heavy), -reach, reach).astype(kind)


def setup_inputs(seed: int = 0) -> dict:
    key_list = jax.random.split(jax.random.key(seed), 13)
    return {
        "tokens": noise(key_list[0], (TOKENS, D), 1.0, 6.0, ((0, 32),)),
        "cotangent": gaussian_with(key_list[1], (TOKENS, D), 1.0, 6.0, ((0, 32),), (0, 1, 32, 2.75)),
        "lengths": draw_lengths(jax.random.fold_in(key_list[12], 71), 0),
        "input_weight": noise(key_list[3], (D, 3 * D), D ** -0.5, 0.21875),
        "output_weight": noise(key_list[4], (D, D), (4 * D / WIN) ** -0.5, 3.5),
        "gate_weight": noise(key_list[5], (D, FF), D ** -0.5, 0.21875),
        "up_weight": noise(key_list[6], (D, FF), D ** -0.5, 0.21875),
        "down_weight": noise(key_list[7], (FF, D), FF ** -0.5, 0.109375),
        "gain_one": jnp.clip(1.0 + 0.1 * jax.random.normal(key_list[8], (D,), jnp.float32), 0.5, 1.5),
        "bias_one": noise(key_list[9], (D,), 0.5, 3.0, (), jnp.float32),
        "gain_two": jnp.clip(1.0 + 0.1 * jax.random.normal(key_list[10], (D,), jnp.float32), 0.5, 1.5),
        "bias_two": noise(key_list[11], (D,), 0.5, 3.0, (), jnp.float32),
    }


@jax.custom_vjp
def low(v):
    return lax.optimization_barrier(v.astype(jnp.bfloat16)).astype(jnp.float32)

@jax.custom_vjp
def low_back(v):
    return v

def low_keep(v):
    return (low(v), None)

def low_pass(kept, grad):
    return (grad,)

def back_keep(v):
    return (v, None)

def back_low(kept, grad):
    return (low(grad),)
low.defvjp(low_keep, low_pass)
low_back.defvjp(back_keep, back_low)
norm_eps = 1e-05
rotary_base = 1000.0
masked_value = -1e+30
highest = lax.Precision.HIGHEST

def doc_layout(lengths_row, count):
    ends = jnp.cumsum(lengths_row).astype(jnp.int32)
    place = jnp.arange(count, dtype=jnp.int32)
    after = (place[:, None] >= ends[None, :]).astype(jnp.int32)
    segment = lax.optimization_barrier(jnp.sum(after, axis=1)).astype(jnp.int32)
    start = lax.optimization_barrier(jnp.sum(after * lengths_row[None, :], axis=1)).astype(jnp.int32)
    return (segment, (place - start).astype(jnp.int32))

def rotate(field, position):
    half = field.shape[-1] // 2
    freq = rotary_base ** (-jnp.arange(half, dtype=jnp.float32) * (2.0 / field.shape[-1]))
    angle = position.astype(jnp.float32)[:, None] * freq[None, :]
    cosine = jnp.cos(angle)[:, None, :]
    sine = jnp.sin(angle)[:, None, :]
    first = field[..., :half]
    second = field[..., half:]
    return jnp.concatenate([first * cosine - second * sine, second * cosine + first * sine], axis=-1)

def layer_norm(value, gain, shift):
    mean = lax.optimization_barrier(jnp.mean(value, axis=-1, keepdims=True))
    centred = value - mean
    spread = lax.optimization_barrier(jnp.mean(centred * centred, axis=-1, keepdims=True))
    return centred * lax.rsqrt(spread + norm_eps) * gain + shift

def reference(tokens, cotangent, lengths, input_weight, output_weight, gate_weight, up_weight, down_weight, gain_one, bias_one, gain_two, bias_two):
    segment, position = jax.vmap(lambda row: doc_layout(row, WIN))(lengths)
    block = math.gcd(WIN, 512)
    scale = 1.0 / math.sqrt(HEAD)

    def one_window(params, item):
        in_matrix, out_matrix, gate_matrix, up_matrix, down_matrix, norm_gain, norm_bias, last_gain, last_bias = params
        window_rows, seg_row, pos_row = item
        projected = low_back(jnp.dot(window_rows, in_matrix, precision=highest))
        query = low(rotate(projected[:, :D].reshape(WIN, HEADS, HEAD), pos_row))
        key = low(rotate(projected[:, D:2 * D].reshape(WIN, HEADS, HEAD), pos_row))
        value = low(projected[:, 2 * D:].reshape(WIN, HEADS, HEAD))

        def attend(piece):
            query_block, seg_block = piece
            scores = low_back(jnp.einsum('qhe,khe->hqk', query_block, key, precision=highest) * scale)
            same = (seg_block[:, None] == seg_row[None, :])[None]
            masked = jnp.where(same, scores, masked_value)
            peak = lax.optimization_barrier(jnp.max(masked, axis=-1, keepdims=True))
            weight = jnp.where(same, jnp.exp(masked - peak), 0.0)
            prob = low(weight / lax.optimization_barrier(jnp.sum(weight, axis=-1, keepdims=True)))
            return jnp.einsum('hqk,khe->qhe', prob, value, precision=highest)
        attended = lax.map(jax.checkpoint(attend), (query.reshape(WIN // block, block, HEADS, HEAD), seg_row.reshape(WIN // block, block)))
        attended = low_back(low(attended.reshape(WIN, D)))
        first = window_rows + low_back(jnp.dot(attended, out_matrix, precision=highest))
        normed = layer_norm(first, norm_gain, norm_bias)
        normed_low = low(normed)
        gate = low_back(jnp.dot(normed_low, gate_matrix, precision=highest))
        upward = low_back(jnp.dot(normed_low, up_matrix, precision=highest))
        hidden = low(jax.nn.silu(gate) * upward)
        second = normed + low_back(jnp.dot(hidden, down_matrix, precision=highest))
        return layer_norm(second, last_gain, last_bias)

    def forward(inputs, in_matrix, out_matrix, gate_matrix, up_matrix, down_matrix, norm_gain, norm_bias, last_gain, last_bias):
        params = (in_matrix, out_matrix, gate_matrix, up_matrix, down_matrix, norm_gain, norm_bias, last_gain, last_bias)
        windows = inputs.reshape(N_DP, WIN, D)
        result = lax.map(jax.checkpoint(lambda item: one_window(params, item)), (windows, segment, position))
        return result.reshape(N_DP * WIN, D)
    primal, pullback = jax.vjp(forward, tokens.astype(jnp.float32), input_weight.astype(jnp.float32), output_weight.astype(jnp.float32), gate_weight.astype(jnp.float32), up_weight.astype(jnp.float32), down_weight.astype(jnp.float32), gain_one, bias_one, gain_two, bias_two)
    grads = pullback(cotangent.astype(jnp.float32))
    return (primal.astype(jnp.bfloat16), grads[0].astype(jnp.bfloat16), grads[1], grads[2], grads[3], grads[4], grads[5], grads[6], grads[7], grads[8], grads[9])
```

```python
import functools
import math

import jax
import jax.numpy as jnp
import numpy as np
from jax import lax
from jax.experimental import pallas as pl
from jax.experimental.pallas import tpu as pltpu
from jax.sharding import PartitionSpec as P

HEAD = 64


norm_eps = 1e-05
rotary_base = 1000.0
masked_value = -1e30


def doc_layout(lengths_row, count):
    ends = jnp.cumsum(lengths_row)
    place = jnp.arange(count, dtype=jnp.int32)
    after = (place[:, None] >= ends[None, :]).astype(jnp.int32)
    segment = jnp.sum(after, axis=1)
    start = jnp.sum(after * lengths_row[None, :], axis=1)
    return (segment, place - start)


def rotate(field, position):
    half = field.shape[-1] // 2
    freq = rotary_base ** (-jnp.arange(half, dtype=jnp.float32) * (2.0 / field.shape[-1]))
    angle = position.astype(jnp.float32)[:, None] * freq[None, :]
    cosine = jnp.cos(angle)[:, None, :]
    sine = jnp.sin(angle)[:, None, :]
    first = field[..., :half]
    second = field[..., half:]
    return jnp.concatenate(
        [first * cosine - second * sine, second * cosine + first * sine], axis=-1
    )


def norm_forward(value, gain, shift):
    mean = jnp.mean(value, axis=-1, keepdims=True)
    centred = value - mean
    inverse = lax.rsqrt(jnp.mean(centred * centred, axis=-1, keepdims=True) + norm_eps)
    scaled = centred * inverse
    return (scaled * gain + shift, scaled, inverse)


def norm_backward(grad, scaled, inverse, gain):
    inner = grad * gain
    back = inverse * (
        inner
        - jnp.mean(inner, axis=-1, keepdims=True)
        - scaled * jnp.mean(inner * scaled, axis=-1, keepdims=True)
    )
    return (back, jnp.sum(grad * scaled, axis=0), jnp.sum(grad, axis=0))


def inner_rows(left, right):
    return lax.dot_general(
        left, right, (((0,), (0,)), ((), ())), preferred_element_type=jnp.float32
    )


def times_transpose(left, right):
    return lax.dot_general(
        left, right, (((1,), (1,)), ((), ())), preferred_element_type=jnp.float32
    )


def general(
    tokens,
    cotangent,
    lengths,
    input_weight,
    output_weight,
    gate_weight,
    up_weight,
    down_weight,
    gain_one,
    bias_one,
    gain_two,
    bias_two,
):
    rows, width = tokens.shape
    heads = width // HEAD
    window = rows * lax.axis_size("seq")
    scale = 1.0 / math.sqrt(HEAD)
    segment_all, position_all = doc_layout(lengths[0], window)
    offset = lax.axis_index("seq") * rows
    seg_mine = lax.dynamic_slice_in_dim(segment_all, offset, rows)
    pos_mine = lax.dynamic_slice_in_dim(position_all, offset, rows)
    projected = jnp.dot(tokens, input_weight, preferred_element_type=jnp.float32)
    query = rotate(projected[:, :width].reshape(rows, heads, HEAD), pos_mine).astype(jnp.bfloat16)
    key = (
        rotate(projected[:, width : 2 * width].reshape(rows, heads, HEAD), pos_mine)
        .astype(jnp.bfloat16)
        .reshape(rows, width)
    )
    value = projected[:, 2 * width :].astype(jnp.bfloat16)

    def scores_for(key_block, seg_block):
        scores = (
            jnp.einsum("qhe,khe->hqk", query, key_block, preferred_element_type=jnp.float32) * scale
        )
        same = (seg_mine[:, None] == seg_block[None, :])[None]
        return (jnp.where(same, scores, masked_value), same)

    def split_blocks(piece, segs):
        count = piece[0].shape[0]
        size = math.gcd(count, 512)
        keys = piece[0].reshape(count // size, size, heads, HEAD)
        values = piece[1].reshape(count // size, size, heads, HEAD)
        return (keys, values, segs.reshape(count // size, size), count, size)

    start_state = (
        jnp.zeros((rows, heads, HEAD), jnp.float32),
        jnp.full((heads, rows), masked_value, jnp.float32),
        jnp.zeros((heads, rows), jnp.float32),
    )
    segs = segment_all
    keys, values, seg_blocks, count, size = split_blocks(
        (
            lax.all_gather(key, "seq", axis=0, tiled=True),
            lax.all_gather(value, "seq", axis=0, tiled=True),
        ),
        segs,
    )

    def forward_step(state, item):
        summed, peak, total = state
        key_block, value_block, seg_block = item
        scores, same = scores_for(key_block, seg_block)
        new_peak = jnp.maximum(peak, jnp.max(scores, axis=-1))
        fade = jnp.exp(peak - new_peak)
        weight = jnp.where(same, jnp.exp(scores - new_peak[..., None]), 0.0)
        total = total * fade + jnp.sum(weight, axis=-1)
        summed = summed * fade.T[..., None] + jnp.einsum(
            "hqk,khe->qhe",
            weight.astype(jnp.bfloat16),
            value_block,
            preferred_element_type=jnp.float32,
        )
        return ((summed, new_peak, total), None)

    state, unused = lax.scan(forward_step, start_state, (keys, values, seg_blocks))
    summed, peak, total = state
    attended = (summed / total.T[..., None]).reshape(rows, width)
    attended_low = attended.astype(jnp.bfloat16)
    first = tokens.astype(jnp.float32) + jnp.dot(
        attended_low, output_weight, preferred_element_type=jnp.float32
    )
    normed, scaled_one, inverse_one = norm_forward(first, gain_one, bias_one)
    normed_low = normed.astype(jnp.bfloat16)
    gate = jnp.dot(normed_low, gate_weight, preferred_element_type=jnp.float32)
    upward = jnp.dot(normed_low, up_weight, preferred_element_type=jnp.float32)
    sigma = jax.nn.sigmoid(gate)
    activated = gate * sigma
    hidden_low = (activated * upward).astype(jnp.bfloat16)
    second = normed + jnp.dot(hidden_low, down_weight, preferred_element_type=jnp.float32)
    result, scaled_two, inverse_two = norm_forward(second, gain_two, bias_two)
    grad_second, grad_gain_two, grad_bias_two = norm_backward(
        cotangent.astype(jnp.float32), scaled_two, inverse_two, gain_two
    )
    grad_ff_low = grad_second.astype(jnp.bfloat16)
    grad_hidden = times_transpose(grad_ff_low, down_weight)
    grad_gate_low = (grad_hidden * upward * (sigma * (1.0 + gate * (1.0 - sigma)))).astype(
        jnp.bfloat16
    )
    grad_up_low = (grad_hidden * activated).astype(jnp.bfloat16)
    grad_normed = (
        grad_second
        + times_transpose(grad_gate_low, gate_weight)
        + times_transpose(grad_up_low, up_weight)
    )
    grad_first, grad_gain_one, grad_bias_one = norm_backward(
        grad_normed, scaled_one, inverse_one, gain_one
    )
    grad_branch_low = grad_first.astype(jnp.bfloat16)
    grad_attended_low = times_transpose(grad_branch_low, output_weight).astype(jnp.bfloat16)
    grad_heads = grad_attended_low.reshape(rows, heads, HEAD)
    delta = jnp.sum(
        (grad_attended_low.astype(jnp.float32) * attended).reshape(rows, heads, HEAD), axis=-1
    ).T
    zero_query = jnp.zeros((rows, heads, HEAD), jnp.float32)
    grad_acc = zero_query
    segs = segment_all
    grad_query = grad_acc
    keys, values, seg_blocks, count, size = split_blocks(
        (
            lax.all_gather(key, "seq", axis=0, tiled=True),
            lax.all_gather(value, "seq", axis=0, tiled=True),
        ),
        segs,
    )

    def backward_step(grad_acc, item):
        key_block, value_block, seg_block = item
        scores, same = scores_for(key_block, seg_block)
        prob = jnp.where(same, jnp.exp(scores - peak[..., None]) / total[..., None], 0.0)
        prob_grad = jnp.einsum(
            "qhe,khe->hqk", grad_heads, value_block, preferred_element_type=jnp.float32
        )
        score_grad = (prob * (prob_grad - delta[..., None])).astype(jnp.bfloat16)
        grad_acc = (
            grad_acc
            + jnp.einsum("hqk,khe->qhe", score_grad, key_block, preferred_element_type=jnp.float32)
            * scale
        )
        prob_low = prob.astype(jnp.bfloat16)
        key_grad = (
            jnp.einsum("hqk,qhe->khe", score_grad, query, preferred_element_type=jnp.float32)
            * scale
        )
        value_grad = jnp.einsum(
            "hqk,qhe->khe", prob_low, grad_heads, preferred_element_type=jnp.float32
        )
        return (grad_acc, (key_grad.reshape(size, width), value_grad.reshape(size, width)))

    grad_query, outputs = lax.scan(backward_step, grad_query, (keys, values, seg_blocks))
    grad_acc = grad_query
    key_part = outputs[0].reshape(count, width)
    value_part = outputs[1].reshape(count, width)
    grad_key, grad_value = (
        lax.psum_scatter(
            key_part.astype(jnp.bfloat16), "seq", scatter_dimension=0, tiled=True
        ).astype(jnp.float32),
        lax.psum_scatter(
            value_part.astype(jnp.bfloat16), "seq", scatter_dimension=0, tiled=True
        ).astype(jnp.float32),
    )
    query_back = rotate(grad_acc, -pos_mine).reshape(rows, width)
    key_back = rotate(grad_key.reshape(rows, heads, HEAD), -pos_mine).reshape(rows, width)
    grad_projected_low = jnp.concatenate([query_back, key_back, grad_value], axis=1).astype(
        jnp.bfloat16
    )
    grad_tokens = (grad_first + times_transpose(grad_projected_low, input_weight)).astype(
        jnp.bfloat16
    )
    column_grads = (
        lax.all_to_all(grad_projected_low, "seq", split_axis=1, concat_axis=0, tiled=True),
        lax.all_to_all(grad_branch_low, "seq", split_axis=1, concat_axis=0, tiled=True),
        lax.all_to_all(grad_gate_low, "seq", split_axis=1, concat_axis=0, tiled=True),
        lax.all_to_all(grad_up_low, "seq", split_axis=1, concat_axis=0, tiled=True),
        lax.all_to_all(grad_ff_low, "seq", split_axis=1, concat_axis=0, tiled=True),
    )
    tok_rows = lax.all_gather(tokens, "seq", axis=0, tiled=True)
    normed_rows = lax.all_gather(normed_low, "seq", axis=0, tiled=True)
    attended_rows = lax.all_gather(attended_low, "seq", axis=0, tiled=True)
    hidden_rows = lax.all_gather(hidden_low, "seq", axis=0, tiled=True)
    count = tok_rows.shape[0]
    cols = [member for member in column_grads]
    summed_grads = (
        lax.psum_scatter(
            inner_rows(tok_rows, cols[0]).astype(jnp.bfloat16),
            "dp",
            scatter_dimension=0,
            tiled=True,
        ).astype(jnp.float32),
        lax.psum_scatter(
            inner_rows(attended_rows, cols[1]).astype(jnp.bfloat16),
            "dp",
            scatter_dimension=0,
            tiled=True,
        ).astype(jnp.float32),
        lax.psum_scatter(
            inner_rows(normed_rows, cols[2]).astype(jnp.bfloat16),
            "dp",
            scatter_dimension=0,
            tiled=True,
        ).astype(jnp.float32),
        lax.psum_scatter(
            inner_rows(normed_rows, cols[3]).astype(jnp.bfloat16),
            "dp",
            scatter_dimension=0,
            tiled=True,
        ).astype(jnp.float32),
        lax.psum_scatter(
            inner_rows(hidden_rows, cols[4]).astype(jnp.bfloat16),
            "dp",
            scatter_dimension=0,
            tiled=True,
        ).astype(jnp.float32),
    )
    norm_grads = lax.psum(
        (grad_gain_one, grad_bias_one, grad_gain_two, grad_bias_two), ("dp", "seq")
    )
    return (
        result.astype(jnp.bfloat16),
        grad_tokens,
        summed_grads[0],
        summed_grads[1],
        summed_grads[2],
        summed_grads[3],
        summed_grads[4],
        norm_grads[0],
        norm_grads[1],
        norm_grads[2],
        norm_grads[3],
    )


low = jnp.bfloat16
full = jnp.float32
TILE = 128
MIB = 1024 * 1024


def nn(left, right):
    return lax.dot_general(
        left, right, (((1,), (0,)), ((), ())), preferred_element_type=jnp.float32
    )


def nt(left, right):
    return lax.dot_general(
        left, right, (((1,), (1,)), ((), ())), preferred_element_type=jnp.float32
    )


def whole(shape):
    return pl.BlockSpec(tuple(shape), lambda *unused: (0,) * len(shape))


def shaped(shape, kind):
    return jax.ShapeDtypeStruct(tuple(shape), kind)


def settings(mib, axes=0):
    return pltpu.CompilerParams(
        vmem_limit_bytes=mib * MIB, dimension_semantics=("arbitrary",) * axes if axes else None
    )


def cost(flops, moved, exps=0):
    return pl.CostEstimate(flops=int(flops), bytes_accessed=int(moved), transcendentals=int(exps))


def turn(field, cosine, sine):
    lane = lax.broadcasted_iota(jnp.int32, field.shape, 1)
    half = HEAD // 2
    other = jnp.where(
        lane % HEAD < half, pltpu.roll(field, TILE - half, 1), pltpu.roll(field, half, 1)
    )
    return field * cosine + other * sine


def head_lanes(rows, which):
    lane = lax.broadcasted_iota(jnp.int32, (rows, TILE), 1)
    return (lane // HEAD) == which


def put_keys(tokens, key_weight, value_weight, cosine, sine, keys, values, start):
    rows, width = tokens.shape
    projected = nn(tokens, key_weight)
    for tile in range(width // TILE):
        cols = slice(tile * TILE, (tile + 1) * TILE)
        keys[start : start + rows, cols] = turn(projected[:, cols], cosine, sine).astype(low)
    values[start : start + rows, :] = nn(tokens, value_weight).astype(low)


def attend_head(query_pair, key_pair, value_pair, bias, which):
    rows = query_pair.shape[0]
    query = jnp.where(head_lanes(rows, which), query_pair, jnp.zeros_like(query_pair))
    scores = nt(query, key_pair) + bias
    peak = jnp.max(scores, axis=1, keepdims=True)
    weight = jnp.exp(scores - peak)
    total = jnp.sum(weight, axis=1, keepdims=True)
    return nn(weight.astype(low), value_pair), peak, total


def first_half(
    own, near, wq, wk, wv, cosine, sine, seg_query, seg_key, query, acc, peak, total, keys, values, bias
):
    rows, width = own.shape
    scale = 1.0 / math.sqrt(HEAD)
    projected = nn(own[...], wq[...])
    for tile in range(width // TILE):
        cols = slice(tile * TILE, (tile + 1) * TILE)
        turned = turn(projected[:, cols], cosine[:rows, :], sine[:rows, :])
        query[:, cols] = (turned.astype(low) * scale).astype(low)
    put_keys(own[...], wk[...], wv[...], cosine[:rows, :], sine[:rows, :], keys, values, 0)
    put_keys(near[...], wk[...], wv[...], cosine[rows:, :], sine[rows:, :], keys, values, rows)
    bias[...] = jnp.where(seg_query[:, :1] == seg_key[...], 0.0, masked_value)
    lane = lax.broadcasted_iota(jnp.int32, (rows, TILE), 1)
    peaks = jnp.zeros((rows, TILE), jnp.float32)
    totals = jnp.zeros((rows, TILE), jnp.float32)
    for tile in range(width // TILE):
        cols = slice(tile * TILE, (tile + 1) * TILE)
        parts = []
        for which in range(TILE // HEAD):
            out, top, norm = attend_head(
                query[:, cols], keys[:, cols], values[:, cols], bias[...], which
            )
            parts.append(out)
            here = lane == tile * (TILE // HEAD) + which
            peaks = jnp.where(here, top, peaks)
            totals = jnp.where(here, norm, totals)
        acc[:, cols] = jnp.where(head_lanes(rows, 0), parts[0], parts[1])
    peak[...] = peaks
    total[...] = totals


def second_half(
    own, far, far_near, wk, wv, wo, cosine, sine, seg_query, seg_key, query, acc, peak, total, gain, shift,
    attended_low, normed, normed_low, scaled, inverse, keys, values, bias,
):
    rows, width = own.shape
    put_keys(far[...], wk[...], wv[...], cosine[:rows, :], sine[:rows, :], keys, values, 0)
    put_keys(far_near[...], wk[...], wv[...], cosine[rows:, :], sine[rows:, :], keys, values, rows)
    bias[...] = jnp.where(seg_query[:, :1] == seg_key[...], 0.0, masked_value)
    for tile in range(width // TILE):
        cols = slice(tile * TILE, (tile + 1) * TILE)
        parts = []
        for which in range(TILE // HEAD):
            head = tile * (TILE // HEAD) + which
            out, top, norm = attend_head(
                query[:, cols], keys[:, cols], values[:, cols], bias[...], which
            )
            before = peak[:, head : head + 1]
            best = jnp.maximum(before, top)
            fade = jnp.exp(before - best)
            grow = jnp.exp(top - best)
            norm = total[:, head : head + 1] * fade + norm * grow
            parts.append((acc[:, cols] * fade + out * grow) / norm)
        both = jnp.where(head_lanes(rows, 0), parts[0], parts[1])
        attended_low[:, cols] = both.astype(low)
    first = own[...].astype(jnp.float32) + nn(attended_low[...], wo[...])
    mean = jnp.mean(first, axis=1, keepdims=True)
    centred = first - mean
    spread = lax.rsqrt(jnp.mean(centred * centred, axis=1, keepdims=True) + norm_eps)
    unit = centred * spread
    value = unit * gain[...] + shift[...]
    scaled[...] = unit
    inverse[...] = jnp.broadcast_to(spread, (rows, TILE))
    normed[...] = value
    normed_low[...] = value.astype(low)


def feed_forward(
    normed, normed_low, wg, wu, wd, cotangent, gain, shift,
    slope_up, slope_gate, result, grad_second, grad_low, sums, acc,
):
    step = pl.program_id(0)
    gate = nn(normed_low[...], wg[...])
    upward = nn(normed_low[...], wu[...])
    sigma = jax.nn.sigmoid(gate)
    active = gate * sigma
    slope_up[...] = active.astype(low)
    slope_gate[...] = (upward * (sigma * (1.0 + gate * (1.0 - sigma)))).astype(low)
    product = nn((active * upward).astype(low), wd[...])

    @pl.when(step == 0)
    def _():
        acc[...] = normed[...] + product

    @pl.when(step > 0)
    def _():
        acc[...] += product

    @pl.when(step == pl.num_programs(0) - 1)
    def _():
        second = acc[...]
        mean = jnp.mean(second, axis=1, keepdims=True)
        centred = second - mean
        spread = lax.rsqrt(jnp.mean(centred * centred, axis=1, keepdims=True) + norm_eps)
        unit = centred * spread
        result[...] = (unit * gain[...] + shift[...]).astype(low)
        grad = cotangent[...].astype(jnp.float32)
        inner = grad * gain[...]
        back = spread * (
            inner
            - jnp.mean(inner, axis=1, keepdims=True)
            - unit * jnp.mean(inner * unit, axis=1, keepdims=True)
        )
        grad_second[...] = back
        grad_low[...] = back.astype(low)
        sums[0:1, :] = jnp.sum(grad * unit, axis=0, keepdims=True)
        sums[1:2, :] = jnp.sum(grad, axis=0, keepdims=True)


def feed_back(
    grad_second, grad_low, slope_up, slope_gate, wg, wu, wd, wo, scaled, inverse, gain,
    grad_first, branch_low, attended_grad, sums, acc,
):
    step = pl.program_id(0)
    hidden = nt(grad_low[...], wd[...])
    gate = (hidden * slope_gate[...].astype(jnp.float32)).astype(low)
    upward = (hidden * slope_up[...].astype(jnp.float32)).astype(low)
    product = nt(gate, wg[...]) + nt(upward, wu[...])

    @pl.when(step == 0)
    def _():
        acc[...] = grad_second[...] + product

    @pl.when(step > 0)
    def _():
        acc[...] += product

    @pl.when(step == pl.num_programs(0) - 1)
    def _():
        grad = acc[...]
        unit = scaled[...]
        inner = grad * gain[...]
        back = inverse[:, :1] * (
            inner
            - jnp.mean(inner, axis=1, keepdims=True)
            - unit * jnp.mean(inner * unit, axis=1, keepdims=True)
        )
        grad_first[...] = back
        branch_low[...] = back.astype(low)
        attended_grad[...] = nt(branch_low[...], wo[...]).astype(low)
        sums[0:1, :] = jnp.sum(grad * unit, axis=0, keepdims=True)
        sums[1:2, :] = jnp.sum(grad, axis=0, keepdims=True)


def column_grads(
    place, *refs,
):
    count = 4
    normed, grads = refs[:count], refs[count : 2 * count]
    wgu, wd = refs[2 * count : 2 * count + 2]
    keep_io, send_io, keep_down, send_down, acc_io, acc_down, turned_io, turned_down = refs[2 * count + 2 :]
    half = wd.shape[0]
    width = wd.shape[1]
    for step in range(count):
        rows = normed[step][...]
        back = grads[step][...]
        both = nt(wgu[...], rows)
        gate, upward = both[:half], both[half:]
        sigma = jax.nn.sigmoid(gate)
        active = gate * sigma
        hidden = (active * upward).astype(low)
        grad_hidden = nt(wd[...], back)
        grad_gate = (grad_hidden * upward * (sigma * (1.0 + gate * (1.0 - sigma)))).astype(low)
        grad_up = (grad_hidden * active).astype(low)
        down = nn(hidden, back)
        gates = nn(grad_gate, rows)
        ups = nn(grad_up, rows)
        if step == 0:
            acc_down[...] = down
            acc_io[:half, :] = gates
            acc_io[half:, :] = ups
        else:
            acc_down[...] += down
            acc_io[:half, :] += gates
            acc_io[half:, :] += ups
    turned_io[...] = acc_io[...].T
    turned_down[...] = acc_down[...].T
    rows = width // 4
    bit = place[0]
    for upper in range(2):
        mine = pl.ds(pl.multiple_of((2 * upper + bit) * rows, rows), rows)
        other = pl.ds(pl.multiple_of((2 * upper + 1 - bit) * rows, rows), rows)
        out = slice(upper * rows, (upper + 1) * rows)
        keep_io[out, :] = turned_io[mine, :]
        send_io[out, :] = turned_io[other, :].astype(low)
        keep_down[out, :] = turned_down[mine, :]
        send_down[out, :] = turned_down[other, :].astype(low)


def attend_back(
    place, own, near, far, far_near, wq, wk, wv, own_grad, far_grad, cosine, sine, seg_key, seg_query,
    dq_own, dq_far, keep, send, keys, values, query, bias,
):
    rows = own.shape[0]
    width = wq.shape[1]
    scale = 1.0 / math.sqrt(HEAD)
    blocks = (own, near, far, far_near)
    for index, block in enumerate(blocks):
        part = slice(index * rows, (index + 1) * rows)
        tokens = block[...]
        projected = nn(tokens, wk[...])
        for tile in range(width // TILE):
            cols = slice(tile * TILE, (tile + 1) * TILE)
            keys[part, cols] = turn(projected[:, cols], cosine[part, :], sine[part, :]).astype(low)
        values[part, :] = nn(tokens, wv[...]).astype(low)
        if index % 2 == 0:
            projected = nn(tokens, wq[...])
            to = slice(index // 2 * rows, (index // 2 + 1) * rows)
            for tile in range(width // TILE):
                cols = slice(tile * TILE, (tile + 1) * TILE)
                turned = turn(projected[:, cols], cosine[part, :], sine[part, :])
                query[to, cols] = (turned.astype(low) * scale).astype(low)
            bias[:, to] = jnp.where(seg_key[:, :1] == seg_query[:, part], 0.0, masked_value)
    for tile in range(width // TILE):
        cols = slice(tile * TILE, (tile + 1) * TILE)
        key_pair = keys[:, cols]
        value_pair = values[:, cols]
        key_turned = key_pair.astype(jnp.float32).T.astype(low)
        grad_key = None
        grad_value = None
        for index, (grads, out) in enumerate(((own_grad, dq_own), (far_grad, dq_far))):
            part = slice(index * rows, (index + 1) * rows)
            query_pair = query[part, cols]
            grad_pair = grads[:, cols]
            pieces = []
            for which in range(TILE // HEAD):
                mask = head_lanes(rows, which)
                query_head = jnp.where(mask, query_pair, jnp.zeros_like(query_pair))
                grad_head = jnp.where(mask, grad_pair, jnp.zeros_like(grad_pair))
                scores = nt(key_pair, query_head) + bias[:, part]
                weight = jnp.exp(scores - jnp.max(scores, axis=0, keepdims=True))
                prob = weight * (1.0 / jnp.sum(weight, axis=0, keepdims=True))
                prob_grad = nt(value_pair, grad_head)
                both = prob * prob_grad
                delta = jnp.sum(both, axis=0, keepdims=True)
                score_grad = (both - prob * delta).astype(low)
                value_part = nn(prob.astype(low), grad_head)
                key_part = nn(score_grad, query_head)
                grad_key = key_part if grad_key is None else grad_key + key_part
                grad_value = value_part if grad_value is None else grad_value + value_part
                pieces.append(nn(key_turned, score_grad)[which * HEAD : (which + 1) * HEAD])
            grad_query = jnp.concatenate(pieces, axis=0).T * scale
            at = slice(2 * index * rows, (2 * index + 1) * rows)
            out[:, cols] = turn(grad_query, cosine[at, :], -sine[at, :]).astype(low)
        grad_key = turn(grad_key, cosine[...], -sine[...])
        shifted = slice(width + tile * TILE, width + (tile + 1) * TILE)
        for index in range(4):
            part = slice(index * rows, (index + 1) * rows)
            to = slice(index // 2 * rows, (index // 2 + 1) * rows)
            if index % 2 == 0:
                keep[to, cols] = grad_key[part]
                keep[to, shifted] = grad_value[part]
            else:
                send[to, cols] = grad_key[part].astype(low)
                send[to, shifted] = grad_value[part].astype(low)


def fast(
    tokens,
    cotangent,
    lengths,
    input_weight,
    output_weight,
    gate_weight,
    up_weight,
    down_weight,
    gain_one,
    bias_one,
    gain_two,
    bias_two,
):
    rows, width = tokens.shape
    hidden = gate_weight.shape[1]
    seq = lax.axis_index("seq")
    data = lax.axis_index("dp")
    n_seq, n_data = lax.axis_size("seq"), lax.axis_size("dp")
    core, side = seq % 2, seq // 2
    bit_x, bit_low, bit_high = data % 2, (data // 2) % 2, data // 4

    def swap(value, axis, bit):
        size = n_seq if axis == "seq" else n_data
        return lax.ppermute(value, axis, [(i, i ^ bit) for i in range(size)])

    def core_swap(value):
        return swap(value, "seq", 1)

    def side_swap(value):
        return swap(value, "seq", 2)

    def x_swap(value):
        return swap(value, "dp", 1)

    def diagonal_swap(value):
        return lax.ppermute(
            value,
            ("dp", "seq"),
            [
                (d * n_seq + s, (d ^ 1) * n_seq + (s ^ 2))
                for d in range(n_data)
                for s in range(n_seq)
            ],
        )

    far = side_swap(tokens)
    near = core_swap(tokens)
    far_near = core_swap(far)

    ends = jnp.cumsum(lengths[0])
    blocks = jnp.stack([seq ^ i for i in range(4)])
    spot = (blocks[:, None] * rows + jnp.arange(rows, dtype=jnp.int32)[None, :]).reshape(-1)
    after = (spot[:, None] >= ends[None, :]).astype(jnp.int32)
    segment = jnp.sum(after, axis=1)
    position = spot - jnp.sum(after * lengths[0][None, :], axis=1)
    half = HEAD // 2
    freq = rotary_base ** (-jnp.arange(half, dtype=jnp.float32) * (2.0 / HEAD))
    angle = freq[:, None] * position.astype(jnp.float32)[None, :]
    cosine, sine = lax.optimization_barrier((jnp.cos(angle).T, jnp.sin(angle).T))
    cosine = jnp.concatenate([cosine] * 4, axis=1)
    sine = jnp.concatenate([-sine, sine] * 2, axis=1)
    seg_col = jnp.broadcast_to(segment[:, None], (4 * rows, TILE))
    seg_row = segment[None, :]

    two = 2 * rows
    vec = lambda v: v.reshape(1, width)
    third = lambda i: pl.BlockSpec((width, width), lambda *unused: (0, i))
    query, acc, peak, total = pl.pallas_call(
        first_half,
        grid=(1,),
        in_specs=[
            whole((rows, width)), whole((rows, width)), third(0), third(1), third(2),
            whole((two, TILE)), whole((two, TILE)), whole((rows, TILE)), whole((1, two)),
        ],
        out_specs=[
            whole((rows, width)), whole((rows, width)), whole((rows, TILE)), whole((rows, TILE)),
        ],
        out_shape=[
            shaped((rows, width), low), shaped((rows, width), full),
            shaped((rows, TILE), full), shaped((rows, TILE), full),
        ],
        scratch_shapes=[
            pltpu.VMEM((two, width), low), pltpu.VMEM((two, width), low), pltpu.VMEM((rows, two), full),
        ],
        compiler_params=settings(40),
        cost_estimate=cost(5 * 2 * rows * width * width + 8 * rows * rows * width, 6 * MIB, 12 * rows * two),
        name="first_half",
    )(
        tokens, near, input_weight, input_weight, input_weight,
        cosine[:two], sine[:two], seg_col[:rows], seg_row[:, :two],
    )
    attended_low, normed, normed_low, scaled, inverse = pl.pallas_call(
        second_half,
        grid=(1,),
        in_specs=[
            whole((rows, width)), whole((rows, width)), whole((rows, width)), third(1), third(2),
            whole((width, width)), whole((two, TILE)), whole((two, TILE)), whole((rows, TILE)),
            whole((1, two)), whole((rows, width)), whole((rows, width)), whole((rows, TILE)),
            whole((rows, TILE)), whole((1, width)), whole((1, width)),
        ],
        out_specs=[
            whole((rows, width)), whole((rows, width)), whole((rows, width)), whole((rows, width)),
            whole((rows, TILE)),
        ],
        out_shape=[
            shaped((rows, width), low), shaped((rows, width), full), shaped((rows, width), low),
            shaped((rows, width), full), shaped((rows, TILE), full),
        ],
        scratch_shapes=[
            pltpu.VMEM((two, width), low), pltpu.VMEM((two, width), low), pltpu.VMEM((rows, two), full),
        ],
        compiler_params=settings(40),
        cost_estimate=cost(5 * 2 * rows * width * width + 8 * rows * rows * width, 6 * MIB, 12 * rows * two),
        name="second_half",
    )(
        tokens, far, far_near, input_weight, input_weight, output_weight,
        cosine[two:], sine[two:], seg_col[:rows], seg_row[:, two:], query, acc, peak, total,
        vec(gain_one), vec(bias_one),
    )

    def spread(value):
        sides = jnp.concatenate([side_swap(value), x_swap(value), diagonal_swap(value)], axis=0)
        return [value, core_swap(value), sides, core_swap(sides)]

    normed_parts = spread(normed_low)

    steps = 6
    chunk = hidden // steps
    slope_up, slope_gate, result, grad_second, grad_low, sums_two = pl.pallas_call(
        feed_forward,
        grid=(steps,),
        in_specs=[
            whole((rows, width)), whole((rows, width)),
            pl.BlockSpec((width, chunk), lambda j: (0, j)), pl.BlockSpec((width, chunk), lambda j: (0, j)),
            pl.BlockSpec((chunk, width), lambda j: (j, 0)),
            whole((rows, width)), whole((1, width)), whole((1, width)),
        ],
        out_specs=[
            pl.BlockSpec((rows, chunk), lambda j: (0, j)), pl.BlockSpec((rows, chunk), lambda j: (0, j)),
            whole((rows, width)), whole((rows, width)), whole((rows, width)), whole((2, width)),
        ],
        out_shape=[
            shaped((rows, hidden), low), shaped((rows, hidden), low), shaped((rows, width), low),
            shaped((rows, width), full), shaped((rows, width), low), shaped((2, width), full),
        ],
        scratch_shapes=[pltpu.VMEM((rows, width), full)],
        compiler_params=settings(32, 1),
        cost_estimate=cost(6 * rows * width * hidden, 18 * MIB, rows * hidden),
        name="feed_forward",
    )(
        normed, normed_low, gate_weight, up_weight, down_weight, cotangent, vec(gain_two), vec(bias_two),
    )
    grad_parts = spread(grad_low)
    grad_first, branch_low, attended_grad, sums_one = pl.pallas_call(
        feed_back,
        grid=(steps,),
        in_specs=[
            whole((rows, width)), whole((rows, width)),
            pl.BlockSpec((rows, chunk), lambda j: (0, j)), pl.BlockSpec((rows, chunk), lambda j: (0, j)),
            pl.BlockSpec((width, chunk), lambda j: (0, j)), pl.BlockSpec((width, chunk), lambda j: (0, j)),
            pl.BlockSpec((chunk, width), lambda j: (j, 0)), whole((width, width)),
            whole((rows, width)), whole((rows, TILE)), whole((1, width)),
        ],
        out_specs=[
            whole((rows, width)), whole((rows, width)), whole((rows, width)), whole((2, width)),
        ],
        out_shape=[
            shaped((rows, width), full), shaped((rows, width), low), shaped((rows, width), low),
            shaped((2, width), full),
        ],
        scratch_shapes=[pltpu.VMEM((rows, width), full)],
        compiler_params=settings(32, 1),
        cost_estimate=cost(6 * rows * width * hidden, 20 * MIB),
        name="feed_back",
    )(
        grad_second, grad_low, slope_up, slope_gate, gate_weight, up_weight, down_weight, output_weight,
        scaled, inverse, vec(gain_one),
    )

    group = width // 2
    mine = lax.dynamic_slice_in_dim(attended_grad, side * group, group, axis=1)
    other = lax.dynamic_slice_in_dim(attended_grad, (1 - side) * group, group, axis=1)
    far_grad = side_swap(other)
    at_side = lambda i: pl.BlockSpec((width, group), lambda j, place: (0, 2 * i + place[0]))
    dq_own, dq_far, keep, send = pl.pallas_call(
        attend_back,
        grid_spec=pltpu.PrefetchScalarGridSpec(
            num_scalar_prefetch=1,
            grid=(1,),
            in_specs=[
                whole((rows, width)), whole((rows, width)), whole((rows, width)), whole((rows, width)),
                at_side(0), at_side(1), at_side(2), whole((rows, group)), whole((rows, group)),
                whole((4 * rows, TILE)), whole((4 * rows, TILE)), whole((4 * rows, TILE)),
                whole((1, 4 * rows)),
            ],
            out_specs=[
                whole((rows, group)), whole((rows, group)), whole((two, width)), whole((two, width)),
            ],
            scratch_shapes=[
                pltpu.VMEM((4 * rows, group), low), pltpu.VMEM((4 * rows, group), low),
                pltpu.VMEM((two, group), low), pltpu.VMEM((4 * rows, two), full),
            ],
        ),
        out_shape=[
            shaped((rows, group), low), shaped((rows, group), low), shaped((two, width), full),
            shaped((two, width), low),
        ],
        compiler_params=settings(48, 1),
        cost_estimate=cost(10 * two * 4 * rows * group, 8 * MIB, 6 * two * 4 * rows),
        name="attend_back",
    )(
        side.reshape(1).astype(jnp.int32), tokens, near, far, far_near, input_weight, input_weight,
        input_weight, mine, far_grad, cosine, sine, seg_col, seg_row,
    )
    key_value = (keep + core_swap(send).astype(jnp.float32)).astype(low)
    back_own = jnp.concatenate([dq_own, key_value[:rows]], axis=1)
    back_far = jnp.concatenate([dq_far, key_value[rows:]], axis=1)
    back_other = side_swap(back_far)
    pieces = []
    for i in range(3):
        cols = slice(i * group, (i + 1) * group)
        pieces.append(jnp.where(side == 0, back_own[:, cols], back_other[:, cols]))
        pieces.append(jnp.where(side == 0, back_other[:, cols], back_own[:, cols]))
    projected_grad = jnp.concatenate(pieces, axis=1)
    grad_tokens = (grad_first + times_transpose(projected_grad, input_weight)).astype(low)

    quarter = width // 4
    pair_at = jnp.array([0, 2, 2, 4], jnp.int32) * quarter
    lone_at = jnp.array([4, 5, 0, 1], jnp.int32) * quarter
    back_both = jnp.concatenate([back_own, back_far], axis=0)

    def pick(owner):
        return jnp.concatenate(
            [
                lax.dynamic_slice_in_dim(back_both, pair_at[owner], 2 * quarter, axis=1),
                lax.dynamic_slice_in_dim(back_both, lone_at[owner], quarter, axis=1),
            ],
            axis=1,
        )

    back_cols = jnp.concatenate([pick(seq), core_swap(pick(seq ^ 1))], axis=0)
    window_tokens = jnp.concatenate([tokens, far, near, far_near], axis=0)
    grad_in = inner_rows(window_tokens, back_cols)

    def quarters(which):
        return jnp.concatenate(
            [
                lax.dynamic_slice_in_dim(branch_low, (2 * i + which) * quarter, quarter, axis=1)
                for i in range(2)
            ],
            axis=1,
        )

    exchanged = core_swap(jnp.concatenate([attended_low, quarters(1 - core)], axis=1))
    grad_out = inner_rows(
        jnp.concatenate([attended_low, exchanged[:, :width]], axis=0),
        jnp.concatenate([quarters(core), exchanged[:, width:]], axis=0),
    )
    out_send = lax.dynamic_slice_in_dim(grad_out, (1 - side) * quarter, quarter, axis=1).astype(low)
    out_keep = lax.dynamic_slice_in_dim(grad_out, side * quarter, quarter, axis=1)
    grad_out = out_keep + side_swap(out_send).astype(jnp.float32)

    def halves(value, bit):
        return (
            lax.dynamic_index_in_dim(value, bit, axis=1, keepdims=False),
            lax.dynamic_index_in_dim(value, 1 - bit, axis=1, keepdims=False),
        )

    def sum_over(value, axis, flip, bit):
        keep, send = halves(value, bit)
        return keep + swap(send.astype(low), axis, flip).astype(jnp.float32)

    part = width // n_data
    both = jnp.concatenate([grad_in, grad_out], axis=1).reshape(n_data // 2, 2, part, width)
    both = sum_over(both, "dp", 1, bit_x).reshape(2, 2, part, width)
    both = sum_over(both, "dp", 2, bit_low).reshape(1, 2, part, width)
    both = sum_over(both, "dp", 4, bit_high).reshape(part, width)
    grad_in, grad_out = both[:, : 3 * quarter], both[:, 3 * quarter :]
    moved = side_swap(grad_in[:, 2 * quarter :].astype(low)).astype(jnp.float32)
    grad_in = jnp.where(
        core == 0,
        jnp.concatenate([grad_in[:, : 2 * quarter], moved], axis=1),
        jnp.concatenate([moved, grad_in[:, : 2 * quarter]], axis=1),
    )

    eighth = hidden // 8
    owned = 2 * seq + bit_x
    gate_cols = lax.dynamic_slice_in_dim(gate_weight, owned * eighth, eighth, axis=1)
    up_cols = lax.dynamic_slice_in_dim(up_weight, owned * eighth, eighth, axis=1)
    gate_up = jnp.concatenate([gate_cols.T, up_cols.T], axis=0)
    down_rows = lax.dynamic_slice_in_dim(down_weight, owned * eighth, eighth, axis=0)
    sizes = [p.shape for p in normed_parts]
    keep_io, send_io, keep_down, send_down = pl.pallas_call(
        column_grads,
        grid_spec=pltpu.PrefetchScalarGridSpec(
            num_scalar_prefetch=1,
            grid=(1,),
            in_specs=[whole(s) for s in sizes]
            + [whole(s) for s in sizes]
            + [whole((2 * eighth, width)), whole((eighth, width))],
            out_specs=[
                whole((width // 2, 2 * eighth)), whole((width // 2, 2 * eighth)),
                whole((width // 2, eighth)), whole((width // 2, eighth)),
            ],
            scratch_shapes=[
                pltpu.VMEM((2 * eighth, width), full), pltpu.VMEM((eighth, width), full),
                pltpu.VMEM((width, 2 * eighth), full), pltpu.VMEM((width, eighth), full),
            ],
        ),
        out_shape=[
            shaped((width // 2, 2 * eighth), full), shaped((width // 2, 2 * eighth), low),
            shaped((width // 2, eighth), full), shaped((width // 2, eighth), low),
        ],
        compiler_params=settings(56, 1),
        cost_estimate=cost(12 * 8 * rows * width * eighth, 12 * MIB, 8 * rows * eighth),
        name="column_grads",
    )(bit_low.reshape(1).astype(jnp.int32), *normed_parts, *grad_parts, gate_up, down_rows)

    def finish(keep, send):
        both = keep + swap(send, "dp", 2).astype(jnp.float32)
        both = both.reshape(1, 2, width // 4, both.shape[1])
        return sum_over(both, "dp", 4, bit_high).reshape(width // 4, both.shape[3])

    down = finish(keep_down, send_down)
    io = finish(keep_io, send_io)
    order = []
    for d in range(n_data):
        for s in range(n_seq):
            order.append((d * n_seq + s, (2 * s + d % 2) * n_seq + d // 2))
    grad_down = lax.ppermute(down.astype(low), ("dp", "seq"), order).astype(jnp.float32).T
    io_keep, io_send = (
        lax.dynamic_slice_in_dim(io, bit_x * part, part, axis=0),
        lax.dynamic_slice_in_dim(io, (1 - bit_x) * part, part, axis=0),
    )
    io_other = x_swap(io_send.astype(low)).astype(jnp.float32)

    def beside(index):
        cols = slice(index * eighth, (index + 1) * eighth)
        a, b = io_keep[:, cols], io_other[:, cols]
        return jnp.where(
            bit_x == 0, jnp.concatenate([a, b], axis=1), jnp.concatenate([b, a], axis=1)
        )

    sums = jnp.concatenate([sums_one, sums_two], axis=0)
    for axis, flip in (("seq", 1), ("seq", 2), ("dp", 1), ("dp", 2), ("dp", 4)):
        sums = sums + swap(sums, axis, flip)
    return (
        result,
        grad_tokens,
        grad_in,
        grad_out,
        beside(0),
        beside(1),
        grad_down,
        sums[0],
        sums[1],
        sums[2],
        sums[3],
    )


def solution(mesh):
    placed = (
        P(("dp", "seq"), None),
        P(("dp", "seq"), None),
        P("dp", None),
        P(),
        P(),
        P(),
        P(),
        P(),
        P(),
        P(),
        P(),
        P(),
    )
    paired = mesh.shape["seq"] == 4 and mesh.shape["dp"] == 8
    return jax.shard_map(
        fast if paired else general,
        mesh=mesh,
        in_specs=placed,
        out_specs=(
            P(("dp", "seq"), None),
            P(("dp", "seq"), None),
            P("dp", "seq"),
            P("dp", "seq"),
            P("dp", "seq"),
            P("dp", "seq"),
            P("dp", "seq"),
            P(),
            P(),
            P(),
            P(),
        ),
        check_vma=False,
    )
```

```python
import functools
import math

import jax
import jax.numpy as jnp
import numpy as np
from jax import lax
from jax.experimental import pallas as pl
from jax.experimental.pallas import tpu as pltpu
from jax.sharding import PartitionSpec as P

HEAD = 64


norm_eps = 1e-05
rotary_base = 1000.0
masked_value = -1e30


def doc_layout(lengths_row, count):
    ends = jnp.cumsum(lengths_row)
    place = jnp.arange(count, dtype=jnp.int32)
    after = (place[:, None] >= ends[None, :]).astype(jnp.int32)
    segment = jnp.sum(after, axis=1)
    start = jnp.sum(after * lengths_row[None, :], axis=1)
    return (segment, place - start)


def rotate(field, position):
    half = field.shape[-1] // 2
    freq = rotary_base ** (-jnp.arange(half, dtype=jnp.float32) * (2.0 / field.shape[-1]))
    angle = position.astype(jnp.float32)[:, None] * freq[None, :]
    cosine = jnp.cos(angle)[:, None, :]
    sine = jnp.sin(angle)[:, None, :]
    first = field[..., :half]
    second = field[..., half:]
    return jnp.concatenate(
        [first * cosine - second * sine, second * cosine + first * sine], axis=-1
    )


def norm_forward(value, gain, shift):
    mean = jnp.mean(value, axis=-1, keepdims=True)
    centred = value - mean
    inverse = lax.rsqrt(jnp.mean(centred * centred, axis=-1, keepdims=True) + norm_eps)
    scaled = centred * inverse
    return (scaled * gain + shift, scaled, inverse)


def norm_backward(grad, scaled, inverse, gain):
    inner = grad * gain
    back = inverse * (
        inner
        - jnp.mean(inner, axis=-1, keepdims=True)
        - scaled * jnp.mean(inner * scaled, axis=-1, keepdims=True)
    )
    return (back, jnp.sum(grad * scaled, axis=0), jnp.sum(grad, axis=0))


def inner_rows(left, right):
    return lax.dot_general(
        left, right, (((0,), (0,)), ((), ())), preferred_element_type=jnp.float32
    )


def times_transpose(left, right):
    return lax.dot_general(
        left, right, (((1,), (1,)), ((), ())), preferred_element_type=jnp.float32
    )


def general(
    tokens,
    cotangent,
    lengths,
    input_weight,
    output_weight,
    gate_weight,
    up_weight,
    down_weight,
    gain_one,
    bias_one,
    gain_two,
    bias_two,
):
    rows, width = tokens.shape
    heads = width // HEAD
    window = rows * lax.axis_size("seq")
    scale = 1.0 / math.sqrt(HEAD)
    segment_all, position_all = doc_layout(lengths[0], window)
    offset = lax.axis_index("seq") * rows
    seg_mine = lax.dynamic_slice_in_dim(segment_all, offset, rows)
    pos_mine = lax.dynamic_slice_in_dim(position_all, offset, rows)
    projected = jnp.dot(tokens, input_weight, preferred_element_type=jnp.float32)
    query = rotate(projected[:, :width].reshape(rows, heads, HEAD), pos_mine).astype(jnp.bfloat16)
    key = (
        rotate(projected[:, width : 2 * width].reshape(rows, heads, HEAD), pos_mine)
        .astype(jnp.bfloat16)
        .reshape(rows, width)
    )
    value = projected[:, 2 * width :].astype(jnp.bfloat16)

    def scores_for(key_block, seg_block):
        scores = (
            jnp.einsum("qhe,khe->hqk", query, key_block, preferred_element_type=jnp.float32) * scale
        )
        same = (seg_mine[:, None] == seg_block[None, :])[None]
        return (jnp.where(same, scores, masked_value), same)

    def split_blocks(piece, segs):
        count = piece[0].shape[0]
        size = math.gcd(count, 512)
        keys = piece[0].reshape(count // size, size, heads, HEAD)
        values = piece[1].reshape(count // size, size, heads, HEAD)
        return (keys, values, segs.reshape(count // size, size), count, size)

    start_state = (
        jnp.zeros((rows, heads, HEAD), jnp.float32),
        jnp.full((heads, rows), masked_value, jnp.float32),
        jnp.zeros((heads, rows), jnp.float32),
    )
    segs = segment_all
    keys, values, seg_blocks, count, size = split_blocks(
        (
            lax.all_gather(key, "seq", axis=0, tiled=True),
            lax.all_gather(value, "seq", axis=0, tiled=True),
        ),
        segs,
    )

    def forward_step(state, item):
        summed, peak, total = state
        key_block, value_block, seg_block = item
        scores, same = scores_for(key_block, seg_block)
        new_peak = jnp.maximum(peak, jnp.max(scores, axis=-1))
        fade = jnp.exp(peak - new_peak)
        weight = jnp.where(same, jnp.exp(scores - new_peak[..., None]), 0.0)
        total = total * fade + jnp.sum(weight, axis=-1)
        summed = summed * fade.T[..., None] + jnp.einsum(
            "hqk,khe->qhe",
            weight.astype(jnp.bfloat16),
            value_block,
            preferred_element_type=jnp.float32,
        )
        return ((summed, new_peak, total), None)

    state, unused = lax.scan(forward_step, start_state, (keys, values, seg_blocks))
    summed, peak, total = state
    attended = (summed / total.T[..., None]).reshape(rows, width)
    attended_low = attended.astype(jnp.bfloat16)
    first = tokens.astype(jnp.float32) + jnp.dot(
        attended_low, output_weight, preferred_element_type=jnp.float32
    )
    normed, scaled_one, inverse_one = norm_forward(first, gain_one, bias_one)
    normed_low = normed.astype(jnp.bfloat16)
    gate = jnp.dot(normed_low, gate_weight, preferred_element_type=jnp.float32)
    upward = jnp.dot(normed_low, up_weight, preferred_element_type=jnp.float32)
    sigma = jax.nn.sigmoid(gate)
    activated = gate * sigma
    hidden_low = (activated * upward).astype(jnp.bfloat16)
    second = normed + jnp.dot(hidden_low, down_weight, preferred_element_type=jnp.float32)
    result, scaled_two, inverse_two = norm_forward(second, gain_two, bias_two)
    grad_second, grad_gain_two, grad_bias_two = norm_backward(
        cotangent.astype(jnp.float32), scaled_two, inverse_two, gain_two
    )
    grad_ff_low = grad_second.astype(jnp.bfloat16)
    grad_hidden = times_transpose(grad_ff_low, down_weight)
    grad_gate_low = (grad_hidden * upward * (sigma * (1.0 + gate * (1.0 - sigma)))).astype(
        jnp.bfloat16
    )
    grad_up_low = (grad_hidden * activated).astype(jnp.bfloat16)
    grad_normed = (
        grad_second
        + times_transpose(grad_gate_low, gate_weight)
        + times_transpose(grad_up_low, up_weight)
    )
    grad_first, grad_gain_one, grad_bias_one = norm_backward(
        grad_normed, scaled_one, inverse_one, gain_one
    )
    grad_branch_low = grad_first.astype(jnp.bfloat16)
    grad_attended_low = times_transpose(grad_branch_low, output_weight).astype(jnp.bfloat16)
    grad_heads = grad_attended_low.reshape(rows, heads, HEAD)
    delta = jnp.sum(
        (grad_attended_low.astype(jnp.float32) * attended).reshape(rows, heads, HEAD), axis=-1
    ).T
    zero_query = jnp.zeros((rows, heads, HEAD), jnp.float32)
    grad_acc = zero_query
    segs = segment_all
    grad_query = grad_acc
    keys, values, seg_blocks, count, size = split_blocks(
        (
            lax.all_gather(key, "seq", axis=0, tiled=True),
            lax.all_gather(value, "seq", axis=0, tiled=True),
        ),
        segs,
    )

    def backward_step(grad_acc, item):
        key_block, value_block, seg_block = item
        scores, same = scores_for(key_block, seg_block)
        prob = jnp.where(same, jnp.exp(scores - peak[..., None]) / total[..., None], 0.0)
        prob_grad = jnp.einsum(
            "qhe,khe->hqk", grad_heads, value_block, preferred_element_type=jnp.float32
        )
        score_grad = (prob * (prob_grad - delta[..., None])).astype(jnp.bfloat16)
        grad_acc = (
            grad_acc
            + jnp.einsum("hqk,khe->qhe", score_grad, key_block, preferred_element_type=jnp.float32)
            * scale
        )
        prob_low = prob.astype(jnp.bfloat16)
        key_grad = (
            jnp.einsum("hqk,qhe->khe", score_grad, query, preferred_element_type=jnp.float32)
            * scale
        )
        value_grad = jnp.einsum(
            "hqk,qhe->khe", prob_low, grad_heads, preferred_element_type=jnp.float32
        )
        return (grad_acc, (key_grad.reshape(size, width), value_grad.reshape(size, width)))

    grad_query, outputs = lax.scan(backward_step, grad_query, (keys, values, seg_blocks))
    grad_acc = grad_query
    key_part = outputs[0].reshape(count, width)
    value_part = outputs[1].reshape(count, width)
    grad_key, grad_value = (
        lax.psum_scatter(
            key_part.astype(jnp.bfloat16), "seq", scatter_dimension=0, tiled=True
        ).astype(jnp.float32),
        lax.psum_scatter(
            value_part.astype(jnp.bfloat16), "seq", scatter_dimension=0, tiled=True
        ).astype(jnp.float32),
    )
    query_back = rotate(grad_acc, -pos_mine).reshape(rows, width)
    key_back = rotate(grad_key.reshape(rows, heads, HEAD), -pos_mine).reshape(rows, width)
    grad_projected_low = jnp.concatenate([query_back, key_back, grad_value], axis=1).astype(
        jnp.bfloat16
    )
    grad_tokens = (grad_first + times_transpose(grad_projected_low, input_weight)).astype(
        jnp.bfloat16
    )
    column_grads = (
        lax.all_to_all(grad_projected_low, "seq", split_axis=1, concat_axis=0, tiled=True),
        lax.all_to_all(grad_branch_low, "seq", split_axis=1, concat_axis=0, tiled=True),
        lax.all_to_all(grad_gate_low, "seq", split_axis=1, concat_axis=0, tiled=True),
        lax.all_to_all(grad_up_low, "seq", split_axis=1, concat_axis=0, tiled=True),
        lax.all_to_all(grad_ff_low, "seq", split_axis=1, concat_axis=0, tiled=True),
    )
    tok_rows = lax.all_gather(tokens, "seq", axis=0, tiled=True)
    normed_rows = lax.all_gather(normed_low, "seq", axis=0, tiled=True)
    attended_rows = lax.all_gather(attended_low, "seq", axis=0, tiled=True)
    hidden_rows = lax.all_gather(hidden_low, "seq", axis=0, tiled=True)
    count = tok_rows.shape[0]
    cols = [member for member in column_grads]
    summed_grads = (
        lax.psum_scatter(
            inner_rows(tok_rows, cols[0]).astype(jnp.bfloat16),
            "dp",
            scatter_dimension=0,
            tiled=True,
        ).astype(jnp.float32),
        lax.psum_scatter(
            inner_rows(attended_rows, cols[1]).astype(jnp.bfloat16),
            "dp",
            scatter_dimension=0,
            tiled=True,
        ).astype(jnp.float32),
        lax.psum_scatter(
            inner_rows(normed_rows, cols[2]).astype(jnp.bfloat16),
            "dp",
            scatter_dimension=0,
            tiled=True,
        ).astype(jnp.float32),
        lax.psum_scatter(
            inner_rows(normed_rows, cols[3]).astype(jnp.bfloat16),
            "dp",
            scatter_dimension=0,
            tiled=True,
        ).astype(jnp.float32),
        lax.psum_scatter(
            inner_rows(hidden_rows, cols[4]).astype(jnp.bfloat16),
            "dp",
            scatter_dimension=0,
            tiled=True,
        ).astype(jnp.float32),
    )
    norm_grads = lax.psum(
        (grad_gain_one, grad_bias_one, grad_gain_two, grad_bias_two), ("dp", "seq")
    )
    return (
        result.astype(jnp.bfloat16),
        grad_tokens,
        summed_grads[0],
        summed_grads[1],
        summed_grads[2],
        summed_grads[3],
        summed_grads[4],
        norm_grads[0],
        norm_grads[1],
        norm_grads[2],
        norm_grads[3],
    )


low = jnp.bfloat16
full = jnp.float32
TILE = 128
MIB = 1024 * 1024


def nn(left, right):
    return lax.dot_general(
        left, right, (((1,), (0,)), ((), ())), preferred_element_type=jnp.float32
    )


def nt(left, right):
    return lax.dot_general(
        left, right, (((1,), (1,)), ((), ())), preferred_element_type=jnp.float32
    )


def tn(left, right):
    return lax.dot_general(
        left, right, (((0,), (0,)), ((), ())), preferred_element_type=jnp.float32
    )


def block(shape, *at):
    at = at or (0,) * len(shape)

    def index(*args):
        return tuple(a(*args[1:]) if callable(a) else a for a in at)

    return pl.BlockSpec(tuple(shape), index)


def shaped(shape, kind):
    return jax.ShapeDtypeStruct(tuple(shape), kind)


COST = {
    "tables": 3, "first_half": 6, "second_half": 9, "feed_forward": 8, "feed_back": 9, "attend_back": 7,
    "column_grads": 7, "token_grad": 3,
}


def took(name):
    return pl.CostEstimate(flops=COST.get(name, 1) * 10**9, bytes_accessed=1, transcendentals=0)


def call(body, name, scalars, operands, results, scratch=(), mib=16, alias=None):
    return pl.pallas_call(
        body,
        grid_spec=pltpu.PrefetchScalarGridSpec(
            num_scalar_prefetch=1,
            grid=(1,),
            in_specs=[spec for unused, spec in operands],
            out_specs=[spec for unused, spec in results],
            scratch_shapes=list(scratch),
        ),
        out_shape=[shape for shape, unused in results],
        compiler_params=pltpu.CompilerParams(
            vmem_limit_bytes=mib * MIB, dimension_semantics=("arbitrary",)
        ),
        cost_estimate=took(name),
        input_output_aliases=alias or {},
        name=name,
    )(scalars, *[value for value, unused in operands])


def whole(value):
    return (value, block(value.shape))


def turn(field, cosine, sine):
    lane = lax.broadcasted_iota(jnp.int32, field.shape, 1)
    half = HEAD // 2
    other = jnp.where(
        lane % HEAD < half, pltpu.roll(field, TILE - half, 1), pltpu.roll(field, half, 1)
    )
    return field * cosine + other * sine


def one_head(pair, which):
    lane = lax.broadcasted_iota(jnp.int32, pair.shape, 1)
    return jnp.where((lane // HEAD) == which, pair, jnp.zeros_like(pair))


def pack(sums):
    high = sums.astype(low)
    return jnp.concatenate([high, (sums - high.astype(jnp.float32)).astype(low)], axis=0)


def unpack(packed):
    wide = packed.astype(jnp.float32)
    return wide[:8] + wide[8:]


def tables(place, lengths, freq, cosine, sine, seg_col, seg_row):
    count = cosine.shape[0]
    rows = count // 4
    lane = lax.broadcasted_iota(jnp.int32, (8, count), 1)
    index = jnp.zeros_like(lane)
    for i in range(1, 4):
        index = index + (lane >= i * rows).astype(jnp.int32)
    spot = (index ^ place[0]) * rows + (lane - index * rows)
    end = jnp.int32(0)
    segment = jnp.zeros_like(lane)
    start = jnp.zeros_like(lane)
    for i in range(lengths.shape[1]):
        length = lengths[0, i]
        end = end + length
        past = (spot >= end).astype(jnp.int32)
        segment = segment + past
        start = start + past * length
    position = (spot - start).astype(jnp.float32)
    angle = freq[:, :1] * position[:1]
    c, s = jnp.cos(angle), jnp.sin(angle)
    cosine[...] = jnp.concatenate([c] * 4, axis=0).T
    sine[...] = jnp.concatenate([-s, s] * 2, axis=0).T
    seg_row[...] = segment
    wide = jnp.broadcast_to(segment[:1].astype(jnp.float32), (TILE, count))
    seg_col[...] = wide.T.astype(jnp.int32)


def put_keys(tokens, wk, wv, cosine, sine, keys, values, start):
    rows, width = tokens.shape
    projected = nn(tokens, wk)
    for tile in range(width // TILE):
        cols = slice(tile * TILE, (tile + 1) * TILE)
        keys[start : start + rows, cols] = turn(projected[:, cols], cosine, sine).astype(low)
    values[start : start + rows, :] = nn(tokens, wv).astype(low)


def put_query(tokens, wq, cosine, sine, query):
    scale = 1.0 / math.sqrt(HEAD)
    projected = nn(tokens, wq)
    for tile in range(projected.shape[1] // TILE):
        cols = slice(tile * TILE, (tile + 1) * TILE)
        turned = turn(projected[:, cols], cosine, sine)
        query[:, cols] = (turned.astype(low) * scale).astype(low)


def attend(query, keys, values, bias):
    for tile in range(query.shape[1] // TILE):
        cols = slice(tile * TILE, (tile + 1) * TILE)
        key_pair = keys[:, cols]
        value_pair = values[:, cols]
        for which in range(TILE // HEAD):
            scores = nt(key_pair, one_head(query[:, cols], which)) + bias[...]
            peak = jnp.max(scores, axis=0, keepdims=True)
            weight = jnp.exp(scores - peak)
            total = jnp.sum(weight, axis=0, keepdims=True)
            out = tn(value_pair, weight.astype(low))[which * HEAD : (which + 1) * HEAD]
            yield tile * (TILE // HEAD) + which, out, peak, total


def first_half(
    place, own, near, wq, wk, wv, cosine, sine, seg_key, seg_query, query, acc, peaks, totals,
    keys, values, bias,
):
    rows = own.shape[0]
    put_query(own[...], wq[...], cosine[:rows, :], sine[:rows, :], query)
    put_keys(own[...], wk[...], wv[...], cosine[:rows, :], sine[:rows, :], keys, values, 0)
    put_keys(near[...], wk[...], wv[...], cosine[rows:, :], sine[rows:, :], keys, values, rows)
    bias[...] = jnp.where(seg_key[:, :1] == seg_query[:1, :], 0.0, masked_value)
    for head, out, peak, total in attend(query, keys, values, bias):
        acc[head * HEAD : (head + 1) * HEAD, :] = out
        peaks[head : head + 1, :] = peak
        totals[head : head + 1, :] = total


def second_half(
    place, own, far, far_near, wk, wv, wo, cosine, sine, seg_key, seg_query, query, acc, peaks, totals,
    gain, shift, attended_low, normed, normed_low, scaled, inverse, keys, values, bias, turned,
):
    rows, width = own.shape
    put_keys(far[...], wk[...], wv[...], cosine[:rows, :], sine[:rows, :], keys, values, 0)
    put_keys(far_near[...], wk[...], wv[...], cosine[rows:, :], sine[rows:, :], keys, values, rows)
    bias[...] = jnp.where(seg_key[:, :1] == seg_query[:1, :], 0.0, masked_value)
    for head, out, peak, total in attend(query, keys, values, bias):
        part = slice(head * HEAD, (head + 1) * HEAD)
        before = peaks[head : head + 1, :]
        best = jnp.maximum(before, peak)
        fade = jnp.exp(before - best)
        grow = jnp.exp(peak - best)
        inverse_total = 1.0 / (totals[head : head + 1, :] * fade + total * grow)
        turned[part, :] = acc[part, :] * (fade * inverse_total) + out * (grow * inverse_total)
    attended = turned[...].T.astype(low)
    attended_low[...] = attended
    first = own[...].astype(jnp.float32) + nn(attended, wo[...])
    mean = jnp.mean(first, axis=1, keepdims=True)
    centred = first - mean
    spread = lax.rsqrt(jnp.mean(centred * centred, axis=1, keepdims=True) + norm_eps)
    unit = centred * spread
    value = unit * gain[...] + shift[...]
    scaled[...] = unit
    inverse[...] = jnp.broadcast_to(spread, (rows, TILE))
    normed[...] = value
    normed_low[...] = value.astype(low)


def feed_forward(
    normed, normed_low, wg, wu, wd, cotangent, gain, shift,
    slope_up, slope_gate, result, grad_second, grad_low, sums, acc,
):
    step = pl.program_id(0)
    gate = nn(normed_low[...], wg[...])
    upward = nn(normed_low[...], wu[...])
    sigma = jax.nn.sigmoid(gate)
    active = gate * sigma
    slope_up[...] = active.astype(low)
    slope_gate[...] = (upward * (sigma * (1.0 + gate * (1.0 - sigma)))).astype(low)
    product = nn((active * upward).astype(low), wd[...])

    @pl.when(step == 0)
    def _():
        acc[...] = normed[...] + product

    @pl.when(step > 0)
    def _():
        acc[...] += product

    @pl.when(step == pl.num_programs(0) - 1)
    def _():
        second = acc[...]
        mean = jnp.mean(second, axis=1, keepdims=True)
        centred = second - mean
        spread = lax.rsqrt(jnp.mean(centred * centred, axis=1, keepdims=True) + norm_eps)
        unit = centred * spread
        result[...] = (unit * gain[...] + shift[...]).astype(low)
        grad = cotangent[...].astype(jnp.float32)
        inner = grad * gain[...]
        back = spread * (
            inner
            - jnp.mean(inner, axis=1, keepdims=True)
            - unit * jnp.mean(inner * unit, axis=1, keepdims=True)
        )
        grad_second[...] = back
        grad_low[...] = back.astype(low)
        sums[0:1, :] = jnp.sum(grad * unit, axis=0, keepdims=True)
        sums[1:2, :] = jnp.sum(grad, axis=0, keepdims=True)


def feed_back(
    place, grad_second, grad_low, slope_up, slope_gate, wg, wu, wd, wo, scaled, inverse, gain, sums_two,
    grad_first, branch_low, mine, other, sums, acc,
):
    step = pl.program_id(0)
    hidden = nt(grad_low[...], wd[...])
    gate = (hidden * slope_gate[...].astype(jnp.float32)).astype(low)
    upward = (hidden * slope_up[...].astype(jnp.float32)).astype(low)
    product = nt(gate, wg[...]) + nt(upward, wu[...])

    @pl.when(step == 0)
    def _():
        acc[...] = grad_second[...] + product

    @pl.when(step > 0)
    def _():
        acc[...] += product

    @pl.when(step == pl.num_programs(0) - 1)
    def _():
        grad = acc[...]
        unit = scaled[...]
        inner = grad * gain[...]
        back = inverse[:, :1] * (
            inner
            - jnp.mean(inner, axis=1, keepdims=True)
            - unit * jnp.mean(inner * unit, axis=1, keepdims=True)
        )
        grad_first[...] = back
        branch_low[...] = back.astype(low)
        attended_grad = nt(branch_low[...], wo[...]).astype(low)
        group = mine.shape[1]
        left, right = attended_grad[:, :group], attended_grad[:, group:]
        second_side = place[0] > 0
        mine[...] = jnp.where(second_side, right, left)
        other[...] = jnp.where(second_side, left, right)
        sums[...] = jnp.zeros_like(sums)
        sums[0:1, :] = jnp.sum(grad * unit, axis=0, keepdims=True)
        sums[1:2, :] = jnp.sum(grad, axis=0, keepdims=True)
        sums[2:4, :] = sums_two[...]


def rows_at(index, count):
    return pl.ds(pl.multiple_of(index * count, count), count)


def out_grad(place, branch_low, attended_low, keep, send, turned):
    turned[...] = tn(branch_low[...], attended_low[...])
    quarter = turned.shape[0] // 4
    core = place[0]
    for i in range(2):
        to = slice(i * quarter, (i + 1) * quarter)
        keep[to, :] = turned[rows_at(2 * i + core, quarter), :]
        send[to, :] = turned[rows_at(2 * i + 1 - core, quarter), :].astype(low)


def out_halve(place, keep, got, sums, kept, send):
    quarter = keep.shape[0] // 2
    side = place[0]
    mine, other = rows_at(side, quarter), rows_at(1 - side, quarter)
    kept[...] = keep[mine, :] + got[mine, :].astype(jnp.float32)
    send[:quarter, :] = (keep[other, :] + got[other, :].astype(jnp.float32)).astype(low)
    send[quarter:, :] = pack(sums[...])


def attend_back(
    place, own, near, far, far_near, wq, wk, wv, own_grad, far_grad, cosine, sine, seg_key, seg_query,
    *refs,
):
    dq, even, odd, grads, keys, values, query, bias = refs[-8:]
    rows = own.shape[0]
    scale = 1.0 / math.sqrt(HEAD)
    blocks = (own, near, far, far_near)
    weights = jnp.concatenate([wk[...], wv[...]], axis=1)
    for index, tokens in enumerate(blocks):
        part = slice(index * rows, (index + 1) * rows)
        projected = nn(tokens[...], weights)
        keys[part, :] = turn(projected[:, :TILE], cosine[part, :], sine[part, :]).astype(low)
        values[part, :] = projected[:, TILE:].astype(low)
        if index % 2 == 0:
            to = slice(index // 2 * rows, (index // 2 + 1) * rows)
            turned = turn(nn(tokens[...], wq[...]), cosine[part, :], sine[part, :])
            query[to, :] = (turned.astype(low) * scale).astype(low)
            bias[:, to] = jnp.where(seg_key[:, :1] == seg_query[:1, part], 0.0, masked_value)
    key_pair = keys[...]
    value_pair = values[...]
    grad_key = None
    grad_value = None
    for index, grad_ref in enumerate((own_grad, far_grad)):
        part = slice(index * rows, (index + 1) * rows)
        query_pair = query[part, :]
        grad_pair = grad_ref[...]
        pieces = []
        for which in range(TILE // HEAD):
            query_head = one_head(query_pair, which)
            grad_head = one_head(grad_pair, which)
            scores = nt(key_pair, query_head) + bias[:, part]
            weight = jnp.exp(scores - jnp.max(scores, axis=0, keepdims=True))
            prob = weight * (1.0 / jnp.sum(weight, axis=0, keepdims=True))
            prob_grad = nt(value_pair, grad_head)
            both = prob * prob_grad
            delta = jnp.sum(both, axis=0, keepdims=True)
            score_grad = (both - prob * delta).astype(low)
            value_part = nn(prob.astype(low), grad_head)
            key_part = nn(score_grad, query_head)
            grad_key = key_part if grad_key is None else grad_key + key_part
            grad_value = value_part if grad_value is None else grad_value + value_part
            pieces.append(tn(key_pair, score_grad)[which * HEAD : (which + 1) * HEAD])
        grad_query = jnp.concatenate(pieces, axis=0).T * scale
        at = slice(2 * index * rows, (2 * index + 1) * rows)
        dq[part, :] = turn(grad_query, cosine[at, :], -sine[at, :]).astype(low)
    grad_key = turn(grad_key, cosine[...], -sine[...]).astype(low)
    grad_value = grad_value.astype(low)
    both = jnp.concatenate([grad_key, grad_value], axis=1)
    for index in range(4):
        part = slice(index * rows, (index + 1) * rows)
        to = slice(index // 2 * rows, (index // 2 + 1) * rows)
        (odd if index % 2 else even)[to, :] = both[part, :]
    total = None
    for index, tokens in enumerate(blocks):
        part = slice(index * rows, (index + 1) * rows)
        product = tn(both[part, :], tokens[...])
        total = product if total is None else total + product
    grads[TILE:, :] = total
    grads[:TILE, :] = tn(dq[:rows, :], own[...]) + tn(dq[rows:, :], far[...])


def fold(place, grads, out_got, sums, keep, send, kept_sums, turned):
    tiles = grads.shape[0] // (3 * TILE)
    for kind in range(3):
        for tile in range(tiles):
            at = (kind * tiles + tile) * TILE
            source = (tile * 3 + kind) * TILE
            turned[at : at + TILE, :] = grads[source : source + TILE, :]
    quarter = keep.shape[0] // 3
    pair, lone, other_pair, other_lone = place[0], place[1], place[2], place[3]
    for i in range(3):
        to = slice(i * quarter, (i + 1) * quarter)
        keep[to, :] = turned[rows_at(pair + i if i < 2 else lone, quarter), :]
        send[to, :] = turned[rows_at(other_pair + i if i < 2 else other_lone, quarter), :].astype(low)
    total = sums[...] + unpack(out_got[-16:, :])
    kept_sums[...] = total
    send[3 * quarter :, :] = pack(total)


def turn_over(place, keep, got, out_keep, out_got, sums, kept, send, kept_sums, turned):
    height = keep.shape[0]
    total = keep[...] + got[:height, :].astype(jnp.float32)
    out = out_keep[...] + out_got[: out_keep.shape[0], :].astype(jnp.float32)
    turned[:, :height] = total.T
    turned[:, height:] = out.T
    bit = place[0]
    part = turned.shape[0] // 8
    for i in range(4):
        to = slice(i * part, (i + 1) * part)
        kept[to, :] = turned[rows_at(2 * i + bit, part), :]
        send[to, :] = turned[rows_at(2 * i + 1 - bit, part), :].astype(low)
    both = sums[...] + unpack(got[height:, :])
    kept_sums[...] = both
    send[4 * part :, :] = pack(both)


def halve(place, keep, got, sums, kept, send, kept_sums):
    bit = place[0]
    height = keep.shape[0]
    count = 2 if height > 192 else 1
    part = height // (2 * count)
    for i in range(count):
        to = slice(i * part, (i + 1) * part)
        mine, other = rows_at(2 * i + bit, part), rows_at(2 * i + 1 - bit, part)
        kept[to, :] = keep[mine, :] + got[mine, :].astype(jnp.float32)
        send[to, :] = (keep[other, :] + got[other, :].astype(jnp.float32)).astype(low)
    both = sums[...] + unpack(got[height:, :])
    kept_sums[...] = both
    send[count * part :, :] = pack(both)


def last_sum(place, keep, got, sums, own, send, out, total_sums):
    height = keep.shape[0]
    total = keep[...] + got[:height, :].astype(jnp.float32)
    quarter = out.shape[1]
    own[...] = total[:, : 2 * quarter]
    send[...] = total[:, 2 * quarter : 3 * quarter].astype(low)
    out[...] = total[:, 3 * quarter :]
    total_sums[...] = sums[...] + unpack(got[height:, :])


def column_grads(place, *refs):
    count = 5
    rows_refs, back_refs = refs[:count], refs[count : 2 * count]
    wgu, wd, out, acc = refs[2 * count :]
    half, width = wd.shape
    for step in range(count):
        rows = rows_refs[step][...]
        back = back_refs[step][...]
        both = nt(wgu[...], rows)
        gate, upward = both[:half], both[half:]
        sigma = jax.nn.sigmoid(gate)
        active = gate * sigma
        hidden = (active * upward).astype(low)
        grad_hidden = nt(wd[...], back)
        grad_gate = (grad_hidden * upward * (sigma * (1.0 + gate * (1.0 - sigma)))).astype(low)
        grad_up = (grad_hidden * active).astype(low)
        products = (nn(grad_gate, rows), nn(grad_up, rows), nn(hidden, back))
        for i, product in enumerate(products):
            part = slice(i * half, (i + 1) * half)
            if step == 0:
                acc[part, :] = product
            else:
                acc[part, :] += product
    for i in range(3):
        part = slice(i * half, (i + 1) * half)
        out[:, part] = acc[part, :].T.astype(out.dtype)


def first_split(place, keep, got, kept, send):
    bit = place[0]
    part = keep.shape[0] // 4
    for i in range(2):
        to = slice(i * part, (i + 1) * part)
        mine, other = rows_at(2 * i + bit, part), rows_at(2 * i + 1 - bit, part)
        kept[to, :] = keep[mine, :] + got[mine, :].astype(jnp.float32)
        send[to, :] = (keep[other, :] + got[other, :].astype(jnp.float32)).astype(low)


def second_split(place, keep, got, kept, send):
    bit = place[0]
    part = keep.shape[0] // 2
    mine, other = rows_at(bit, part), rows_at(1 - bit, part)
    kept[...] = keep[mine, :] + got[mine, :].astype(jnp.float32)
    send[...] = (keep[other, :] + got[other, :].astype(jnp.float32)).astype(low)


def down_sum(place, keep, got, out):
    out[...] = (keep[...] + got[...].astype(jnp.float32)).astype(low)


def pair_sum(place, keep_gate, got_gate, keep_up, got_up, kept, send):
    part = kept.shape[0]
    half = keep_gate.shape[1]
    mine, other = rows_at(place[0], part), rows_at(1 - place[0], part)
    for i, (keep, got) in enumerate(((keep_gate, got_gate), (keep_up, got_up))):
        cols = slice(i * half, (i + 1) * half)
        kept[:, cols] = keep[mine, :] + got[mine, :].astype(jnp.float32)
        send[:, cols] = (keep[other, :] + got[other, :].astype(jnp.float32)).astype(low)


def pair_place(place, kept, got, gate, upward):
    half = kept.shape[1] // 2
    for i, out in enumerate((gate, upward)):
        cols = slice(i * half, (i + 1) * half)
        out[:, rows_at(place[0], half)] = kept[:, cols]
        out[:, rows_at(1 - place[0], half)] = got[:, cols].astype(jnp.float32)


def token_grad(
    place, grad_first, dq, even, got, far_dq, far_kv, *refs,
):
    weights, out = refs[:-1], refs[-1]
    rows = grad_first.shape[0]
    kind = len(weights) // 2
    total = grad_first[...]
    key_value = (
        even[:rows, :].astype(jnp.float32) + got[:rows, :].astype(jnp.float32)
    ).astype(low)
    group = dq.shape[1]
    for query, both, parts in (
        (dq[:rows, :], key_value, weights[:kind]),
        (far_dq[...], far_kv[...], weights[kind:]),
    ):
        wq, wk, wv = parts
        total = total + nt(query, wq[...])
        keys = jnp.concatenate(
            [both[:, 2 * t * TILE : (2 * t + 1) * TILE] for t in range(group // TILE)], axis=1
        )
        values = jnp.concatenate(
            [both[:, (2 * t + 1) * TILE : (2 * t + 2) * TILE] for t in range(group // TILE)], axis=1
        )
        total = total + nt(keys, wk[...]) + nt(values, wv[...])
    out[...] = total.astype(low)


def after(value, *others):
    return lax.optimization_barrier((value,) + others)[0]


def fast(
    tokens,
    cotangent,
    lengths,
    input_weight,
    output_weight,
    gate_weight,
    up_weight,
    down_weight,
    gain_one,
    bias_one,
    gain_two,
    bias_two,
):
    rows, width = tokens.shape
    hidden = gate_weight.shape[1]
    seq = lax.axis_index("seq")
    data = lax.axis_index("dp")
    n_seq, n_data = lax.axis_size("seq"), lax.axis_size("dp")
    core, side = seq % 2, seq // 2
    bit_x, bit_low, bit_high = data % 2, (data // 2) % 2, data // 4
    scalar = lambda *values: jnp.stack([jnp.asarray(v, jnp.int32) for v in values])
    at_core, at_side, at_x, at_low, at_high = (
        scalar(v) for v in (core, side, bit_x, bit_low, bit_high)
    )

    def swap(value, axis, bit):
        size = n_seq if axis == "seq" else n_data
        return lax.ppermute(value, axis, [(i, i ^ bit) for i in range(size)])

    def core_swap(value):
        return swap(value, "seq", 1)

    def side_swap(value):
        return swap(value, "seq", 2)

    def x_swap(value):
        return swap(value, "dp", 1)

    far = side_swap(tokens)
    near = core_swap(tokens)
    far_near = core_swap(far)

    window = 4 * rows
    two = 2 * rows
    half = HEAD // 2
    freq = rotary_base ** (-jnp.arange(half, dtype=jnp.float32) * (2.0 / HEAD))
    cosine, sine, seg_col, seg_row = pl.pallas_call(
        tables,
        grid_spec=pltpu.PrefetchScalarGridSpec(
            num_scalar_prefetch=2,
            grid=(1,),
            in_specs=[block((half, TILE))],
            out_specs=[block((window, TILE))] * 3 + [block((8, window))],
        ),
        out_shape=[
            shaped((window, TILE), full), shaped((window, TILE), full),
            shaped((window, TILE), jnp.int32), shaped((8, window), jnp.int32),
        ],
        compiler_params=pltpu.CompilerParams(vmem_limit_bytes=16 * MIB),
        cost_estimate=took("tables"),
        name="tables",
    )(scalar(seq), lengths, jnp.broadcast_to(freq[:, None], (half, TILE)))

    vec = lambda v: v.reshape(1, width)
    third = lambda i: (input_weight, block((width, width), 0, i))
    heads = width // HEAD
    stats = shaped((16, rows), full)
    part = lambda v, i: (v, block((two, TILE), i, 0))
    query_row = (seg_row, block((8, rows), 0, 0))
    res = lambda shape, kind: (shaped(shape, kind), block(shape))
    query, acc, peaks, totals = call(
        first_half, "first_half", at_core,
        [whole(tokens), whole(near), third(0), third(1), third(2),
         part(cosine, 0), part(sine, 0), part(seg_col, 0), query_row],
        [res((rows, width), low), res((width, rows), full), res((16, rows), full), res((16, rows), full)],
        [pltpu.VMEM((two, width), low), pltpu.VMEM((two, width), low), pltpu.VMEM((two, rows), full)],
        mib=24,
    )
    attended_low, normed, normed_low, scaled, inverse = call(
        second_half, "second_half", at_core,
        [whole(tokens), whole(far), whole(far_near), third(1), third(2), whole(output_weight),
         part(cosine, 1), part(sine, 1), part(seg_col, 1), query_row,
         whole(query), whole(acc), whole(peaks), whole(totals), whole(vec(gain_one)), whole(vec(bias_one))],
        [res((rows, width), low), res((rows, width), full), res((rows, width), low),
         res((rows, width), full), res((rows, TILE), full)],
        [pltpu.VMEM((two, width), low), pltpu.VMEM((two, width), low), pltpu.VMEM((two, rows), full),
         pltpu.VMEM((width, rows), full)],
        mib=24,
    )

    def spread_first(value):
        return side_swap(value), x_swap(value)

    def spread_second(got):
        by_side, by_x = got
        return x_swap(by_side[: rows // 2]), side_swap(by_x[rows // 2 :])

    normed_near = spread_first(normed_low)

    steps = 6
    chunk = hidden // steps
    slope_up, slope_gate, result, grad_second, grad_low, sums_two = pl.pallas_call(
        feed_forward,
        grid=(steps,),
        in_specs=[
            block((rows, width)), block((rows, width)),
            pl.BlockSpec((width, chunk), lambda j: (0, j)), pl.BlockSpec((width, chunk), lambda j: (0, j)),
            pl.BlockSpec((chunk, width), lambda j: (j, 0)),
            block((rows, width)), block((1, width)), block((1, width)),
        ],
        out_specs=[
            pl.BlockSpec((rows, chunk), lambda j: (0, j)), pl.BlockSpec((rows, chunk), lambda j: (0, j)),
            block((rows, width)), block((rows, width)), block((rows, width)), block((2, width)),
        ],
        out_shape=[
            shaped((rows, hidden), low), shaped((rows, hidden), low), shaped((rows, width), low),
            shaped((rows, width), full), shaped((rows, width), low), shaped((2, width), full),
        ],
        scratch_shapes=[pltpu.VMEM((rows, width), full)],
        compiler_params=pltpu.CompilerParams(
            vmem_limit_bytes=20 * MIB, dimension_semantics=("arbitrary",)
        ),
        cost_estimate=took("feed_forward"),
        name="feed_forward",
    )(
        normed, normed_low, gate_weight, up_weight, down_weight, cotangent, vec(gain_two), vec(bias_two),
    )
    normed_near, grad_low = lax.optimization_barrier((normed_near, grad_low))
    normed_next = spread_second(normed_near)
    grad_near = spread_first(grad_low)
    group = width // 2
    grad_first, branch_low, mine, other, sums = pl.pallas_call(
        feed_back,
        grid_spec=pltpu.PrefetchScalarGridSpec(
            num_scalar_prefetch=1,
            grid=(steps,),
            in_specs=[
                block((rows, width)), block((rows, width)),
                pl.BlockSpec((rows, chunk), lambda j, p: (0, j)),
                pl.BlockSpec((rows, chunk), lambda j, p: (0, j)),
                pl.BlockSpec((width, chunk), lambda j, p: (0, j)),
                pl.BlockSpec((width, chunk), lambda j, p: (0, j)),
                pl.BlockSpec((chunk, width), lambda j, p: (j, 0)), block((width, width)),
                block((rows, width)), block((rows, TILE)), block((1, width)), block((2, width)),
            ],
            out_specs=[
                block((rows, width)), block((rows, width)), block((rows, group)), block((rows, group)),
                block((8, width)),
            ],
            scratch_shapes=[pltpu.VMEM((rows, width), full)],
        ),
        out_shape=[
            shaped((rows, width), full), shaped((rows, width), low), shaped((rows, group), low),
            shaped((rows, group), low), shaped((8, width), full),
        ],
        compiler_params=pltpu.CompilerParams(
            vmem_limit_bytes=20 * MIB, dimension_semantics=("arbitrary",)
        ),
        cost_estimate=took("feed_back"),
        name="feed_back",
    )(
        at_side, grad_second, grad_low, slope_up, slope_gate, gate_weight, up_weight, down_weight,
        output_weight, scaled, inverse, vec(gain_one), sums_two,
    )
    far_grad = side_swap(other)
    quarter = width // 4
    out_keep, out_send = call(
        out_grad, "out_grad", at_core,
        [whole(branch_low), whole(attended_low)],
        [res((2 * quarter, width), full), res((2 * quarter, width), low)],
        [pltpu.VMEM((width, width), full)],
    )
    out_got = core_swap(out_send)
    out_keep, out_send = call(
        out_halve, "out_halve", at_side,
        [whole(out_keep), whole(out_got), whole(sums)],
        [res((quarter, width), full), res((quarter + 16, width), low)],
    )
    grad_near, far_grad = lax.optimization_barrier((grad_near, far_grad))
    grad_next = spread_second(grad_near)
    out_got = side_swap(out_send)

    tiles = group // TILE

    def back_tile(tile, tokens, earlier):
        at = lambda i: (
            input_weight,
            block((width, TILE), 0, lambda place: 2 * tiles * i + tiles * place[0] + tile),
        )
        cut = lambda v: (v, block((rows, TILE), 0, tile))
        operands = [
            whole(tokens), whole(near), whole(far), whole(far_near), at(0), at(1), at(2),
            cut(mine), cut(far_grad), whole(cosine), whole(sine), whole(seg_col), whole(seg_row),
        ]
        alias = {}
        for i, value in enumerate(earlier):
            alias[1 + len(operands)] = i
            operands.append((value, pl.BlockSpec(memory_space=pl.ANY)))
        return call(
            attend_back, "attend_back", at_side, operands,
            [(shaped((two, group), low), block((two, TILE), 0, tile)),
             (shaped((two, width), low), block((two, 2 * TILE), 0, tile)),
             (shaped((two, width), low), block((two, 2 * TILE), 0, tile)),
             (shaped((3 * group, width), full), block((3 * TILE, width), tile, 0))],
            [pltpu.VMEM((window, TILE), low), pltpu.VMEM((window, TILE), low),
             pltpu.VMEM((two, TILE), low), pltpu.VMEM((window, two), full)],
            mib=32, alias=alias,
        )

    back = ()
    for tile in range(tiles):
        back = back_tile(tile, tokens, back)
    dq, even, odd, grads = back

    odd_got = core_swap(odd)
    far_dq = side_swap(dq[rows:])
    far_kv = side_swap(
        (even[rows:].astype(jnp.float32) + odd_got[rows:].astype(jnp.float32)).astype(low)
    )

    pairs, lones = (0, 2, 2, 4), (4, 5, 0, 1)
    table = lambda values, i: sum(jnp.where(i == k, v, 0) for k, v in enumerate(values))
    mates = seq ^ 1
    in_keep, in_send, sums = call(
        fold, "fold",
        scalar(table(pairs, seq), table(lones, seq), table(pairs, mates), table(lones, mates)),
        [whole(grads), whole(out_got), whole(sums)],
        [res((3 * quarter, width), full), res((3 * quarter + 16, width), low), res((8, width), full)],
        [pltpu.VMEM((3 * group, width), full)],
        mib=24,
    )
    in_got = core_swap(in_send)
    share = width // n_data
    keep, send, sums = call(
        turn_over, "turn_over", at_x,
        [whole(in_keep), whole(in_got), whole(out_keep), whole(out_got), whole(sums)],
        [res((4 * share, width), full), res((4 * share + 16, width), low), res((8, width), full)],
        [pltpu.VMEM((width, width), full)],
        mib=24,
    )
    got = x_swap(send)
    keep, send, sums = call(
        halve, "halve", at_low, [whole(keep), whole(got), whole(sums)],
        [res((2 * share, width), full), res((2 * share + 16, width), low), res((8, width), full)],
    )
    got = swap(send, "dp", 2)
    keep, send, sums = call(
        halve, "halve", at_high, [whole(keep), whole(got), whole(sums)],
        [res((share, width), full), res((share + 16, width), low), res((8, width), full)],
    )
    got = swap(send, "dp", 4)
    in_own, in_send, grad_out, sums = call(
        last_sum, "last_sum", at_high, [whole(keep), whole(got), whole(sums)],
        [res((share, 2 * quarter), full), res((share, quarter), low), res((share, quarter), full),
         res((8, width), full)],
    )
    in_moved = side_swap(in_send).astype(jnp.float32)
    grad_in = jnp.where(
        core == 0,
        jnp.concatenate([in_own, in_moved], axis=1),
        jnp.concatenate([in_moved, in_own], axis=1),
    )

    eighth = hidden // 8
    normed_all = (normed_low,) + tuple(normed_near) + tuple(normed_next)
    grad_all = (grad_low,) + tuple(grad_near) + tuple(grad_next)

    def columns(owner, kind, normed_all):
        start = (2 * (2 * side + owner) + bit_x) * eighth
        gate_cols = lax.dynamic_slice_in_dim(gate_weight, start, eighth, axis=1)
        up_cols = lax.dynamic_slice_in_dim(up_weight, start, eighth, axis=1)
        gate_up = jnp.concatenate([gate_cols.T, up_cols.T], axis=0)
        down_rows = lax.dynamic_slice_in_dim(down_weight, start, eighth, axis=0)
        return call(
            column_grads, "column_grads", at_core,
            [whole(v) for v in normed_all] + [whole(v) for v in grad_all]
            + [whole(gate_up), whole(down_rows)],
            [res((width, 3 * eighth), kind)],
            [pltpu.VMEM((3 * eighth, width), full)],
            mib=32,
        )[0]

    col_send = columns(1 - core, low, normed_all)
    col_got = core_swap(col_send)
    col_keep = columns(core, full, (after(normed_low, col_send),) + normed_all[1:])
    results = []
    for i in range(3):
        third_of = lambda v: (v, block((width, eighth), 0, i))
        keep, send = call(
            first_split, "first_split", at_low, [third_of(col_keep), third_of(col_got)],
            [res((width // 2, eighth), full), res((width // 2, eighth), low)],
        )
        got = swap(send, "dp", 2)
        keep, send = call(
            second_split, "second_split", at_high, [whole(keep), whole(got)],
            [res((width // 4, eighth), full), res((width // 4, eighth), low)],
        )
        results.append((keep, swap(send, "dp", 4)))
    (down,) = call(
        down_sum, "down_sum", at_x, [whole(v) for v in results[2]], [res((width // 4, eighth), low)]
    )
    order = []
    for d in range(n_data):
        for s in range(n_seq):
            order.append((d * n_seq + s, (2 * s + d % 2) * n_seq + d // 2))
    grad_down = lax.ppermute(down, ("dp", "seq"), order).astype(jnp.float32).T
    pair_kept, pair_send = call(
        pair_sum, "pair_sum", at_x, [whole(v) for v in results[0] + results[1]],
        [res((share, 2 * eighth), full), res((share, 2 * eighth), low)],
    )
    pair_got = x_swap(pair_send)
    grad_gate, grad_up = call(
        pair_place, "pair_place", at_x, [whole(pair_kept), whole(pair_got)],
        [res((share, 2 * eighth), full), res((share, 2 * eighth), full)],
    )
    weight_at = lambda i, own: (
        input_weight,
        block((width, group), 0, lambda place: 2 * i + (place[0] if own else 1 - place[0])),
    )
    (grad_tokens,) = call(
        token_grad, "token_grad", at_side,
        [whole(grad_first), whole(dq), whole(even), whole(odd_got), whole(far_dq), whole(far_kv)]
        + [weight_at(i, True) for i in range(3)] + [weight_at(i, False) for i in range(3)],
        [res((rows, width), low)],
        mib=24,
    )
    return (
        result,
        grad_tokens,
        grad_in,
        grad_out,
        grad_gate,
        grad_up,
        grad_down,
        sums[0],
        sums[1],
        sums[2],
        sums[3],
    )


def solution(mesh):
    placed = (
        P(("dp", "seq"), None),
        P(("dp", "seq"), None),
        P("dp", None),
        P(),
        P(),
        P(),
        P(),
        P(),
        P(),
        P(),
        P(),
        P(),
    )
    paired = mesh.shape["seq"] == 4 and mesh.shape["dp"] == 8
    return jax.shard_map(
        fast if paired else general,
        mesh=mesh,
        in_specs=placed,
        out_specs=(
            P(("dp", "seq"), None),
            P(("dp", "seq"), None),
            P("dp", "seq"),
            P("dp", "seq"),
            P("dp", "seq"),
            P("dp", "seq"),
            P("dp", "seq"),
            P(),
            P(),
            P(),
            P(),
        ),
        check_vma=False,
    )
```

```python
import functools
import math

import jax
import jax.numpy as jnp
import numpy as np
from jax import lax
from jax.experimental import pallas as pl
from jax.experimental.pallas import tpu as pltpu
from jax.sharding import PartitionSpec as P

HEAD = 64


norm_eps = 1e-05
rotary_base = 1000.0
masked_value = -1e30


def doc_layout(lengths_row, count):
    ends = jnp.cumsum(lengths_row)
    place = jnp.arange(count, dtype=jnp.int32)
    after = (place[:, None] >= ends[None, :]).astype(jnp.int32)
    segment = jnp.sum(after, axis=1)
    start = jnp.sum(after * lengths_row[None, :], axis=1)
    return (segment, place - start)


def rotate(field, position):
    half = field.shape[-1] // 2
    freq = rotary_base ** (-jnp.arange(half, dtype=jnp.float32) * (2.0 / field.shape[-1]))
    angle = position.astype(jnp.float32)[:, None] * freq[None, :]
    cosine = jnp.cos(angle)[:, None, :]
    sine = jnp.sin(angle)[:, None, :]
    first = field[..., :half]
    second = field[..., half:]
    return jnp.concatenate(
        [first * cosine - second * sine, second * cosine + first * sine], axis=-1
    )


def norm_forward(value, gain, shift):
    mean = jnp.mean(value, axis=-1, keepdims=True)
    centred = value - mean
    inverse = lax.rsqrt(jnp.mean(centred * centred, axis=-1, keepdims=True) + norm_eps)
    scaled = centred * inverse
    return (scaled * gain + shift, scaled, inverse)


def norm_backward(grad, scaled, inverse, gain):
    inner = grad * gain
    back = inverse * (
        inner
        - jnp.mean(inner, axis=-1, keepdims=True)
        - scaled * jnp.mean(inner * scaled, axis=-1, keepdims=True)
    )
    return (back, jnp.sum(grad * scaled, axis=0), jnp.sum(grad, axis=0))


def inner_rows(left, right):
    return lax.dot_general(
        left, right, (((0,), (0,)), ((), ())), preferred_element_type=jnp.float32
    )


def times_transpose(left, right):
    return lax.dot_general(
        left, right, (((1,), (1,)), ((), ())), preferred_element_type=jnp.float32
    )


def general(
    tokens,
    cotangent,
    lengths,
    input_weight,
    output_weight,
    gate_weight,
    up_weight,
    down_weight,
    gain_one,
    bias_one,
    gain_two,
    bias_two,
):
    rows, width = tokens.shape
    heads = width // HEAD
    window = rows * lax.axis_size("seq")
    scale = 1.0 / math.sqrt(HEAD)
    segment_all, position_all = doc_layout(lengths[0], window)
    offset = lax.axis_index("seq") * rows
    seg_mine = lax.dynamic_slice_in_dim(segment_all, offset, rows)
    pos_mine = lax.dynamic_slice_in_dim(position_all, offset, rows)
    projected = jnp.dot(tokens, input_weight, preferred_element_type=jnp.float32)
    query = rotate(projected[:, :width].reshape(rows, heads, HEAD), pos_mine).astype(jnp.bfloat16)
    key = (
        rotate(projected[:, width : 2 * width].reshape(rows, heads, HEAD), pos_mine)
        .astype(jnp.bfloat16)
        .reshape(rows, width)
    )
    value = projected[:, 2 * width :].astype(jnp.bfloat16)

    def scores_for(key_block, seg_block):
        scores = (
            jnp.einsum("qhe,khe->hqk", query, key_block, preferred_element_type=jnp.float32) * scale
        )
        same = (seg_mine[:, None] == seg_block[None, :])[None]
        return (jnp.where(same, scores, masked_value), same)

    def split_blocks(piece, segs):
        count = piece[0].shape[0]
        size = math.gcd(count, 512)
        keys = piece[0].reshape(count // size, size, heads, HEAD)
        values = piece[1].reshape(count // size, size, heads, HEAD)
        return (keys, values, segs.reshape(count // size, size), count, size)

    start_state = (
        jnp.zeros((rows, heads, HEAD), jnp.float32),
        jnp.full((heads, rows), masked_value, jnp.float32),
        jnp.zeros((heads, rows), jnp.float32),
    )
    segs = segment_all
    keys, values, seg_blocks, count, size = split_blocks(
        (
            lax.all_gather(key, "seq", axis=0, tiled=True),
            lax.all_gather(value, "seq", axis=0, tiled=True),
        ),
        segs,
    )

    def forward_step(state, item):
        summed, peak, total = state
        key_block, value_block, seg_block = item
        scores, same = scores_for(key_block, seg_block)
        new_peak = jnp.maximum(peak, jnp.max(scores, axis=-1))
        fade = jnp.exp(peak - new_peak)
        weight = jnp.where(same, jnp.exp(scores - new_peak[..., None]), 0.0)
        total = total * fade + jnp.sum(weight, axis=-1)
        summed = summed * fade.T[..., None] + jnp.einsum(
            "hqk,khe->qhe",
            weight.astype(jnp.bfloat16),
            value_block,
            preferred_element_type=jnp.float32,
        )
        return ((summed, new_peak, total), None)

    state, unused = lax.scan(forward_step, start_state, (keys, values, seg_blocks))
    summed, peak, total = state
    attended = (summed / total.T[..., None]).reshape(rows, width)
    attended_low = attended.astype(jnp.bfloat16)
    first = tokens.astype(jnp.float32) + jnp.dot(
        attended_low, output_weight, preferred_element_type=jnp.float32
    )
    normed, scaled_one, inverse_one = norm_forward(first, gain_one, bias_one)
    normed_low = normed.astype(jnp.bfloat16)
    gate = jnp.dot(normed_low, gate_weight, preferred_element_type=jnp.float32)
    upward = jnp.dot(normed_low, up_weight, preferred_element_type=jnp.float32)
    sigma = jax.nn.sigmoid(gate)
    activated = gate * sigma
    hidden_low = (activated * upward).astype(jnp.bfloat16)
    second = normed + jnp.dot(hidden_low, down_weight, preferred_element_type=jnp.float32)
    result, scaled_two, inverse_two = norm_forward(second, gain_two, bias_two)
    grad_second, grad_gain_two, grad_bias_two = norm_backward(
        cotangent.astype(jnp.float32), scaled_two, inverse_two, gain_two
    )
    grad_ff_low = grad_second.astype(jnp.bfloat16)
    grad_hidden = times_transpose(grad_ff_low, down_weight)
    grad_gate_low = (grad_hidden * upward * (sigma * (1.0 + gate * (1.0 - sigma)))).astype(
        jnp.bfloat16
    )
    grad_up_low = (grad_hidden * activated).astype(jnp.bfloat16)
    grad_normed = (
        grad_second
        + times_transpose(grad_gate_low, gate_weight)
        + times_transpose(grad_up_low, up_weight)
    )
    grad_first, grad_gain_one, grad_bias_one = norm_backward(
        grad_normed, scaled_one, inverse_one, gain_one
    )
    grad_branch_low = grad_first.astype(jnp.bfloat16)
    grad_attended_low = times_transpose(grad_branch_low, output_weight).astype(jnp.bfloat16)
    grad_heads = grad_attended_low.reshape(rows, heads, HEAD)
    delta = jnp.sum(
        (grad_attended_low.astype(jnp.float32) * attended).reshape(rows, heads, HEAD), axis=-1
    ).T
    zero_query = jnp.zeros((rows, heads, HEAD), jnp.float32)
    grad_acc = zero_query
    segs = segment_all
    grad_query = grad_acc
    keys, values, seg_blocks, count, size = split_blocks(
        (
            lax.all_gather(key, "seq", axis=0, tiled=True),
            lax.all_gather(value, "seq", axis=0, tiled=True),
        ),
        segs,
    )

    def backward_step(grad_acc, item):
        key_block, value_block, seg_block = item
        scores, same = scores_for(key_block, seg_block)
        prob = jnp.where(same, jnp.exp(scores - peak[..., None]) / total[..., None], 0.0)
        prob_grad = jnp.einsum(
            "qhe,khe->hqk", grad_heads, value_block, preferred_element_type=jnp.float32
        )
        score_grad = (prob * (prob_grad - delta[..., None])).astype(jnp.bfloat16)
        grad_acc = (
            grad_acc
            + jnp.einsum("hqk,khe->qhe", score_grad, key_block, preferred_element_type=jnp.float32)
            * scale
        )
        prob_low = prob.astype(jnp.bfloat16)
        key_grad = (
            jnp.einsum("hqk,qhe->khe", score_grad, query, preferred_element_type=jnp.float32)
            * scale
        )
        value_grad = jnp.einsum(
            "hqk,qhe->khe", prob_low, grad_heads, preferred_element_type=jnp.float32
        )
        return (grad_acc, (key_grad.reshape(size, width), value_grad.reshape(size, width)))

    grad_query, outputs = lax.scan(backward_step, grad_query, (keys, values, seg_blocks))
    grad_acc = grad_query
    key_part = outputs[0].reshape(count, width)
    value_part = outputs[1].reshape(count, width)
    grad_key, grad_value = (
        lax.psum_scatter(
            key_part.astype(jnp.bfloat16), "seq", scatter_dimension=0, tiled=True
        ).astype(jnp.float32),
        lax.psum_scatter(
            value_part.astype(jnp.bfloat16), "seq", scatter_dimension=0, tiled=True
        ).astype(jnp.float32),
    )
    query_back = rotate(grad_acc, -pos_mine).reshape(rows, width)
    key_back = rotate(grad_key.reshape(rows, heads, HEAD), -pos_mine).reshape(rows, width)
    grad_projected_low = jnp.concatenate([query_back, key_back, grad_value], axis=1).astype(
        jnp.bfloat16
    )
    grad_tokens = (grad_first + times_transpose(grad_projected_low, input_weight)).astype(
        jnp.bfloat16
    )
    column_grads = (
        lax.all_to_all(grad_projected_low, "seq", split_axis=1, concat_axis=0, tiled=True),
        lax.all_to_all(grad_branch_low, "seq", split_axis=1, concat_axis=0, tiled=True),
        lax.all_to_all(grad_gate_low, "seq", split_axis=1, concat_axis=0, tiled=True),
        lax.all_to_all(grad_up_low, "seq", split_axis=1, concat_axis=0, tiled=True),
        lax.all_to_all(grad_ff_low, "seq", split_axis=1, concat_axis=0, tiled=True),
    )
    tok_rows = lax.all_gather(tokens, "seq", axis=0, tiled=True)
    normed_rows = lax.all_gather(normed_low, "seq", axis=0, tiled=True)
    attended_rows = lax.all_gather(attended_low, "seq", axis=0, tiled=True)
    hidden_rows = lax.all_gather(hidden_low, "seq", axis=0, tiled=True)
    count = tok_rows.shape[0]
    cols = [member for member in column_grads]
    summed_grads = (
        lax.psum_scatter(
            inner_rows(tok_rows, cols[0]).astype(jnp.bfloat16),
            "dp",
            scatter_dimension=0,
            tiled=True,
        ).astype(jnp.float32),
        lax.psum_scatter(
            inner_rows(attended_rows, cols[1]).astype(jnp.bfloat16),
            "dp",
            scatter_dimension=0,
            tiled=True,
        ).astype(jnp.float32),
        lax.psum_scatter(
            inner_rows(normed_rows, cols[2]).astype(jnp.bfloat16),
            "dp",
            scatter_dimension=0,
            tiled=True,
        ).astype(jnp.float32),
        lax.psum_scatter(
            inner_rows(normed_rows, cols[3]).astype(jnp.bfloat16),
            "dp",
            scatter_dimension=0,
            tiled=True,
        ).astype(jnp.float32),
        lax.psum_scatter(
            inner_rows(hidden_rows, cols[4]).astype(jnp.bfloat16),
            "dp",
            scatter_dimension=0,
            tiled=True,
        ).astype(jnp.float32),
    )
    norm_grads = lax.psum(
        (grad_gain_one, grad_bias_one, grad_gain_two, grad_bias_two), ("dp", "seq")
    )
    return (
        result.astype(jnp.bfloat16),
        grad_tokens,
        summed_grads[0],
        summed_grads[1],
        summed_grads[2],
        summed_grads[3],
        summed_grads[4],
        norm_grads[0],
        norm_grads[1],
        norm_grads[2],
        norm_grads[3],
    )


low = jnp.bfloat16
full = jnp.float32
TILE = 128
MIB = 1024 * 1024


def nn(left, right):
    return lax.dot_general(
        left, right, (((1,), (0,)), ((), ())), preferred_element_type=jnp.float32
    )


def nt(left, right):
    return lax.dot_general(
        left, right, (((1,), (1,)), ((), ())), preferred_element_type=jnp.float32
    )


def tn(left, right):
    return lax.dot_general(
        left, right, (((0,), (0,)), ((), ())), preferred_element_type=jnp.float32
    )


def block(shape, *at):
    at = at or (0,) * len(shape)

    def index(*args):
        return tuple(a(*args[1:]) if callable(a) else a for a in at)

    return pl.BlockSpec(tuple(shape), index)


def shaped(shape, kind):
    return jax.ShapeDtypeStruct(tuple(shape), kind)


SEQ, SIDE, X, LOW, HIGH, PAIR, LONE, OTHER_PAIR, OTHER_LONE, OWN, OTHER, CORE = range(12)

COST = {
    "tables": 1.5, "first_half": 6.9, "second_half": 7.9, "feed_forward": 8.4, "feed_back": 8.6,
    "project_heads": 4, "back_one": 6.5, "back_rest": 7, "column_grads": 7.5, "token_grad": 3,
    "out_grad": 1.2,
}


def took(name):
    return pl.CostEstimate(flops=int(COST.get(name, 0.5) * 10**9), bytes_accessed=1, transcendentals=0)


def still(value):
    return pltpu.with_memory_space_constraint(value, pltpu.HBM)


def call(body, name, scalars, operands, results, scratch=(), mib=16):
    return pl.pallas_call(
        body,
        grid_spec=pltpu.PrefetchScalarGridSpec(
            num_scalar_prefetch=1,
            grid=(1,),
            in_specs=[spec for unused, spec in operands],
            out_specs=[spec for unused, spec in results],
            scratch_shapes=list(scratch),
        ),
        out_shape=[shape for shape, unused in results],
        compiler_params=pltpu.CompilerParams(
            vmem_limit_bytes=mib * MIB, dimension_semantics=("arbitrary",)
        ),
        cost_estimate=took(name),
        name=name,
    )(scalars, *[value for value, unused in operands])


def whole(value):
    return (value, block(value.shape))


def turn(field, cosine, sine):
    lane = lax.broadcasted_iota(jnp.int32, field.shape, 1)
    half = HEAD // 2
    other = jnp.where(
        lane % HEAD < half, pltpu.roll(field, TILE - half, 1), pltpu.roll(field, half, 1)
    )
    return field * cosine + other * sine


def one_head(pair, which):
    lane = lax.broadcasted_iota(jnp.int32, pair.shape, 1)
    return jnp.where((lane // HEAD) == which, pair, jnp.zeros_like(pair))


def pack(sums):
    high = sums.astype(low)
    return jnp.concatenate([high, (sums - high.astype(jnp.float32)).astype(low)], axis=0)


def unpack(packed):
    wide = packed.astype(jnp.float32)
    return wide[:8] + wide[8:]


def tables(place, lengths, freq, cosine, sine, seg_col, seg_row):
    count = cosine.shape[0]
    rows = count // 4
    lane = lax.broadcasted_iota(jnp.int32, (8, count), 1)
    index = jnp.zeros_like(lane)
    for i in range(1, 4):
        index = index + (lane >= i * rows).astype(jnp.int32)
    spot = (index ^ place[SEQ]) * rows + (lane - index * rows)
    end = jnp.int32(0)
    segment = jnp.zeros_like(lane)
    start = jnp.zeros_like(lane)
    for i in range(lengths.shape[1]):
        length = lengths[0, i]
        end = end + length
        past = (spot >= end).astype(jnp.int32)
        segment = segment + past
        start = start + past * length
    position = (spot - start).astype(jnp.float32)
    angle = freq[:, :1] * position[:1]
    c, s = jnp.cos(angle), jnp.sin(angle)
    cosine[...] = jnp.concatenate([c] * 4, axis=0).T
    sine[...] = jnp.concatenate([-s, s] * 2, axis=0).T
    seg_row[...] = segment
    wide = jnp.broadcast_to(segment[:1].astype(jnp.float32), (TILE, count))
    seg_col[...] = wide.T.astype(jnp.int32)


def put_keys(tokens, wk, wv, cosine, sine, keys, values, start):
    rows = tokens.shape[0]
    projected = nn(tokens, wk)
    for tile in range(projected.shape[1] // TILE):
        cols = slice(tile * TILE, (tile + 1) * TILE)
        keys[start : start + rows, cols] = turn(projected[:, cols], cosine, sine).astype(low)
    values[start : start + rows, :] = nn(tokens, wv).astype(low)


def put_query(tokens, wq, cosine, sine, query):
    scale = 1.0 / math.sqrt(HEAD)
    projected = nn(tokens, wq)
    for tile in range(projected.shape[1] // TILE):
        cols = slice(tile * TILE, (tile + 1) * TILE)
        turned = turn(projected[:, cols], cosine, sine)
        query[:, cols] = (turned.astype(low) * scale).astype(low)


def attend(query, keys, values, bias):
    for tile in range(query.shape[1] // TILE):
        cols = slice(tile * TILE, (tile + 1) * TILE)
        key_pair = keys[:, cols]
        value_pair = values[:, cols]
        for which in range(TILE // HEAD):
            scores = nt(key_pair, one_head(query[:, cols], which)) + bias[...]
            peak = jnp.max(scores, axis=0, keepdims=True)
            weight = jnp.exp(scores - peak)
            total = jnp.sum(weight, axis=0, keepdims=True)
            out = tn(value_pair, weight.astype(low))[which * HEAD : (which + 1) * HEAD]
            yield tile * (TILE // HEAD) + which, out, peak, total


def first_half(
    place, own, near, wq, wk, wv, cosine, sine, seg_key, seg_query, query, acc, peaks, totals,
    keys, values, bias,
):
    rows = own.shape[0]
    put_query(own[...], wq[...], cosine[:rows, :], sine[:rows, :], query)
    put_keys(own[...], wk[...], wv[...], cosine[:rows, :], sine[:rows, :], keys, values, 0)
    put_keys(near[...], wk[...], wv[...], cosine[rows:, :], sine[rows:, :], keys, values, rows)
    bias[...] = jnp.where(seg_key[:, :1] == seg_query[:1, :], 0.0, masked_value)
    for head, out, peak, total in attend(query, keys, values, bias):
        acc[head * HEAD : (head + 1) * HEAD, :] = out
        peaks[head : head + 1, :] = peak
        totals[head : head + 1, :] = total


def second_half(
    place, own, far, far_near, wk, wv, wo, cosine, sine, seg_key, seg_query, query, acc, peaks, totals,
    gain, shift, attended_low, normed, normed_low, scaled, inverse, keys, values, bias, turned,
):
    rows, width = own.shape
    put_keys(far[...], wk[...], wv[...], cosine[:rows, :], sine[:rows, :], keys, values, 0)
    put_keys(far_near[...], wk[...], wv[...], cosine[rows:, :], sine[rows:, :], keys, values, rows)
    bias[...] = jnp.where(seg_key[:, :1] == seg_query[:1, :], 0.0, masked_value)
    for head, out, peak, total in attend(query, keys, values, bias):
        part = slice(head * HEAD, (head + 1) * HEAD)
        before = peaks[head : head + 1, :]
        best = jnp.maximum(before, peak)
        fade = jnp.exp(before - best)
        grow = jnp.exp(peak - best)
        inverse_total = 1.0 / (totals[head : head + 1, :] * fade + total * grow)
        turned[part, :] = acc[part, :] * (fade * inverse_total) + out * (grow * inverse_total)
    attended = turned[...].T.astype(low)
    attended_low[...] = attended
    first = own[...].astype(jnp.float32) + nn(attended, wo[...])
    mean = jnp.mean(first, axis=1, keepdims=True)
    centred = first - mean
    spread = lax.rsqrt(jnp.mean(centred * centred, axis=1, keepdims=True) + norm_eps)
    unit = centred * spread
    value = unit * gain[...][None, :] + shift[...][None, :]
    scaled[...] = unit
    inverse[...] = jnp.broadcast_to(spread, (rows, TILE))
    normed[...] = value
    normed_low[...] = value.astype(low)


def feed_forward(
    normed, normed_low, wg, wu, wd, cotangent, gain, shift,
    slope_up, slope_gate, result, grad_second, grad_low, sums, acc,
):
    step = pl.program_id(0)
    gate = nn(normed_low[...], wg[...])
    upward = nn(normed_low[...], wu[...])
    sigma = jax.nn.sigmoid(gate)
    active = gate * sigma
    slope_up[...] = active.astype(low)
    slope_gate[...] = (upward * (sigma * (1.0 + gate * (1.0 - sigma)))).astype(low)
    product = nn((active * upward).astype(low), wd[...])

    @pl.when(step == 0)
    def _():
        acc[...] = normed[...] + product

    @pl.when(step > 0)
    def _():
        acc[...] += product

    @pl.when(step == pl.num_programs(0) - 1)
    def _():
        second = acc[...]
        mean = jnp.mean(second, axis=1, keepdims=True)
        centred = second - mean
        spread = lax.rsqrt(jnp.mean(centred * centred, axis=1, keepdims=True) + norm_eps)
        unit = centred * spread
        result[...] = (unit * gain[...][None, :] + shift[...][None, :]).astype(low)
        grad = cotangent[...].astype(jnp.float32)
        inner = grad * gain[...][None, :]
        back = spread * (
            inner
            - jnp.mean(inner, axis=1, keepdims=True)
            - unit * jnp.mean(inner * unit, axis=1, keepdims=True)
        )
        grad_second[...] = back
        grad_low[...] = back.astype(low)
        sums[0:1, :] = jnp.sum(grad * unit, axis=0, keepdims=True)
        sums[1:2, :] = jnp.sum(grad, axis=0, keepdims=True)


def feed_back(
    place, grad_second, grad_low, slope_up, slope_gate, wg, wu, wd, wo, scaled, inverse, gain, sums_two,
    grad_first, branch_low, mine, other, sums, acc,
):
    step = pl.program_id(0)
    hidden = nt(grad_low[...], wd[...])
    gate = (hidden * slope_gate[...].astype(jnp.float32)).astype(low)
    upward = (hidden * slope_up[...].astype(jnp.float32)).astype(low)
    product = nt(gate, wg[...]) + nt(upward, wu[...])

    @pl.when(step == 0)
    def _():
        acc[...] = grad_second[...] + product

    @pl.when(step > 0)
    def _():
        acc[...] += product

    @pl.when(step == pl.num_programs(0) - 1)
    def _():
        grad = acc[...]
        unit = scaled[...]
        inner = grad * gain[...][None, :]
        back = inverse[:, :1] * (
            inner
            - jnp.mean(inner, axis=1, keepdims=True)
            - unit * jnp.mean(inner * unit, axis=1, keepdims=True)
        )
        grad_first[...] = back
        branch_low[...] = back.astype(low)
        attended_grad = nt(branch_low[...], wo[...]).astype(low)
        group = mine.shape[1]
        height = mine.shape[0]
        left, right = attended_grad[:, :group], attended_grad[:, group:]
        second_side = place[SIDE] > 0
        mine[...] = jnp.where(second_side, right, left)
        other[:height, :] = jnp.where(second_side, left, right)
        sums[...] = jnp.zeros_like(sums)
        sums[0:1, :] = jnp.sum(grad * unit, axis=0, keepdims=True)
        sums[1:2, :] = jnp.sum(grad, axis=0, keepdims=True)
        sums[2:4, :] = sums_two[...]
        for i in range(2):
            part = slice(height + i * 16, height + (i + 1) * 16)
            other[part, :] = pack(sums[:, i * group : (i + 1) * group])


def rows_at(index, count):
    return pl.ds(pl.multiple_of(index * count, count), count)


def out_grad(place, branch_low, attended_low, keep, send, turned):
    turned[...] = tn(branch_low[...], attended_low[...])
    quarter = turned.shape[0] // 4
    core = place[CORE]
    for i in range(2):
        to = slice(i * quarter, (i + 1) * quarter)
        keep[to, :] = turned[rows_at(2 * i + core, quarter), :]
        send[to, :] = turned[rows_at(2 * i + 1 - core, quarter), :].astype(low)


def out_halve(place, keep, got, kept, send):
    quarter = keep.shape[0] // 2
    mine, other = rows_at(place[SIDE], quarter), rows_at(1 - place[SIDE], quarter)
    kept[...] = keep[mine, :] + got[mine, :].astype(jnp.float32)
    send[...] = (keep[other, :] + got[other, :].astype(jnp.float32)).astype(low)


def project_heads(
    place, own, near, far, far_near, wq, wk, wv, cosine, sine, keys, values, query,
):
    rows = own.shape[0]
    scale = 1.0 / math.sqrt(HEAD)
    for index, tokens in enumerate((own, near, far, far_near)):
        part = slice(index * rows, (index + 1) * rows)
        put_keys(tokens[...], wk[...], wv[...], cosine[part, :], sine[part, :], keys, values, index * rows)
        if index % 2 == 0:
            to = slice(index // 2 * rows, (index // 2 + 1) * rows)
            projected = nn(tokens[...], wq[...])
            for tile in range(projected.shape[1] // TILE):
                cols = slice(tile * TILE, (tile + 1) * TILE)
                turned = turn(projected[:, cols], cosine[part, :], sine[part, :])
                query[to, cols] = (turned.astype(low) * scale).astype(low)


def back_tile(key_pair, value_pair, query_pair, grad_pair, bias):
    scale = 1.0 / math.sqrt(HEAD)
    grad_key = None
    grad_value = None
    pieces = []
    for which in range(TILE // HEAD):
        query_head = one_head(query_pair, which)
        grad_head = one_head(grad_pair, which)
        scores = nt(key_pair, query_head) + bias[...]
        weight = jnp.exp(scores - jnp.max(scores, axis=0, keepdims=True))
        prob = weight * (1.0 / jnp.sum(weight, axis=0, keepdims=True))
        prob_grad = nt(value_pair, grad_head)
        product = prob * prob_grad
        delta = jnp.sum(product, axis=0, keepdims=True)
        score_grad = (product - prob * delta).astype(low)
        value_part = nn(prob.astype(low), grad_head)
        key_part = nn(score_grad, query_head)
        grad_key = key_part if grad_key is None else grad_key + key_part
        grad_value = value_part if grad_value is None else grad_value + value_part
        pieces.append(tn(key_pair, score_grad)[which * HEAD : (which + 1) * HEAD])
    return jnp.concatenate(pieces, axis=0).T * scale, grad_key, grad_value


def back_some(tiles, first, place, *refs):
    (own, near, far, far_near, keys, values, query, own_grad, far_grad, cosine, sine, seg_key, seg_query) = refs[:13]
    rows = own.shape[0]
    blocks = (own, near, far, far_near)
    if first:
        dq, both, grads, bias, back = refs[13:]
    else:
        before, sums = refs[13:19], refs[19]
        dq, even, keep, send, kept_sums, bias, back, both, grads = refs[20:]
    group = keys.shape[1]
    for index in range(2):
        part = slice(2 * index * rows, (2 * index + 1) * rows)
        to = slice(index * rows, (index + 1) * rows)
        bias[:, to] = jnp.where(seg_key[:, :1] == seg_query[:1, part], 0.0, masked_value)
    back[:rows, :] = own_grad[...]
    back[rows:, :] = far_grad[:rows, :]
    for tile in tiles:
        cols = slice(tile * TILE, (tile + 1) * TILE)
        grad_query, grad_key, grad_value = back_tile(
            keys[:, cols], values[:, cols], query[:, cols], back[:, cols], bias
        )
        to = slice(0, TILE) if first else cols
        shifted = slice(TILE, 2 * TILE) if first else slice(group + tile * TILE, group + (tile + 1) * TILE)
        for index in range(2):
            part = slice(index * rows, (index + 1) * rows)
            at = slice(2 * index * rows, (2 * index + 1) * rows)
            dq[part, to] = turn(grad_query[part], cosine[at, :], -sine[at, :]).astype(low)
        both[:, to] = turn(grad_key, cosine[...], -sine[...]).astype(low)
        both[:, shifted] = grad_value.astype(low)
        pair = jnp.concatenate([both[:, to], both[:, shifted]], axis=1)
        total = None
        for index in range(4):
            part = slice(index * rows, (index + 1) * rows)
            product = tn(pair[part], blocks[index][...])
            total = product if total is None else total + product
        query_rows = tn(dq[:rows, to], own[...]) + tn(dq[rows:, to], far[...])
        if first:
            grads[:TILE, :] = query_rows
            grads[TILE:, :] = total
        else:
            grads[tile * TILE : (tile + 1) * TILE, :] = query_rows
            for kind in range(2):
                at = (kind + 1) * group + tile * TILE
                grads[at : at + TILE, :] = total[kind * TILE : (kind + 1) * TILE]
    if first:
        return
    for tile in range(2):
        dq_before, both_before, grads_before = before[3 * tile : 3 * tile + 3]
        dq[:, tile * TILE : (tile + 1) * TILE] = dq_before[...]
        for kind in range(3):
            at = kind * group + tile * TILE
            if kind < 2:
                both[:, at : at + TILE] = both_before[:, kind * TILE : (kind + 1) * TILE]
            grads[at : at + TILE, :] = grads_before[kind * TILE : (kind + 1) * TILE, :]
    for index in range(4):
        part = slice(index * rows, (index + 1) * rows)
        to = slice(index // 2 * rows, (index // 2 + 1) * rows)
        if index % 2 == 0:
            even[to, :] = both[part, :]
        else:
            send[to, :] = both[part, :]
    quarter = keep.shape[0] // 3
    pair, lone, other_pair, other_lone = (place[i] for i in (PAIR, LONE, OTHER_PAIR, OTHER_LONE))
    for i in range(3):
        to = slice(i * quarter, (i + 1) * quarter)
        keep[to, :] = grads[rows_at(pair + i if i < 2 else lone, quarter), :]
        to = slice(2 * rows + i * quarter, 2 * rows + (i + 1) * quarter)
        send[to, :] = grads[rows_at(other_pair + i if i < 2 else other_lone, quarter), :].astype(low)
    got = jnp.concatenate([unpack(far_grad[-32:-16, :]), unpack(far_grad[-16:, :])], axis=1)
    total = sums[...] + got
    kept_sums[...] = total
    send[2 * rows + 3 * quarter :, :] = pack(total)


def turn_over(place, keep, got, out_keep, out_got, sums, kept, send, kept_sums, turned):
    height = keep.shape[0]
    first = got.shape[0] - height - 16
    total = keep[...] + got[first : first + height, :].astype(jnp.float32)
    turned[:, :height] = total.T
    turned[:, height:] = (out_keep[...] + out_got[...].astype(jnp.float32)).T
    bit = place[X]
    part = turned.shape[0] // 8
    for i in range(4):
        to = slice(i * part, (i + 1) * part)
        kept[to, :] = turned[rows_at(2 * i + bit, part), :]
        send[to, :] = turned[rows_at(2 * i + 1 - bit, part), :].astype(low)
    both = sums[...] + unpack(got[first + height :, :])
    kept_sums[...] = both
    send[4 * part :, :] = pack(both)


def halve(which, place, keep, got, sums, kept, send, kept_sums):
    bit = place[which]
    height = keep.shape[0]
    count = 2 if height > 192 else 1
    part = height // (2 * count)
    for i in range(count):
        to = slice(i * part, (i + 1) * part)
        mine, other = rows_at(2 * i + bit, part), rows_at(2 * i + 1 - bit, part)
        kept[to, :] = keep[mine, :] + got[mine, :].astype(jnp.float32)
        send[to, :] = (keep[other, :] + got[other, :].astype(jnp.float32)).astype(low)
    both = sums[...] + unpack(got[height:, :])
    kept_sums[...] = both
    send[count * part :, :] = pack(both)


def last_sum(place, keep, got, sums, own, send, out, *vectors):
    height = keep.shape[0]
    total = keep[...] + got[:height, :].astype(jnp.float32)
    quarter = out.shape[1]
    own[...] = total[:, : 2 * quarter]
    send[...] = total[:, 2 * quarter : 3 * quarter].astype(low)
    out[...] = total[:, 3 * quarter :]
    both = sums[...] + unpack(got[height:, :])
    for i, vector in enumerate(vectors):
        vector[...] = both[i]


def column_grads(last, place, *refs):
    count = 4
    rows_refs, back_refs = refs[:count], refs[count : 2 * count]
    wg, wu, wd = refs[2 * count : 2 * count + 3]
    rest = refs[2 * count + 3 :]
    if last:
        earlier = (rest[0], rest[-1])
        outs, wgu, acc = rest[1:4], rest[4], rest[5]
    else:
        outs, wgu, acc = rest[:1], rest[1], rest[2]
    half, width = wd.shape
    wgu[:half, :] = wg[...].astype(jnp.float32).T.astype(low)
    wgu[half:, :] = wu[...].astype(jnp.float32).T.astype(low)
    for step in range(count):
        rows = rows_refs[step][...]
        back = back_refs[step][...]
        both = nt(wgu[...], rows)
        gate, upward = both[:half], both[half:]
        sigma = jax.nn.sigmoid(gate)
        active = gate * sigma
        hidden = (active * upward).astype(low)
        grad_hidden = nt(wd[...], back)
        grad_gate = (grad_hidden * upward * (sigma * (1.0 + gate * (1.0 - sigma)))).astype(low)
        grad_up = (grad_hidden * active).astype(low)
        products = (nn(grad_gate, rows), nn(grad_up, rows), nn(hidden, back))
        for i, product in enumerate(products):
            part = slice(i * half, (i + 1) * half)
            if step == 0:
                acc[part, :] = product
            else:
                acc[part, :] += product
    if last:
        got, total = earlier
        bit = place[LOW]
        cut = width // 4
        for i in range(3):
            part = slice(i * half, (i + 1) * half)
            total[...] = acc[part, :].T + got[:, part].astype(jnp.float32)
            for upper in range(2):
                to = slice(upper * cut, (upper + 1) * cut)
                outs[0][to, part] = total[rows_at(2 * upper + bit, cut), :]
                sent = total[rows_at(2 * upper + 1 - bit, cut), :].astype(low)
                if i < 2:
                    outs[1][to, part] = sent
                else:
                    outs[2][to, :] = sent
    else:
        for i in range(3):
            part = slice(i * half, (i + 1) * half)
            outs[0][:, part] = acc[part, :].T.astype(low)


def second_split(place, keep, got, kept, send):
    bit = place[HIGH]
    part = keep.shape[0] // 2
    mine, other = rows_at(bit, part), rows_at(1 - bit, part)
    kept[...] = keep[mine, :] + got[mine, :].astype(jnp.float32)
    send[...] = (keep[other, :] + got[other, :].astype(jnp.float32)).astype(low)


def down_sum(place, keep, got, out):
    out[...] = (keep[...] + got[...].astype(jnp.float32)).astype(low)


def turned_back(place, got, out):
    out[...] = got[...].astype(jnp.float32).T


def in_place(place, own, moved, out):
    got = moved[...].astype(jnp.float32)
    first = jnp.concatenate([own[...], got], axis=1)
    second = jnp.concatenate([got, own[...]], axis=1)
    out[...] = jnp.where(place[CORE] == 0, first, second)


def pair_sum(place, keep, got, kept, send):
    part = kept.shape[0]
    mine, other = rows_at(place[X], part), rows_at(1 - place[X], part)
    kept[...] = keep[mine, :] + got[mine, :].astype(jnp.float32)
    send[...] = (keep[other, :] + got[other, :].astype(jnp.float32)).astype(low)


def pair_place(place, kept, got, gate, upward):
    half = kept.shape[1] // 2
    for i, out in enumerate((gate, upward)):
        cols = slice(i * half, (i + 1) * half)
        out[:, rows_at(place[X], half)] = kept[:, cols]
        out[:, rows_at(1 - place[X], half)] = got[:, cols].astype(jnp.float32)


def far_pack(place, dq, even, got, out):
    rows, group = out.shape[0], dq.shape[1]
    out[:, :group] = dq[rows:, :]
    total = even[rows:, :].astype(jnp.float32) + got[rows : 2 * rows, :].astype(jnp.float32)
    out[:, group:] = total.astype(low)


def token_grad(place, grad_first, dq, even, got, far_part, *refs):
    weights, out = refs[:-1], refs[-1]
    rows = grad_first.shape[0]
    kind = len(weights) // 2
    total = grad_first[...]
    key_value = (
        even[:rows, :].astype(jnp.float32) + got[:rows, :].astype(jnp.float32)
    ).astype(low)
    group = dq.shape[1]
    for i in range(kind):
        cols = slice(i * group, (i + 1) * group)
        mine = dq[:rows, :] if i == 0 else key_value[:, (i - 1) * group : i * group]
        total = total + nt(mine, weights[i][...]) + nt(far_part[:, cols], weights[kind + i][...])
    out[...] = total.astype(low)


def after(value, *others):
    return lax.optimization_barrier((value,) + others)[0]


def fast(
    tokens,
    cotangent,
    lengths,
    input_weight,
    output_weight,
    gate_weight,
    up_weight,
    down_weight,
    gain_one,
    bias_one,
    gain_two,
    bias_two,
):
    rows, width = tokens.shape
    hidden = gate_weight.shape[1]
    seq = lax.axis_index("seq")
    data = lax.axis_index("dp")
    n_seq, n_data = lax.axis_size("seq"), lax.axis_size("dp")
    core, side = seq % 2, seq // 2
    bit_x, bit_low, bit_high = data % 2, (data // 2) % 2, data // 4
    pairs, lones = (0, 2, 2, 4), (4, 5, 0, 1)
    table = lambda values, i: sum(jnp.where(i == k, v, 0) for k, v in enumerate(values))
    place = jnp.stack(
        [
            jnp.asarray(v, jnp.int32)
            for v in (
                seq, side, bit_x, bit_low, bit_high,
                table(pairs, seq), table(lones, seq), table(pairs, seq ^ 1), table(lones, seq ^ 1),
                2 * seq + bit_x, 2 * (seq ^ 1) + bit_x, core,
            )
        ]
    )

    def swap(value, axis, bit):
        size = n_seq if axis == "seq" else n_data
        return lax.ppermute(value, axis, [(i, i ^ bit) for i in range(size)])

    def core_swap(value):
        return swap(value, "seq", 1)

    def side_swap(value):
        return swap(value, "seq", 2)

    def x_swap(value):
        return swap(value, "dp", 1)

    far = side_swap(tokens)
    near = core_swap(tokens)

    window = 4 * rows
    two = 2 * rows
    half = HEAD // 2
    freq = rotary_base ** (-jnp.arange(half, dtype=jnp.float32) * (2.0 / HEAD))
    cosine, sine, seg_col, seg_row = pl.pallas_call(
        tables,
        grid_spec=pltpu.PrefetchScalarGridSpec(
            num_scalar_prefetch=2,
            grid=(1,),
            in_specs=[block((half, TILE))],
            out_specs=[block((window, TILE))] * 3 + [block((8, window))],
        ),
        out_shape=[
            shaped((window, TILE), full), shaped((window, TILE), full),
            shaped((window, TILE), jnp.int32), shaped((8, window), jnp.int32),
        ],
        compiler_params=pltpu.CompilerParams(vmem_limit_bytes=16 * MIB),
        cost_estimate=took("tables"),
        name="tables",
    )(place, lengths, jnp.broadcast_to(freq[:, None], (half, TILE)))

    third = lambda i: (input_weight, block((width, width), 0, i))
    heads = width // HEAD
    stats = shaped((16, rows), full)
    part = lambda v, i: (v, block((two, TILE), i, 0))
    query_row = (seg_row, block((8, rows), 0, 0))
    res = lambda shape, kind: (shaped(shape, kind), block(shape))
    query, acc, peaks, totals = call(
        first_half, "first_half", place,
        [whole(tokens), whole(near), third(0), third(1), third(2),
         part(cosine, 0), part(sine, 0), part(seg_col, 0), query_row],
        [res((rows, width), low), res((width, rows), full), res((16, rows), full), res((16, rows), full)],
        [pltpu.VMEM((two, width), low), pltpu.VMEM((two, width), low), pltpu.VMEM((two, rows), full)],
        mib=24,
    )
    far_near = core_swap(after(far, peaks))
    attended_low, normed, normed_low, scaled, inverse = call(
        second_half, "second_half", place,
        [whole(tokens), whole(far), whole(far_near), third(1), third(2), whole(output_weight),
         part(cosine, 1), part(sine, 1), part(seg_col, 1), query_row,
         whole(query), whole(acc), whole(peaks), whole(totals), whole(gain_one), whole(bias_one)],
        [res((rows, width), low), res((rows, width), full), res((rows, width), low),
         res((rows, width), full), res((rows, TILE), full)],
        [pltpu.VMEM((two, width), low), pltpu.VMEM((two, width), low), pltpu.VMEM((two, rows), full),
         pltpu.VMEM((width, rows), full)],
        mib=24,
    )

    def spread(value):
        corner = [
            (d * n_seq + s, (d ^ 1) * n_seq + (s ^ 2)) for d in range(n_data) for s in range(n_seq)
        ]
        return [value, side_swap(value), x_swap(value), lax.ppermute(value, ("dp", "seq"), corner)]

    normed_all = spread(normed_low)

    steps = 6
    chunk = hidden // steps
    slope_up, slope_gate, result, grad_second, grad_low, sums_two = pl.pallas_call(
        feed_forward,
        grid=(steps,),
        in_specs=[
            block((rows, width)), block((rows, width)),
            pl.BlockSpec((width, chunk), lambda j: (0, j)), pl.BlockSpec((width, chunk), lambda j: (0, j)),
            pl.BlockSpec((chunk, width), lambda j: (j, 0)),
            block((rows, width)), block((width,)), block((width,)),
        ],
        out_specs=[
            pl.BlockSpec((rows, chunk), lambda j: (0, j)), pl.BlockSpec((rows, chunk), lambda j: (0, j)),
            block((rows, width)), block((rows, width)), block((rows, width)), block((2, width)),
        ],
        out_shape=[
            shaped((rows, hidden), low), shaped((rows, hidden), low), shaped((rows, width), low),
            shaped((rows, width), full), shaped((rows, width), low), shaped((2, width), full),
        ],
        scratch_shapes=[pltpu.VMEM((rows, width), full)],
        compiler_params=pltpu.CompilerParams(
            vmem_limit_bytes=20 * MIB, dimension_semantics=("arbitrary",)
        ),
        cost_estimate=took("feed_forward"),
        name="feed_forward",
    )(
        normed, normed_low, gate_weight, up_weight, down_weight, cotangent, gain_two, bias_two,
    )
    grad_all = spread(grad_low)
    group = width // 2
    grad_first, branch_low, mine, other, sums = pl.pallas_call(
        feed_back,
        grid_spec=pltpu.PrefetchScalarGridSpec(
            num_scalar_prefetch=1,
            grid=(steps,),
            in_specs=[
                block((rows, width)), block((rows, width)),
                pl.BlockSpec((rows, chunk), lambda j, p: (0, j)),
                pl.BlockSpec((rows, chunk), lambda j, p: (0, j)),
                pl.BlockSpec((width, chunk), lambda j, p: (0, j)),
                pl.BlockSpec((width, chunk), lambda j, p: (0, j)),
                pl.BlockSpec((chunk, width), lambda j, p: (j, 0)), block((width, width)),
                block((rows, width)), block((rows, TILE)), block((width,)), block((2, width)),
            ],
            out_specs=[
                block((rows, width)), block((rows, width)), block((rows, group)), block((rows + 32, group)),
                block((8, width)),
            ],
            scratch_shapes=[pltpu.VMEM((rows, width), full)],
        ),
        out_shape=[
            shaped((rows, width), full), shaped((rows, width), low), shaped((rows, group), low),
            shaped((rows + 32, group), low), shaped((8, width), full),
        ],
        compiler_params=pltpu.CompilerParams(
            vmem_limit_bytes=20 * MIB, dimension_semantics=("arbitrary",)
        ),
        cost_estimate=took("feed_back"),
        name="feed_back",
    )(
        after(place, normed_all[1], normed_all[2]), grad_second, grad_low, slope_up, slope_gate, gate_weight, up_weight, down_weight,
        output_weight, scaled, inverse, gain_one, sums_two,
    )
    far_grad = side_swap(other)
    quarter = width // 4
    quarter = width // 4
    out_keep, out_send = call(
        out_grad, "out_grad", after(place, sums, normed_all[3]), [whole(branch_low), whole(attended_low)],
        [res((2 * quarter, width), full), res((2 * quarter, width), low)],
        [pltpu.VMEM((width, width), full)],
    )
    out_got = core_swap(out_send)

    at = lambda i: (still(input_weight), block((width, group), 0, lambda place: 2 * i + place[SIDE]))
    window_rows = [whole(tokens), whole(near), whole(far), whole(far_near)]
    keys, values, query = call(
        project_heads, "project_heads", after(place, out_keep),
        window_rows + [at(0), at(1), at(2), whole(cosine), whole(sine)],
        [res((window, group), low), res((window, group), low), res((two, group), low)],
        mib=28,
    )
    heads_of = window_rows + [
        whole(keys), whole(values), whole(query), whole(mine), whole(far_grad), whole(cosine),
        whole(sine), whole(seg_col), whole(seg_row),
    ]
    def back_one(tile, order):
        return call(
            functools.partial(back_some, (tile,), True), "back_one", order, heads_of,
            [res((two, TILE), low), res((window, 2 * TILE), low), res((3 * TILE, width), full)],
            [pltpu.VMEM((window, two), full), pltpu.VMEM((two, group), low)],
            mib=32,
        )

    back_first = back_one(0, after(place, keys, grad_all[1], grad_all[2]))
    back_second = back_one(1, after(place, back_first[0]))

    eighth = hidden // 8

    def columns(owner, order, last, *earlier):
        eight = lambda place: place[owner]
        split = [
            res((width // 2, 3 * eighth), full), res((width // 2, 2 * eighth), low),
            res((width // 2, eighth), low),
        ]
        return call(
            functools.partial(column_grads, last), "column_grads", order,
            [whole(v) for v in normed_all] + [whole(v) for v in grad_all]
            + [(still(gate_weight), block((width, eighth), 0, eight)),
               (still(up_weight), block((width, eighth), 0, eight)),
               (still(down_weight), block((eighth, width), eight, 0))]
            + [whole(v) for v in earlier],
            split if last else [res((width, 3 * eighth), low)],
            [pltpu.VMEM((2 * eighth, width), low), pltpu.VMEM((3 * eighth, width), full)]
            + ([pltpu.VMEM((width, eighth), full)] if last else []),
            mib=36,
        )

    out_keep, out_send = call(
        out_halve, "out_halve", after(place, back_second[0]), [whole(out_keep), whole(out_got)],
        [res((quarter, width), full), res((quarter, width), low)],
    )
    out_got = side_swap(out_send)
    (col_part,) = columns(OTHER, after(place, out_keep), False)
    col_got = core_swap(col_part)
    dq, even, in_keep, in_send, sums = call(
        functools.partial(back_some, (2,), False), "back_rest", after(place, col_part, out_got),
        heads_of + [whole(v) for v in back_first + back_second] + [whole(sums)],
        [res((two, group), low), res((two, width), low), res((3 * quarter, width), full),
         res((two + 3 * quarter + 16, width), low), res((8, width), full)],
        [pltpu.VMEM((window, two), full), pltpu.VMEM((two, group), low),
         pltpu.VMEM((window, width), low), pltpu.VMEM((3 * group, width), full)],
        mib=40,
    )
    in_got = core_swap(in_send)
    col_keep, *col_sends = columns(OWN, after(place, dq), True, col_got)
    col_gots = [swap(v, "dp", 2) for v in col_sends]

    share = width // n_data
    keep, send, sums = call(
        turn_over, "turn_over", after(place, col_keep),
        [whole(in_keep), whole(in_got), whole(out_keep), whole(out_got), whole(sums)],
        [res((4 * share, width), full), res((4 * share + 16, width), low), res((8, width), full)],
        [pltpu.VMEM((width, width), full)],
        mib=24,
    )
    got = x_swap(send)
    (far_send,) = call(
        far_pack, "far_pack", after(place, sums), [whole(dq), whole(even), whole(in_got)],
        [res((rows, 3 * group), low)],
    )
    far_part = side_swap(far_send)
    last = far_send
    parts = []
    for i, wide in ((0, 2 * eighth), (2, eighth)):
        half_keep, half_send = call(
            second_split, "second_split", after(place, last),
            [(col_keep, block((width // 2, wide), 0, i)), whole(col_gots[i // 2])],
            [res((width // 4, wide), full), res((width // 4, wide), low)],
        )
        last = half_send
        parts.append((half_keep, swap(half_send, "dp", 4)))
    keep, send, sums = call(
        functools.partial(halve, LOW), "halve", after(place, last),
        [whole(keep), whole(got), whole(sums)],
        [res((2 * share, width), full), res((2 * share + 16, width), low), res((8, width), full)],
    )
    got = swap(send, "dp", 2)
    pair_kept, pair_send = call(
        pair_sum, "pair_sum", after(place, sums), [whole(v) for v in parts[0]],
        [res((share, 2 * eighth), full), res((share, 2 * eighth), low)],
    )
    pair_got = x_swap(pair_send)
    order = []
    for d in range(n_data):
        for s in range(n_seq):
            order.append((d * n_seq + s, (2 * s + d % 2) * n_seq + d // 2))
    (down,) = call(
        down_sum, "down_sum", after(place, pair_send), [whole(v) for v in parts[1]],
        [res((width // 4, eighth), low)],
    )
    down_got = lax.ppermute(down, ("dp", "seq"), order)
    keep, send, sums = call(
        functools.partial(halve, HIGH), "halve", after(place, down),
        [whole(keep), whole(got), whole(sums)],
        [res((share, width), full), res((share + 16, width), low), res((8, width), full)],
    )
    got = swap(send, "dp", 4)
    weight_at = lambda i, own: (
        still(input_weight),
        block((width, group), 0, lambda place: 2 * i + (place[SIDE] if own else 1 - place[SIDE])),
    )
    (grad_tokens,) = call(
        token_grad, "token_grad", after(place, sums),
        [whole(grad_first), whole(dq), whole(even), whole(in_got), whole(far_part)]
        + [weight_at(i, True) for i in range(3)] + [weight_at(i, False) for i in range(3)],
        [res((rows, width), low)],
        mib=24,
    )
    grad_gate, grad_up = call(
        pair_place, "pair_place", after(place, grad_tokens), [whole(pair_kept), whole(pair_got)],
        [res((share, 2 * eighth), full), res((share, 2 * eighth), full)],
    )
    in_own, in_send, grad_out, *vectors = call(
        last_sum, "last_sum", after(place, grad_gate), [whole(keep), whole(got), whole(sums)],
        [res((share, 2 * quarter), full), res((share, quarter), low), res((share, quarter), full)]
        + [res((width,), full)] * 4,
    )
    in_moved = side_swap(in_send)
    (grad_down,) = call(
        turned_back, "turned_back", after(place, in_send), [whole(down_got)],
        [res((eighth, quarter), full)],
    )
    (grad_in,) = call(
        in_place, "in_place", after(place, grad_down), [whole(in_own), whole(in_moved)],
        [res((share, 3 * quarter), full)],
    )
    return (
        result,
        grad_tokens,
        grad_in,
        grad_out,
        grad_gate,
        grad_up,
        grad_down,
        *vectors,
    )


def solution(mesh):
    placed = (
        P(("dp", "seq"), None),
        P(("dp", "seq"), None),
        P("dp", None),
        P(),
        P(),
        P(),
        P(),
        P(),
        P(),
        P(),
        P(),
        P(),
    )
    paired = mesh.shape["seq"] == 4 and mesh.shape["dp"] == 8
    return jax.shard_map(
        fast if paired else general,
        mesh=mesh,
        in_specs=placed,
        out_specs=(
            P(("dp", "seq"), None),
            P(("dp", "seq"), None),
            P("dp", "seq"),
            P("dp", "seq"),
            P("dp", "seq"),
            P("dp", "seq"),
            P("dp", "seq"),
            P(),
            P(),
            P(),
            P(),
        ),
        check_vma=False,
    )
```

```python
import functools
import math

import jax
import jax.numpy as jnp
import numpy as np
from jax import lax
from jax.experimental import pallas as pl
from jax.experimental.pallas import tpu as pltpu
from jax.sharding import PartitionSpec as P

HEAD = 64


norm_eps = 1e-05
rotary_base = 1000.0
masked_value = -1e30


def doc_layout(lengths_row, count):
    ends = jnp.cumsum(lengths_row)
    place = jnp.arange(count, dtype=jnp.int32)
    after = (place[:, None] >= ends[None, :]).astype(jnp.int32)
    segment = jnp.sum(after, axis=1)
    start = jnp.sum(after * lengths_row[None, :], axis=1)
    return (segment, place - start)


def rotate(field, position):
    half = field.shape[-1] // 2
    freq = rotary_base ** (-jnp.arange(half, dtype=jnp.float32) * (2.0 / field.shape[-1]))
    angle = position.astype(jnp.float32)[:, None] * freq[None, :]
    cosine = jnp.cos(angle)[:, None, :]
    sine = jnp.sin(angle)[:, None, :]
    first = field[..., :half]
    second = field[..., half:]
    return jnp.concatenate(
        [first * cosine - second * sine, second * cosine + first * sine], axis=-1
    )


def norm_forward(value, gain, shift):
    mean = jnp.mean(value, axis=-1, keepdims=True)
    centred = value - mean
    inverse = lax.rsqrt(jnp.mean(centred * centred, axis=-1, keepdims=True) + norm_eps)
    scaled = centred * inverse
    return (scaled * gain + shift, scaled, inverse)


def norm_backward(grad, scaled, inverse, gain):
    inner = grad * gain
    back = inverse * (
        inner
        - jnp.mean(inner, axis=-1, keepdims=True)
        - scaled * jnp.mean(inner * scaled, axis=-1, keepdims=True)
    )
    return (back, jnp.sum(grad * scaled, axis=0), jnp.sum(grad, axis=0))


def inner_rows(left, right):
    return lax.dot_general(
        left, right, (((0,), (0,)), ((), ())), preferred_element_type=jnp.float32
    )


def times_transpose(left, right):
    return lax.dot_general(
        left, right, (((1,), (1,)), ((), ())), preferred_element_type=jnp.float32
    )


def general(
    tokens,
    cotangent,
    lengths,
    input_weight,
    output_weight,
    gate_weight,
    up_weight,
    down_weight,
    gain_one,
    bias_one,
    gain_two,
    bias_two,
):
    rows, width = tokens.shape
    heads = width // HEAD
    window = rows * lax.axis_size("seq")
    scale = 1.0 / math.sqrt(HEAD)
    segment_all, position_all = doc_layout(lengths[0], window)
    offset = lax.axis_index("seq") * rows
    seg_mine = lax.dynamic_slice_in_dim(segment_all, offset, rows)
    pos_mine = lax.dynamic_slice_in_dim(position_all, offset, rows)
    projected = jnp.dot(tokens, input_weight, preferred_element_type=jnp.float32)
    query = rotate(projected[:, :width].reshape(rows, heads, HEAD), pos_mine).astype(jnp.bfloat16)
    key = (
        rotate(projected[:, width : 2 * width].reshape(rows, heads, HEAD), pos_mine)
        .astype(jnp.bfloat16)
        .reshape(rows, width)
    )
    value = projected[:, 2 * width :].astype(jnp.bfloat16)

    def scores_for(key_block, seg_block):
        scores = (
            jnp.einsum("qhe,khe->hqk", query, key_block, preferred_element_type=jnp.float32) * scale
        )
        same = (seg_mine[:, None] == seg_block[None, :])[None]
        return (jnp.where(same, scores, masked_value), same)

    def split_blocks(piece, segs):
        count = piece[0].shape[0]
        size = math.gcd(count, 512)
        keys = piece[0].reshape(count // size, size, heads, HEAD)
        values = piece[1].reshape(count // size, size, heads, HEAD)
        return (keys, values, segs.reshape(count // size, size), count, size)

    start_state = (
        jnp.zeros((rows, heads, HEAD), jnp.float32),
        jnp.full((heads, rows), masked_value, jnp.float32),
        jnp.zeros((heads, rows), jnp.float32),
    )
    segs = segment_all
    keys, values, seg_blocks, count, size = split_blocks(
        (
            lax.all_gather(key, "seq", axis=0, tiled=True),
            lax.all_gather(value, "seq", axis=0, tiled=True),
        ),
        segs,
    )

    def forward_step(state, item):
        summed, peak, total = state
        key_block, value_block, seg_block = item
        scores, same = scores_for(key_block, seg_block)
        new_peak = jnp.maximum(peak, jnp.max(scores, axis=-1))
        fade = jnp.exp(peak - new_peak)
        weight = jnp.where(same, jnp.exp(scores - new_peak[..., None]), 0.0)
        total = total * fade + jnp.sum(weight, axis=-1)
        summed = summed * fade.T[..., None] + jnp.einsum(
            "hqk,khe->qhe",
            weight.astype(jnp.bfloat16),
            value_block,
            preferred_element_type=jnp.float32,
        )
        return ((summed, new_peak, total), None)

    state, unused = lax.scan(forward_step, start_state, (keys, values, seg_blocks))
    summed, peak, total = state
    attended = (summed / total.T[..., None]).reshape(rows, width)
    attended_low = attended.astype(jnp.bfloat16)
    first = tokens.astype(jnp.float32) + jnp.dot(
        attended_low, output_weight, preferred_element_type=jnp.float32
    )
    normed, scaled_one, inverse_one = norm_forward(first, gain_one, bias_one)
    normed_low = normed.astype(jnp.bfloat16)
    gate = jnp.dot(normed_low, gate_weight, preferred_element_type=jnp.float32)
    upward = jnp.dot(normed_low, up_weight, preferred_element_type=jnp.float32)
    sigma = jax.nn.sigmoid(gate)
    activated = gate * sigma
    hidden_low = (activated * upward).astype(jnp.bfloat16)
    second = normed + jnp.dot(hidden_low, down_weight, preferred_element_type=jnp.float32)
    result, scaled_two, inverse_two = norm_forward(second, gain_two, bias_two)
    grad_second, grad_gain_two, grad_bias_two = norm_backward(
        cotangent.astype(jnp.float32), scaled_two, inverse_two, gain_two
    )
    grad_ff_low = grad_second.astype(jnp.bfloat16)
    grad_hidden = times_transpose(grad_ff_low, down_weight)
    grad_gate_low = (grad_hidden * upward * (sigma * (1.0 + gate * (1.0 - sigma)))).astype(
        jnp.bfloat16
    )
    grad_up_low = (grad_hidden * activated).astype(jnp.bfloat16)
    grad_normed = (
        grad_second
        + times_transpose(grad_gate_low, gate_weight)
        + times_transpose(grad_up_low, up_weight)
    )
    grad_first, grad_gain_one, grad_bias_one = norm_backward(
        grad_normed, scaled_one, inverse_one, gain_one
    )
    grad_branch_low = grad_first.astype(jnp.bfloat16)
    grad_attended_low = times_transpose(grad_branch_low, output_weight).astype(jnp.bfloat16)
    grad_heads = grad_attended_low.reshape(rows, heads, HEAD)
    delta = jnp.sum(
        (grad_attended_low.astype(jnp.float32) * attended).reshape(rows, heads, HEAD), axis=-1
    ).T
    zero_query = jnp.zeros((rows, heads, HEAD), jnp.float32)
    grad_acc = zero_query
    segs = segment_all
    grad_query = grad_acc
    keys, values, seg_blocks, count, size = split_blocks(
        (
            lax.all_gather(key, "seq", axis=0, tiled=True),
            lax.all_gather(value, "seq", axis=0, tiled=True),
        ),
        segs,
    )

    def backward_step(grad_acc, item):
        key_block, value_block, seg_block = item
        scores, same = scores_for(key_block, seg_block)
        prob = jnp.where(same, jnp.exp(scores - peak[..., None]) / total[..., None], 0.0)
        prob_grad = jnp.einsum(
            "qhe,khe->hqk", grad_heads, value_block, preferred_element_type=jnp.float32
        )
        score_grad = (prob * (prob_grad - delta[..., None])).astype(jnp.bfloat16)
        grad_acc = (
            grad_acc
            + jnp.einsum("hqk,khe->qhe", score_grad, key_block, preferred_element_type=jnp.float32)
            * scale
        )
        prob_low = prob.astype(jnp.bfloat16)
        key_grad = (
            jnp.einsum("hqk,qhe->khe", score_grad, query, preferred_element_type=jnp.float32)
            * scale
        )
        value_grad = jnp.einsum(
            "hqk,qhe->khe", prob_low, grad_heads, preferred_element_type=jnp.float32
        )
        return (grad_acc, (key_grad.reshape(size, width), value_grad.reshape(size, width)))

    grad_query, outputs = lax.scan(backward_step, grad_query, (keys, values, seg_blocks))
    grad_acc = grad_query
    key_part = outputs[0].reshape(count, width)
    value_part = outputs[1].reshape(count, width)
    grad_key, grad_value = (
        lax.psum_scatter(
            key_part.astype(jnp.bfloat16), "seq", scatter_dimension=0, tiled=True
        ).astype(jnp.float32),
        lax.psum_scatter(
            value_part.astype(jnp.bfloat16), "seq", scatter_dimension=0, tiled=True
        ).astype(jnp.float32),
    )
    query_back = rotate(grad_acc, -pos_mine).reshape(rows, width)
    key_back = rotate(grad_key.reshape(rows, heads, HEAD), -pos_mine).reshape(rows, width)
    grad_projected_low = jnp.concatenate([query_back, key_back, grad_value], axis=1).astype(
        jnp.bfloat16
    )
    grad_tokens = (grad_first + times_transpose(grad_projected_low, input_weight)).astype(
        jnp.bfloat16
    )
    column_grads = (
        lax.all_to_all(grad_projected_low, "seq", split_axis=1, concat_axis=0, tiled=True),
        lax.all_to_all(grad_branch_low, "seq", split_axis=1, concat_axis=0, tiled=True),
        lax.all_to_all(grad_gate_low, "seq", split_axis=1, concat_axis=0, tiled=True),
        lax.all_to_all(grad_up_low, "seq", split_axis=1, concat_axis=0, tiled=True),
        lax.all_to_all(grad_ff_low, "seq", split_axis=1, concat_axis=0, tiled=True),
    )
    tok_rows = lax.all_gather(tokens, "seq", axis=0, tiled=True)
    normed_rows = lax.all_gather(normed_low, "seq", axis=0, tiled=True)
    attended_rows = lax.all_gather(attended_low, "seq", axis=0, tiled=True)
    hidden_rows = lax.all_gather(hidden_low, "seq", axis=0, tiled=True)
    count = tok_rows.shape[0]
    cols = [member for member in column_grads]
    summed_grads = (
        lax.psum_scatter(
            inner_rows(tok_rows, cols[0]).astype(jnp.bfloat16),
            "dp",
            scatter_dimension=0,
            tiled=True,
        ).astype(jnp.float32),
        lax.psum_scatter(
            inner_rows(attended_rows, cols[1]).astype(jnp.bfloat16),
            "dp",
            scatter_dimension=0,
            tiled=True,
        ).astype(jnp.float32),
        lax.psum_scatter(
            inner_rows(normed_rows, cols[2]).astype(jnp.bfloat16),
            "dp",
            scatter_dimension=0,
            tiled=True,
        ).astype(jnp.float32),
        lax.psum_scatter(
            inner_rows(normed_rows, cols[3]).astype(jnp.bfloat16),
            "dp",
            scatter_dimension=0,
            tiled=True,
        ).astype(jnp.float32),
        lax.psum_scatter(
            inner_rows(hidden_rows, cols[4]).astype(jnp.bfloat16),
            "dp",
            scatter_dimension=0,
            tiled=True,
        ).astype(jnp.float32),
    )
    norm_grads = lax.psum(
        (grad_gain_one, grad_bias_one, grad_gain_two, grad_bias_two), ("dp", "seq")
    )
    return (
        result.astype(jnp.bfloat16),
        grad_tokens,
        summed_grads[0],
        summed_grads[1],
        summed_grads[2],
        summed_grads[3],
        summed_grads[4],
        norm_grads[0],
        norm_grads[1],
        norm_grads[2],
        norm_grads[3],
    )


low = jnp.bfloat16
full = jnp.float32
TILE = 128
MIB = 1024 * 1024


def nn(left, right):
    return lax.dot_general(
        left, right, (((1,), (0,)), ((), ())), preferred_element_type=jnp.float32
    )


def nt(left, right):
    return lax.dot_general(
        left, right, (((1,), (1,)), ((), ())), preferred_element_type=jnp.float32
    )


def tn(left, right):
    return lax.dot_general(
        left, right, (((0,), (0,)), ((), ())), preferred_element_type=jnp.float32
    )


def block(shape, *at):
    at = at or (0,) * len(shape)

    def index(*args):
        return tuple(a(*args[1:]) if callable(a) else a for a in at)

    return pl.BlockSpec(tuple(shape), index)


def shaped(shape, kind):
    return jax.ShapeDtypeStruct(tuple(shape), kind)


SEQ, SIDE, X, LOW, HIGH, PAIR, LONE, OTHER_PAIR, OTHER_LONE, OWN, OTHER, CORE = range(12)

COST = {
    "tables": 1.5, "first_half": 6.9, "second_half": 7.9, "feed_forward": 8.4, "feed_back": 8.6,
    "project_heads": 4, "back_one": 6.5, "back_rest": 7, "column_grads": 7.5, "token_grad": 3,
    "out_grad": 1.2,
}


def took(name):
    return pl.CostEstimate(flops=int(COST.get(name, 0.5) * 10**9), bytes_accessed=1, transcendentals=0)


def still(value):
    return pltpu.with_memory_space_constraint(value, pltpu.HBM)


def call(body, name, scalars, operands, results, scratch=(), mib=16):
    return pl.pallas_call(
        body,
        grid_spec=pltpu.PrefetchScalarGridSpec(
            num_scalar_prefetch=1,
            grid=(1,),
            in_specs=[spec for unused, spec in operands],
            out_specs=[spec for unused, spec in results],
            scratch_shapes=list(scratch),
        ),
        out_shape=[shape for shape, unused in results],
        compiler_params=pltpu.CompilerParams(
            vmem_limit_bytes=mib * MIB, dimension_semantics=("arbitrary",)
        ),
        cost_estimate=took(name),
        name=name,
    )(scalars, *[value for value, unused in operands])


def whole(value):
    return (value, block(value.shape))


def turn(field, cosine, sine):
    lane = lax.broadcasted_iota(jnp.int32, field.shape, 1)
    half = HEAD // 2
    other = jnp.where(
        lane % HEAD < half, pltpu.roll(field, TILE - half, 1), pltpu.roll(field, half, 1)
    )
    return field * cosine + other * sine


def one_head(pair, which):
    lane = lax.broadcasted_iota(jnp.int32, pair.shape, 1)
    return jnp.where((lane // HEAD) == which, pair, jnp.zeros_like(pair))


def pack(sums):
    high = sums.astype(low)
    return jnp.concatenate([high, (sums - high.astype(jnp.float32)).astype(low)], axis=0)


def unpack(packed):
    wide = packed.astype(jnp.float32)
    return wide[:8] + wide[8:]


def tables(place, lengths, freq, cosine, sine, seg_col, seg_row):
    count = cosine.shape[0]
    rows = count // 4
    lane = lax.broadcasted_iota(jnp.int32, (8, count), 1)
    index = jnp.zeros_like(lane)
    for i in range(1, 4):
        index = index + (lane >= i * rows).astype(jnp.int32)
    spot = (index ^ place[SEQ]) * rows + (lane - index * rows)
    end = jnp.int32(0)
    segment = jnp.zeros_like(lane)
    start = jnp.zeros_like(lane)
    for i in range(lengths.shape[1]):
        length = lengths[0, i]
        end = end + length
        past = (spot >= end).astype(jnp.int32)
        segment = segment + past
        start = start + past * length
    position = (spot - start).astype(jnp.float32)
    angle = freq[:, :1] * position[:1]
    c, s = jnp.cos(angle), jnp.sin(angle)
    cosine[...] = jnp.concatenate([c] * 4, axis=0).T
    sine[...] = jnp.concatenate([-s, s] * 2, axis=0).T
    seg_row[...] = segment
    wide = jnp.broadcast_to(segment[:1].astype(jnp.float32), (TILE, count))
    seg_col[...] = wide.T.astype(jnp.int32)


def put_keys(tokens, wk, wv, cosine, sine, keys, values, start):
    rows = tokens.shape[0]
    projected = nn(tokens, wk)
    for tile in range(projected.shape[1] // TILE):
        cols = slice(tile * TILE, (tile + 1) * TILE)
        keys[start : start + rows, cols] = turn(projected[:, cols], cosine, sine).astype(low)
    values[start : start + rows, :] = nn(tokens, wv).astype(low)


def put_query(tokens, wq, cosine, sine, query):
    scale = 1.0 / math.sqrt(HEAD)
    projected = nn(tokens, wq)
    for tile in range(projected.shape[1] // TILE):
        cols = slice(tile * TILE, (tile + 1) * TILE)
        turned = turn(projected[:, cols], cosine, sine)
        query[:, cols] = (turned.astype(low) * scale).astype(low)


def attend(query, keys, values, bias):
    for tile in range(query.shape[1] // TILE):
        cols = slice(tile * TILE, (tile + 1) * TILE)
        key_pair = keys[:, cols]
        value_pair = values[:, cols]
        for which in range(TILE // HEAD):
            scores = nt(key_pair, one_head(query[:, cols], which)) + bias[...]
            peak = jnp.max(scores, axis=0, keepdims=True)
            weight = jnp.exp(scores - peak)
            total = jnp.sum(weight, axis=0, keepdims=True)
            out = tn(value_pair, weight.astype(low))[which * HEAD : (which + 1) * HEAD]
            yield tile * (TILE // HEAD) + which, out, peak, total


def first_half(
    place, own, near, wq, wk, wv, cosine, sine, seg_key, seg_query, query, acc, peaks, totals,
    keys, values, bias,
):
    rows = own.shape[0]
    put_query(own[...], wq[...], cosine[:rows, :], sine[:rows, :], query)
    put_keys(own[...], wk[...], wv[...], cosine[:rows, :], sine[:rows, :], keys, values, 0)
    put_keys(near[...], wk[...], wv[...], cosine[rows:, :], sine[rows:, :], keys, values, rows)
    bias[...] = jnp.where(seg_key[:, :1] == seg_query[:1, :], 0.0, masked_value)
    for head, out, peak, total in attend(query, keys, values, bias):
        acc[head * HEAD : (head + 1) * HEAD, :] = out
        peaks[head : head + 1, :] = peak
        totals[head : head + 1, :] = total


def second_half(
    place, own, far, far_near, wk, wv, wo, cosine, sine, seg_key, seg_query, query, acc, peaks, totals,
    gain, shift, far_wq, attended_low, normed, normed_low, scaled, inverse, keys, values, far_query, bias,
    turned,
):
    rows, width = own.shape
    put_keys(far[...], wk[...], wv[...], cosine[:rows, :], sine[:rows, :], keys, values, 0)
    put_keys(far_near[...], wk[...], wv[...], cosine[rows:, :], sine[rows:, :], keys, values, rows)
    bias[...] = jnp.where(seg_key[:, :1] == seg_query[:1, :], 0.0, masked_value)
    put_query(far[...], far_wq[...], cosine[:rows, :], sine[:rows, :], far_query)
    for head, out, peak, total in attend(query, keys, values, bias):
        part = slice(head * HEAD, (head + 1) * HEAD)
        before = peaks[head : head + 1, :]
        best = jnp.maximum(before, peak)
        fade = jnp.exp(before - best)
        grow = jnp.exp(peak - best)
        inverse_total = 1.0 / (totals[head : head + 1, :] * fade + total * grow)
        turned[part, :] = acc[part, :] * (fade * inverse_total) + out * (grow * inverse_total)
    attended = turned[...].T.astype(low)
    attended_low[...] = attended
    first = own[...].astype(jnp.float32) + nn(attended, wo[...])
    mean = jnp.mean(first, axis=1, keepdims=True)
    centred = first - mean
    spread = lax.rsqrt(jnp.mean(centred * centred, axis=1, keepdims=True) + norm_eps)
    unit = centred * spread
    value = unit * gain[...][None, :] + shift[...][None, :]
    scaled[...] = unit
    inverse[...] = jnp.broadcast_to(spread, (rows, TILE))
    normed[...] = value
    normed_low[...] = value.astype(low)


def halves(place, by_side, by_x, first, second):
    half = first.shape[0]
    first[...] = by_side[:half, :]
    second[...] = by_x[half:, :]


def feed_forward(
    normed, normed_low, wg, wu, wd, cotangent, gain, shift,
    slope_up, slope_gate, result, grad_second, grad_low, sums, acc,
):
    step = pl.program_id(0)
    gate = nn(normed_low[...], wg[...])
    upward = nn(normed_low[...], wu[...])
    sigma = jax.nn.sigmoid(gate)
    active = gate * sigma
    slope_up[...] = active.astype(low)
    slope_gate[...] = (upward * (sigma * (1.0 + gate * (1.0 - sigma)))).astype(low)
    product = nn((active * upward).astype(low), wd[...])

    @pl.when(step == 0)
    def _():
        acc[...] = normed[...] + product

    @pl.when(step > 0)
    def _():
        acc[...] += product

    @pl.when(step == pl.num_programs(0) - 1)
    def _():
        second = acc[...]
        mean = jnp.mean(second, axis=1, keepdims=True)
        centred = second - mean
        spread = lax.rsqrt(jnp.mean(centred * centred, axis=1, keepdims=True) + norm_eps)
        unit = centred * spread
        result[...] = (unit * gain[...][None, :] + shift[...][None, :]).astype(low)
        grad = cotangent[...].astype(jnp.float32)
        inner = grad * gain[...][None, :]
        back = spread * (
            inner
            - jnp.mean(inner, axis=1, keepdims=True)
            - unit * jnp.mean(inner * unit, axis=1, keepdims=True)
        )
        grad_second[...] = back
        grad_low[...] = back.astype(low)
        sums[0:1, :] = jnp.sum(grad * unit, axis=0, keepdims=True)
        sums[1:2, :] = jnp.sum(grad, axis=0, keepdims=True)


def feed_back(
    place, grad_second, grad_low, slope_up, slope_gate, wg, wu, wd, wo, scaled, inverse, gain, sums_two,
    grad_first, branch_low, mine, other, sums, acc,
):
    step = pl.program_id(0)
    hidden = nt(grad_low[...], wd[...])
    gate = (hidden * slope_gate[...].astype(jnp.float32)).astype(low)
    upward = (hidden * slope_up[...].astype(jnp.float32)).astype(low)
    product = nt(gate, wg[...]) + nt(upward, wu[...])

    @pl.when(step == 0)
    def _():
        acc[...] = grad_second[...] + product

    @pl.when(step > 0)
    def _():
        acc[...] += product

    @pl.when(step == pl.num_programs(0) - 1)
    def _():
        grad = acc[...]
        unit = scaled[...]
        inner = grad * gain[...][None, :]
        back = inverse[:, :1] * (
            inner
            - jnp.mean(inner, axis=1, keepdims=True)
            - unit * jnp.mean(inner * unit, axis=1, keepdims=True)
        )
        grad_first[...] = back
        branch_low[...] = back.astype(low)
        attended_grad = nt(branch_low[...], wo[...]).astype(low)
        group = mine.shape[1]
        height = mine.shape[0]
        left, right = attended_grad[:, :group], attended_grad[:, group:]
        second_side = place[SIDE] > 0
        mine[...] = jnp.where(second_side, right, left)
        other[:height, :] = jnp.where(second_side, left, right)
        sums[...] = jnp.zeros_like(sums)
        sums[0:1, :] = jnp.sum(grad * unit, axis=0, keepdims=True)
        sums[1:2, :] = jnp.sum(grad, axis=0, keepdims=True)
        sums[2:4, :] = sums_two[...]
        for i in range(2):
            part = slice(height + i * 16, height + (i + 1) * 16)
            other[part, :] = pack(sums[:, i * group : (i + 1) * group])


def rows_at(index, count):
    return pl.ds(pl.multiple_of(index * count, count), count)


def out_grad(place, branch_low, attended_low, keep, send, turned):
    turned[...] = tn(branch_low[...], attended_low[...])
    quarter = turned.shape[0] // 4
    core = place[CORE]
    for i in range(2):
        to = slice(i * quarter, (i + 1) * quarter)
        keep[to, :] = turned[rows_at(2 * i + core, quarter), :]
        send[to, :] = turned[rows_at(2 * i + 1 - core, quarter), :].astype(low)


def out_halve(place, keep, got, kept, send):
    quarter = keep.shape[0] // 2
    mine, other = rows_at(place[SIDE], quarter), rows_at(1 - place[SIDE], quarter)
    kept[...] = keep[mine, :] + got[mine, :].astype(jnp.float32)
    send[...] = (keep[other, :] + got[other, :].astype(jnp.float32)).astype(low)


def back_tile(key_pair, value_pair, query_pair, grad_pair, bias):
    scale = 1.0 / math.sqrt(HEAD)
    grad_key = None
    grad_value = None
    pieces = []
    for which in range(TILE // HEAD):
        query_head = one_head(query_pair, which)
        grad_head = one_head(grad_pair, which)
        scores = nt(key_pair, query_head) + bias[...]
        weight = jnp.exp(scores - jnp.max(scores, axis=0, keepdims=True))
        prob = weight * (1.0 / jnp.sum(weight, axis=0, keepdims=True))
        prob_grad = nt(value_pair, grad_head)
        product = prob * prob_grad
        delta = jnp.sum(product, axis=0, keepdims=True)
        score_grad = (product - prob * delta).astype(low)
        value_part = nn(prob.astype(low), grad_head)
        key_part = nn(score_grad, query_head)
        grad_key = key_part if grad_key is None else grad_key + key_part
        grad_value = value_part if grad_value is None else grad_value + value_part
        pieces.append(tn(key_pair, score_grad)[which * HEAD : (which + 1) * HEAD])
    return jnp.concatenate(pieces, axis=0).T * scale, grad_key, grad_value


def back_some(tiles, first, place, *refs):
    own, near, far, far_near = refs[:4]
    pairs = [refs[i : i + 2] for i in range(4, 12, 2)]
    cosine, sine, seg_key, seg_query = refs[12:16]
    far_grad = refs[11]
    rows = own.shape[0]
    blocks = (own, near, far, far_near)
    if first:
        dq, both, grads, bias = refs[16:]
    else:
        before = refs[16:22]
        dq, even, odd_near, odd_far, grads, bias, both = refs[22:]
    group = pairs[0][0].shape[1]
    for index in range(2):
        part = slice(2 * index * rows, (2 * index + 1) * rows)
        to = slice(index * rows, (index + 1) * rows)
        bias[:, to] = jnp.where(seg_key[:, :1] == seg_query[:1, part], 0.0, masked_value)
    for tile in tiles:
        cols = slice(tile * TILE, (tile + 1) * TILE)
        keys, values, queries, outs = (
            jnp.concatenate([one[:, cols], two[: one.shape[0], cols]], axis=0) for one, two in pairs
        )
        grad_query, grad_key, grad_value = back_tile(keys, values, queries, outs, bias)
        to = slice(0, TILE) if first else cols
        shifted = slice(TILE, 2 * TILE) if first else slice(group + tile * TILE, group + (tile + 1) * TILE)
        for index in range(2):
            part = slice(index * rows, (index + 1) * rows)
            at = slice(2 * index * rows, (2 * index + 1) * rows)
            dq[part, to] = turn(grad_query[part], cosine[at, :], -sine[at, :]).astype(low)
        both[:, to] = turn(grad_key, cosine[...], -sine[...]).astype(low)
        both[:, shifted] = grad_value.astype(low)
        pair = jnp.concatenate([both[:, to], both[:, shifted]], axis=1)
        total = None
        for index in range(4):
            part = slice(index * rows, (index + 1) * rows)
            product = tn(pair[part], blocks[index][...])
            total = product if total is None else total + product
        query_rows = tn(dq[:rows, to], own[...]) + tn(dq[rows:, to], far[...])
        if first:
            grads[:TILE, :] = query_rows
            grads[TILE:, :] = total
        else:
            grads[tile * TILE : (tile + 1) * TILE, :] = query_rows
            for kind in range(2):
                at = (kind + 1) * group + tile * TILE
                grads[at : at + TILE, :] = total[kind * TILE : (kind + 1) * TILE]
    if first:
        return
    for tile in range(2):
        dq_before, both_before, grads_before = before[3 * tile : 3 * tile + 3]
        dq[:, tile * TILE : (tile + 1) * TILE] = dq_before[...]
        for kind in range(3):
            at = kind * group + tile * TILE
            if kind < 2:
                both[:, at : at + TILE] = both_before[:, kind * TILE : (kind + 1) * TILE]
            grads[at : at + TILE, :] = grads_before[kind * TILE : (kind + 1) * TILE, :]
    for index in range(4):
        part = slice(index * rows, (index + 1) * rows)
        if index % 2:
            (odd_far if index > 1 else odd_near)[...] = both[part, :]
        else:
            even[index // 2 * rows : (index // 2 + 1) * rows, :] = both[part, :]


def fold(place, grads, far_grad, sums, odd_near, odd_far, keep, send, near_send, far_send, kept_sums):
    quarter = keep.shape[0] // 3
    pair, lone, other_pair, other_lone = (place[i] for i in (PAIR, LONE, OTHER_PAIR, OTHER_LONE))
    for i in range(3):
        to = slice(i * quarter, (i + 1) * quarter)
        keep[to, :] = grads[rows_at(pair + i if i < 2 else lone, quarter), :]
        send[to, :] = grads[rows_at(other_pair + i if i < 2 else other_lone, quarter), :].astype(low)
    got = jnp.concatenate([unpack(far_grad[-32:-16, :]), unpack(far_grad[-16:, :])], axis=1)
    total = sums[...] + got
    kept_sums[...] = total
    send[3 * quarter :, :] = pack(total)
    near_send[...] = odd_near[...]
    far_send[...] = odd_far[...]


def turn_over(place, keep, got, out_keep, out_got, sums, kept, send, kept_sums, turned):
    height = keep.shape[0]
    turned[:, :height] = (keep[...] + got[:height, :].astype(jnp.float32)).T
    turned[:, height:] = (out_keep[...] + out_got[...].astype(jnp.float32)).T
    bit = place[X]
    part = turned.shape[0] // 8
    for i in range(4):
        to = slice(i * part, (i + 1) * part)
        kept[to, :] = turned[rows_at(2 * i + bit, part), :]
        send[to, :] = turned[rows_at(2 * i + 1 - bit, part), :].astype(low)
    both = sums[...] + unpack(got[height:, :])
    kept_sums[...] = both
    send[4 * part :, :] = pack(both)


def halve_low(place, keep, got, sums, kept, send, kept_sums):
    bit = place[LOW]
    part = keep.shape[0] // 4
    for i in range(2):
        to = slice(i * part, (i + 1) * part)
        for at, out in ((bit, kept), (1 - bit, send)):
            there = rows_at(2 * i + at, part)
            out[to, :] = (keep[there, :] + got[there, :].astype(jnp.float32)).astype(out.dtype)
    both = sums[...] + unpack(got[4 * part :, :])
    kept_sums[...] = both
    send[2 * part :, :] = pack(both)


def halve(place, keep, got, sums, kept, send, kept_sums):
    bit = place[HIGH]
    height = keep.shape[0]
    part = height // 2
    mine, other = rows_at(bit, part), rows_at(1 - bit, part)
    kept[...] = keep[mine, :] + got[mine, :].astype(jnp.float32)
    send[:part, :] = (keep[other, :] + got[other, :].astype(jnp.float32)).astype(low)
    both = sums[...] + unpack(got[height:, :])
    kept_sums[...] = both
    send[part:, :] = pack(both)


def last_sum(place, keep, got, sums, own, send, out, *vectors):
    height = keep.shape[0]
    total = keep[...] + got[:height, :].astype(jnp.float32)
    quarter = out.shape[1]
    own[...] = total[:, : 2 * quarter]
    send[...] = total[:, 2 * quarter : 3 * quarter].astype(low)
    out[...] = total[:, 3 * quarter :]
    both = sums[...] + unpack(got[height:, :])
    for i, vector in enumerate(vectors):
        vector[...] = both[i]


def column_grads(last, place, *refs):
    count = 5
    rows_refs, back_refs = refs[:count], refs[count : 2 * count]
    wg, wu, wd = refs[2 * count : 2 * count + 3]
    rest = refs[2 * count + 3 :]
    if last:
        earlier = (rest[0], rest[-1])
        outs, wgu, acc = rest[1:5], rest[5], rest[6]
    else:
        outs, wgu, acc = rest[:1], rest[1], rest[2]
    half, width = wd.shape
    wgu[:half, :] = wg[...].astype(jnp.float32).T.astype(low)
    wgu[half:, :] = wu[...].astype(jnp.float32).T.astype(low)
    for step in range(count - 1):
        rows, back = (
            v[step][...] if step < count - 2 else jnp.concatenate([v[step][...], v[step + 1][...]], axis=0)
            for v in (rows_refs, back_refs)
        )
        both = nt(wgu[...], rows)
        gate, upward = both[:half], both[half:]
        sigma = jax.nn.sigmoid(gate)
        active = gate * sigma
        hidden = (active * upward).astype(low)
        grad_hidden = nt(wd[...], back)
        grad_gate = (grad_hidden * upward * (sigma * (1.0 + gate * (1.0 - sigma)))).astype(low)
        grad_up = (grad_hidden * active).astype(low)
        products = (nn(grad_gate, rows), nn(grad_up, rows), nn(hidden, back))
        for i, product in enumerate(products):
            part = slice(i * half, (i + 1) * half)
            if step == 0:
                acc[part, :] = product
            else:
                acc[part, :] += product
    if last:
        got, total = earlier
        cut = width // 4
        for i in range(3):
            part = slice(i * half, (i + 1) * half)
            total[...] = acc[part, :].T + got[:, part].astype(jnp.float32)
            keep, send, to_cols = (outs[0], outs[2], part) if i < 2 else (outs[1], outs[3], slice(None))
            for j in range(2):
                to = slice(j * cut, (j + 1) * cut)
                keep[to, to_cols] = total[rows_at(2 * j + place[LOW], cut), :]
                send[to, to_cols] = total[rows_at(2 * j + 1 - place[LOW], cut), :].astype(low)
    else:
        for i in range(3):
            part = slice(i * half, (i + 1) * half)
            outs[0][:, part] = acc[part, :].T.astype(low)


def second_split(place, keep, got, kept, send):
    bit = place[HIGH]
    part = keep.shape[0] // 2
    mine, other = rows_at(bit, part), rows_at(1 - bit, part)
    kept[...] = keep[mine, :] + got[mine, :].astype(jnp.float32)
    send[...] = (keep[other, :] + got[other, :].astype(jnp.float32)).astype(low)


def pair_sum(place, keep, got, kept, send):
    part = kept.shape[0]
    mine, other = rows_at(place[X], part), rows_at(1 - place[X], part)
    kept[...] = keep[mine, :] + got[mine, :].astype(jnp.float32)
    send[...] = (keep[other, :] + got[other, :].astype(jnp.float32)).astype(low)


def down_sum(place, keep, got, out):
    out[...] = (keep[...] + got[...].astype(jnp.float32)).astype(low)


def turned_back(place, got, out):
    out[...] = got[...].astype(jnp.float32).T


def in_place(place, own, moved, out):
    got = moved[...].astype(jnp.float32)
    first = jnp.concatenate([own[...], got], axis=1)
    second = jnp.concatenate([got, own[...]], axis=1)
    out[...] = jnp.where(place[CORE] == 0, first, second)


def pair_place(place, kept, got, gate, upward):
    half = kept.shape[1] // 2
    for i, out in enumerate((gate, upward)):
        cols = slice(i * half, (i + 1) * half)
        out[:, rows_at(place[X], half)] = kept[:, cols]
        out[:, rows_at(1 - place[X], half)] = got[:, cols].astype(jnp.float32)


def far_pack(place, dq, even, got, out):
    rows, group = out.shape[0], dq.shape[1]
    out[:, :group] = dq[rows:, :]
    total = even[rows:, :].astype(jnp.float32) + got[...].astype(jnp.float32)
    out[:, group:] = total.astype(low)


def token_grad(place, grad_first, dq, even, got, far_part, *refs):
    weights, out = refs[:-1], refs[-1]
    rows = grad_first.shape[0]
    kind = len(weights) // 2
    total = grad_first[...]
    key_value = (
        even[:rows, :].astype(jnp.float32) + got[...].astype(jnp.float32)
    ).astype(low)
    group = dq.shape[1]
    for i in range(kind):
        cols = slice(i * group, (i + 1) * group)
        mine = dq[:rows, :] if i == 0 else key_value[:, (i - 1) * group : i * group]
        total = total + nt(mine, weights[i][...]) + nt(far_part[:, cols], weights[kind + i][...])
    out[...] = total.astype(low)


def after(value, *others):
    return lax.optimization_barrier((value,) + others)[0]


def fast(
    tokens,
    cotangent,
    lengths,
    input_weight,
    output_weight,
    gate_weight,
    up_weight,
    down_weight,
    gain_one,
    bias_one,
    gain_two,
    bias_two,
):
    rows, width = tokens.shape
    hidden = gate_weight.shape[1]
    seq = lax.axis_index("seq")
    data = lax.axis_index("dp")
    n_seq, n_data = lax.axis_size("seq"), lax.axis_size("dp")
    core, side = seq % 2, seq // 2
    bit_x, bit_low, bit_high = data % 2, (data // 2) % 2, data // 4
    pairs, lones = (0, 2, 2, 4), (4, 5, 0, 1)
    table = lambda values, i: sum(jnp.where(i == k, v, 0) for k, v in enumerate(values))
    place = jnp.stack(
        [
            jnp.asarray(v, jnp.int32)
            for v in (
                seq, side, bit_x, bit_low, bit_high,
                table(pairs, seq), table(lones, seq), table(pairs, seq ^ 1), table(lones, seq ^ 1),
                2 * seq + bit_x, 2 * (seq ^ 1) + bit_x, core,
            )
        ]
    )

    def swap(value, axis, bit):
        size = n_seq if axis == "seq" else n_data
        return lax.ppermute(value, axis, [(i, i ^ bit) for i in range(size)])

    def core_swap(value):
        return swap(value, "seq", 1)

    def side_swap(value):
        return swap(value, "seq", 2)

    def x_swap(value):
        return swap(value, "dp", 1)

    far = side_swap(tokens)
    near = core_swap(tokens)

    window = 4 * rows
    two = 2 * rows
    half = HEAD // 2
    freq = rotary_base ** (-jnp.arange(half, dtype=jnp.float32) * (2.0 / HEAD))
    cosine, sine, seg_col, seg_row = pl.pallas_call(
        tables,
        grid_spec=pltpu.PrefetchScalarGridSpec(
            num_scalar_prefetch=2,
            grid=(1,),
            in_specs=[block((half, TILE))],
            out_specs=[block((window, TILE))] * 3 + [block((8, window))],
        ),
        out_shape=[
            shaped((window, TILE), full), shaped((window, TILE), full),
            shaped((window, TILE), jnp.int32), shaped((8, window), jnp.int32),
        ],
        compiler_params=pltpu.CompilerParams(vmem_limit_bytes=16 * MIB),
        cost_estimate=took("tables"),
        name="tables",
    )(place, lengths, jnp.broadcast_to(freq[:, None], (half, TILE)))

    third = lambda i: (input_weight, block((width, width), 0, i))
    heads = width // HEAD
    stats = shaped((16, rows), full)
    part = lambda v, i: (v, block((two, TILE), i, 0))
    query_row = (seg_row, block((8, rows), 0, 0))
    res = lambda shape, kind: (shaped(shape, kind), block(shape))
    query, acc, peaks, totals, near_keys, near_values = call(
        first_half, "first_half", place,
        [whole(tokens), whole(near), third(0), third(1), third(2),
         part(cosine, 0), part(sine, 0), part(seg_col, 0), query_row],
        [res((rows, width), low), res((width, rows), full), res((16, rows), full), res((16, rows), full),
         res((two, width), low), res((two, width), low)],
        [pltpu.VMEM((two, rows), full)],
        mib=22,
    )
    far_near = core_swap(after(far, peaks))
    attended_low, normed, normed_low, scaled, inverse, far_keys, far_values, far_query = call(
        second_half, "second_half", place,
        [whole(tokens), whole(far), whole(far_near), third(1), third(2), whole(output_weight),
         part(cosine, 1), part(sine, 1), part(seg_col, 1), query_row,
         whole(query), whole(acc), whole(peaks), whole(totals), whole(gain_one), whole(bias_one),
         (input_weight, block((width, width // 2), 0, lambda place: place[SIDE]))],
        [res((rows, width), low), res((rows, width), full), res((rows, width), low),
         res((rows, width), full), res((rows, TILE), full), res((two, width), low),
         res((two, width), low), res((rows, width // 2), low)],
        [pltpu.VMEM((two, rows), full), pltpu.VMEM((width, rows), full)],
        mib=22,
    )

    def spread(value):
        return [value, side_swap(value), x_swap(value)]

    normed_all = spread(normed_low)

    steps = 6
    chunk = hidden // steps
    slope_up, slope_gate, result, grad_second, grad_low, sums_two = pl.pallas_call(
        feed_forward,
        grid=(steps,),
        in_specs=[
            block((rows, width)), block((rows, width)),
            pl.BlockSpec((width, chunk), lambda j: (0, j)), pl.BlockSpec((width, chunk), lambda j: (0, j)),
            pl.BlockSpec((chunk, width), lambda j: (j, 0)),
            block((rows, width)), block((width,)), block((width,)),
        ],
        out_specs=[
            pl.BlockSpec((rows, chunk), lambda j: (0, j)), pl.BlockSpec((rows, chunk), lambda j: (0, j)),
            block((rows, width)), block((rows, width)), block((rows, width)), block((2, width)),
        ],
        out_shape=[
            shaped((rows, hidden), low), shaped((rows, hidden), low), shaped((rows, width), low),
            shaped((rows, width), full), shaped((rows, width), low), shaped((2, width), full),
        ],
        scratch_shapes=[pltpu.VMEM((rows, width), full)],
        compiler_params=pltpu.CompilerParams(
            vmem_limit_bytes=20 * MIB, dimension_semantics=("arbitrary",)
        ),
        cost_estimate=took("feed_forward"),
        name="feed_forward",
    )(
        normed, normed_low, gate_weight, up_weight, still(down_weight), cotangent, gain_two, bias_two,
    )

    def pass_on(rows_there, order):
        by_side, by_x = call(
            halves, "halves", after(place, order), [whole(v) for v in rows_there[1:]],
            [res((rows // 2, width), low)] * 2,
        )
        return [x_swap(by_side), side_swap(by_x)]

    normed_all += pass_on(normed_all, grad_low)
    grad_all = spread(grad_low)
    group = width // 2
    grad_first, branch_low, mine, other, sums = pl.pallas_call(
        feed_back,
        grid_spec=pltpu.PrefetchScalarGridSpec(
            num_scalar_prefetch=1,
            grid=(steps,),
            in_specs=[
                block((rows, width)), block((rows, width)),
                pl.BlockSpec((rows, chunk), lambda j, p: (0, j)),
                pl.BlockSpec((rows, chunk), lambda j, p: (0, j)),
                pl.BlockSpec((width, chunk), lambda j, p: (0, j)),
                pl.BlockSpec((width, chunk), lambda j, p: (0, j)),
                pl.BlockSpec((chunk, width), lambda j, p: (j, 0)), block((width, width)),
                block((rows, width)), block((rows, TILE)), block((width,)), block((2, width)),
            ],
            out_specs=[
                block((rows, width)), block((rows, width)), block((rows, group)), block((rows + 32, group)),
                block((8, width)),
            ],
            scratch_shapes=[pltpu.VMEM((rows, width), full)],
        ),
        out_shape=[
            shaped((rows, width), full), shaped((rows, width), low), shaped((rows, group), low),
            shaped((rows + 32, group), low), shaped((8, width), full),
        ],
        compiler_params=pltpu.CompilerParams(
            vmem_limit_bytes=20 * MIB, dimension_semantics=("arbitrary",)
        ),
        cost_estimate=took("feed_back"),
        name="feed_back",
    )(
        after(place, normed_all[1], normed_all[2]), grad_second, grad_low, slope_up, slope_gate, gate_weight, up_weight, down_weight,
        output_weight, scaled, inverse, gain_one, sums_two,
    )
    far_grad = side_swap(other)
    grad_all += pass_on(grad_all, sums)
    quarter = width // 4
    quarter = width // 4
    out_keep, out_send = call(
        out_grad, "out_grad", after(place, sums), [whole(branch_low), whole(attended_low)],
        [res((2 * quarter, width), full), res((2 * quarter, width), low)],
        [pltpu.VMEM((width, width), full)],
    )
    out_got = core_swap(out_send)

    of_side = lambda v: (v, block((v.shape[0], group), 0, lambda place: place[SIDE]))
    heads_of = [
        whole(tokens), whole(near), whole(far), whole(far_near), of_side(near_keys), of_side(far_keys),
        of_side(near_values), of_side(far_values), of_side(query), whole(far_query), whole(mine),
        whole(far_grad), whole(cosine), whole(sine), whole(seg_col), whole(seg_row),
    ]

    def back_one(tile, order):
        return call(
            functools.partial(back_some, (tile,), True), "back_one", order, heads_of,
            [res((two, TILE), low), res((window, 2 * TILE), low), res((3 * TILE, width), full)],
            [pltpu.VMEM((window, two), full)],
            mib=32,
        )

    back_first = back_one(0, after(place, out_keep, grad_all[1], grad_all[2]))
    eighth = hidden // 8

    def columns(owner, order, last, *earlier):
        eight = lambda place: place[owner]
        split = [
            res((width // 2, wide), kind) for kind in (full, low) for wide in (2 * eighth, eighth)
        ]
        return call(
            functools.partial(column_grads, last), "column_grads", order,
            [whole(v) for v in normed_all] + [whole(v) for v in grad_all]
            + [(still(gate_weight), block((width, eighth), 0, eight)),
               (still(up_weight), block((width, eighth), 0, eight)),
               (still(down_weight), block((eighth, width), eight, 0))]
            + [whole(v) for v in earlier],
            split if last else [res((width, 3 * eighth), low)],
            [pltpu.VMEM((2 * eighth, width), low), pltpu.VMEM((3 * eighth, width), full)]
            + ([pltpu.VMEM((width, eighth), full)] if last else []),
            mib=36,
        )

    out_keep, out_send = call(
        out_halve, "out_halve", after(place, back_first[0]), [whole(out_keep), whole(out_got)],
        [res((quarter, width), full), res((quarter, width), low)],
    )
    out_got = side_swap(out_send)
    (col_part,) = columns(OTHER, after(place, out_keep), False)
    col_got = core_swap(col_part)
    back_second = back_one(1, after(place, col_part))
    col_keep, down_keep, col_send, down_send = columns(OWN, after(place, back_second[0]), True, col_got)
    col_got = swap(col_send, "dp", 2)
    down_got = swap(down_send, "dp", 2)
    dq, even, odd_near, odd_far, grads = call(
        functools.partial(back_some, (2,), False), "back_rest", after(place, col_keep, out_got),
        heads_of + [whole(v) for v in back_first + back_second],
        [res((two, group), low), res((two, width), low), res((rows, width), low), res((rows, width), low),
         res((3 * group, width), full)],
        [pltpu.VMEM((window, two), full), pltpu.VMEM((window, width), low)],
        mib=36,
    )
    in_keep, in_send, odd_near, odd_far, sums = call(
        fold, "fold", after(place, down_got),
        [whole(grads), whole(far_grad), whole(sums), whole(odd_near), whole(odd_far)],
        [res((3 * quarter, width), full), res((3 * quarter + 16, width), low), res((rows, width), low),
         res((rows, width), low), res((8, width), full)],
    )
    in_got = core_swap(in_send)
    odd_near, odd_far = core_swap(odd_near), core_swap(odd_far)
    down_keep, down_send = call(
        second_split, "second_split", after(place, sums), [whole(down_keep), whole(down_got)],
        [res((width // 4, eighth), full), res((width // 4, eighth), low)],
    )
    down_got = swap(down_send, "dp", 4)

    share = width // n_data
    keep, send, sums = call(
        turn_over, "turn_over", after(place, down_keep),
        [whole(in_keep), whole(in_got), whole(out_keep), whole(out_got), whole(sums)],
        [res((4 * share, width), full), res((4 * share + 16, width), low), res((8, width), full)],
        [pltpu.VMEM((width, width), full)],
        mib=24,
    )
    got = x_swap(send)
    (far_send,) = call(
        far_pack, "far_pack", after(place, sums), [whole(dq), whole(even), whole(odd_far)],
        [res((rows, 3 * group), low)],
    )
    far_part = side_swap(far_send)
    col_keep, col_send = call(
        second_split, "second_split", after(place, far_send), [whole(col_keep), whole(col_got)],
        [res((width // 4, 2 * eighth), full), res((width // 4, 2 * eighth), low)],
    )
    col_got = swap(col_send, "dp", 4)
    keep, send, sums = call(
        halve_low, "halve_low", after(place, col_keep),
        [whole(keep), whole(got), whole(sums)],
        [res((2 * share, width), full), res((2 * share + 16, width), low), res((8, width), full)],
    )
    got = swap(send, "dp", 2)
    weight_at = lambda i, own: (
        still(input_weight),
        block((width, group), 0, lambda place: 2 * i + (place[SIDE] if own else 1 - place[SIDE])),
    )
    (grad_tokens,) = call(
        token_grad, "token_grad", after(place, sums),
        [whole(grad_first), whole(dq), whole(even), whole(odd_near), whole(far_part)]
        + [weight_at(i, True) for i in range(3)] + [weight_at(i, False) for i in range(3)],
        [res((rows, width), low)],
        mib=24,
    )
    order = []
    for d in range(n_data):
        for s in range(n_seq):
            order.append((d * n_seq + s, (2 * s + d % 2) * n_seq + d // 2))
    (down,) = call(
        down_sum, "down_sum", after(place, grad_tokens), [whole(down_keep), whole(down_got)],
        [res((width // 4, eighth), low)],
    )
    down_got = lax.ppermute(down, ("dp", "seq"), order)
    keep, send, sums = call(
        halve, "halve", after(place, down), [whole(keep), whole(got), whole(sums)],
        [res((share, width), full), res((share + 16, width), low), res((8, width), full)],
    )
    got = swap(send, "dp", 4)
    pair_kept, pair_send = call(
        pair_sum, "pair_sum", after(place, sums), [whole(col_keep), whole(col_got)],
        [res((share, 2 * eighth), full), res((share, 2 * eighth), low)],
    )
    pair_got = x_swap(pair_send)
    in_own, in_send, grad_out, *vectors = call(
        last_sum, "last_sum", after(place, pair_send), [whole(keep), whole(got), whole(sums)],
        [res((share, 2 * quarter), full), res((share, quarter), low), res((share, quarter), full)]
        + [res((width,), full)] * 4,
    )
    in_moved = side_swap(in_send)
    grad_gate, grad_up = call(
        pair_place, "pair_place", after(place, in_send), [whole(pair_kept), whole(pair_got)],
        [res((share, 2 * eighth), full), res((share, 2 * eighth), full)],
    )
    (grad_down,) = call(
        turned_back, "turned_back", after(place, grad_gate), [whole(down_got)],
        [res((eighth, quarter), full)],
    )
    (grad_in,) = call(
        in_place, "in_place", after(place, grad_down), [whole(in_own), whole(in_moved)],
        [res((share, 3 * quarter), full)],
    )
    return (
        result,
        grad_tokens,
        grad_in,
        grad_out,
        grad_gate,
        grad_up,
        grad_down,
        *vectors,
    )


def solution(mesh):
    placed = (
        P(("dp", "seq"), None),
        P(("dp", "seq"), None),
        P("dp", None),
        P(),
        P(),
        P(),
        P(),
        P(),
        P(),
        P(),
        P(),
        P(),
    )
    paired = mesh.shape["seq"] == 4 and mesh.shape["dp"] == 8
    return jax.shard_map(
        fast if paired else general,
        mesh=mesh,
        in_specs=placed,
        out_specs=(
            P(("dp", "seq"), None),
            P(("dp", "seq"), None),
            P("dp", "seq"),
            P("dp", "seq"),
            P("dp", "seq"),
            P("dp", "seq"),
            P("dp", "seq"),
            P(),
            P(),
            P(),
            P(),
        ),
        check_vma=False,
    )
```

```python
import functools
import math

import jax
import jax.numpy as jnp
import numpy as np
from jax import lax
from jax.experimental import pallas as pl
from jax.experimental.pallas import tpu as pltpu
from jax.sharding import PartitionSpec as P

HEAD = 64


norm_eps = 1e-05
rotary_base = 1000.0
masked_value = -1e30


def doc_layout(lengths_row, count):
    ends = jnp.cumsum(lengths_row)
    place = jnp.arange(count, dtype=jnp.int32)
    after = (place[:, None] >= ends[None, :]).astype(jnp.int32)
    segment = jnp.sum(after, axis=1)
    start = jnp.sum(after * lengths_row[None, :], axis=1)
    return (segment, place - start)


def rotate(field, position):
    half = field.shape[-1] // 2
    freq = rotary_base ** (-jnp.arange(half, dtype=jnp.float32) * (2.0 / field.shape[-1]))
    angle = position.astype(jnp.float32)[:, None] * freq[None, :]
    cosine = jnp.cos(angle)[:, None, :]
    sine = jnp.sin(angle)[:, None, :]
    first = field[..., :half]
    second = field[..., half:]
    return jnp.concatenate(
        [first * cosine - second * sine, second * cosine + first * sine], axis=-1
    )


def norm_forward(value, gain, shift):
    mean = jnp.mean(value, axis=-1, keepdims=True)
    centred = value - mean
    inverse = lax.rsqrt(jnp.mean(centred * centred, axis=-1, keepdims=True) + norm_eps)
    scaled = centred * inverse
    return (scaled * gain + shift, scaled, inverse)


def norm_backward(grad, scaled, inverse, gain):
    inner = grad * gain
    back = inverse * (
        inner
        - jnp.mean(inner, axis=-1, keepdims=True)
        - scaled * jnp.mean(inner * scaled, axis=-1, keepdims=True)
    )
    return (back, jnp.sum(grad * scaled, axis=0), jnp.sum(grad, axis=0))


def inner_rows(left, right):
    return lax.dot_general(
        left, right, (((0,), (0,)), ((), ())), preferred_element_type=jnp.float32
    )


def times_transpose(left, right):
    return lax.dot_general(
        left, right, (((1,), (1,)), ((), ())), preferred_element_type=jnp.float32
    )


def general(
    tokens,
    cotangent,
    lengths,
    input_weight,
    output_weight,
    gate_weight,
    up_weight,
    down_weight,
    gain_one,
    bias_one,
    gain_two,
    bias_two,
):
    rows, width = tokens.shape
    heads = width // HEAD
    window = rows * lax.axis_size("seq")
    scale = 1.0 / math.sqrt(HEAD)
    segment_all, position_all = doc_layout(lengths[0], window)
    offset = lax.axis_index("seq") * rows
    seg_mine = lax.dynamic_slice_in_dim(segment_all, offset, rows)
    pos_mine = lax.dynamic_slice_in_dim(position_all, offset, rows)
    projected = jnp.dot(tokens, input_weight, preferred_element_type=jnp.float32)
    query = rotate(projected[:, :width].reshape(rows, heads, HEAD), pos_mine).astype(jnp.bfloat16)
    key = (
        rotate(projected[:, width : 2 * width].reshape(rows, heads, HEAD), pos_mine)
        .astype(jnp.bfloat16)
        .reshape(rows, width)
    )
    value = projected[:, 2 * width :].astype(jnp.bfloat16)

    def scores_for(key_block, seg_block):
        scores = (
            jnp.einsum("qhe,khe->hqk", query, key_block, preferred_element_type=jnp.float32) * scale
        )
        same = (seg_mine[:, None] == seg_block[None, :])[None]
        return (jnp.where(same, scores, masked_value), same)

    def split_blocks(piece, segs):
        count = piece[0].shape[0]
        size = math.gcd(count, 512)
        keys = piece[0].reshape(count // size, size, heads, HEAD)
        values = piece[1].reshape(count // size, size, heads, HEAD)
        return (keys, values, segs.reshape(count // size, size), count, size)

    start_state = (
        jnp.zeros((rows, heads, HEAD), jnp.float32),
        jnp.full((heads, rows), masked_value, jnp.float32),
        jnp.zeros((heads, rows), jnp.float32),
    )
    segs = segment_all
    keys, values, seg_blocks, count, size = split_blocks(
        (
            lax.all_gather(key, "seq", axis=0, tiled=True),
            lax.all_gather(value, "seq", axis=0, tiled=True),
        ),
        segs,
    )

    def forward_step(state, item):
        summed, peak, total = state
        key_block, value_block, seg_block = item
        scores, same = scores_for(key_block, seg_block)
        new_peak = jnp.maximum(peak, jnp.max(scores, axis=-1))
        fade = jnp.exp(peak - new_peak)
        weight = jnp.where(same, jnp.exp(scores - new_peak[..., None]), 0.0)
        total = total * fade + jnp.sum(weight, axis=-1)
        summed = summed * fade.T[..., None] + jnp.einsum(
            "hqk,khe->qhe",
            weight.astype(jnp.bfloat16),
            value_block,
            preferred_element_type=jnp.float32,
        )
        return ((summed, new_peak, total), None)

    state, unused = lax.scan(forward_step, start_state, (keys, values, seg_blocks))
    summed, peak, total = state
    attended = (summed / total.T[..., None]).reshape(rows, width)
    attended_low = attended.astype(jnp.bfloat16)
    first = tokens.astype(jnp.float32) + jnp.dot(
        attended_low, output_weight, preferred_element_type=jnp.float32
    )
    normed, scaled_one, inverse_one = norm_forward(first, gain_one, bias_one)
    normed_low = normed.astype(jnp.bfloat16)
    gate = jnp.dot(normed_low, gate_weight, preferred_element_type=jnp.float32)
    upward = jnp.dot(normed_low, up_weight, preferred_element_type=jnp.float32)
    sigma = jax.nn.sigmoid(gate)
    activated = gate * sigma
    hidden_low = (activated * upward).astype(jnp.bfloat16)
    second = normed + jnp.dot(hidden_low, down_weight, preferred_element_type=jnp.float32)
    result, scaled_two, inverse_two = norm_forward(second, gain_two, bias_two)
    grad_second, grad_gain_two, grad_bias_two = norm_backward(
        cotangent.astype(jnp.float32), scaled_two, inverse_two, gain_two
    )
    grad_ff_low = grad_second.astype(jnp.bfloat16)
    grad_hidden = times_transpose(grad_ff_low, down_weight)
    grad_gate_low = (grad_hidden * upward * (sigma * (1.0 + gate * (1.0 - sigma)))).astype(
        jnp.bfloat16
    )
    grad_up_low = (grad_hidden * activated).astype(jnp.bfloat16)
    grad_normed = (
        grad_second
        + times_transpose(grad_gate_low, gate_weight)
        + times_transpose(grad_up_low, up_weight)
    )
    grad_first, grad_gain_one, grad_bias_one = norm_backward(
        grad_normed, scaled_one, inverse_one, gain_one
    )
    grad_branch_low = grad_first.astype(jnp.bfloat16)
    grad_attended_low = times_transpose(grad_branch_low, output_weight).astype(jnp.bfloat16)
    grad_heads = grad_attended_low.reshape(rows, heads, HEAD)
    delta = jnp.sum(
        (grad_attended_low.astype(jnp.float32) * attended).reshape(rows, heads, HEAD), axis=-1
    ).T
    zero_query = jnp.zeros((rows, heads, HEAD), jnp.float32)
    grad_acc = zero_query
    segs = segment_all
    grad_query = grad_acc
    keys, values, seg_blocks, count, size = split_blocks(
        (
            lax.all_gather(key, "seq", axis=0, tiled=True),
            lax.all_gather(value, "seq", axis=0, tiled=True),
        ),
        segs,
    )

    def backward_step(grad_acc, item):
        key_block, value_block, seg_block = item
        scores, same = scores_for(key_block, seg_block)
        prob = jnp.where(same, jnp.exp(scores - peak[..., None]) / total[..., None], 0.0)
        prob_grad = jnp.einsum(
            "qhe,khe->hqk", grad_heads, value_block, preferred_element_type=jnp.float32
        )
        score_grad = (prob * (prob_grad - delta[..., None])).astype(jnp.bfloat16)
        grad_acc = (
            grad_acc
            + jnp.einsum("hqk,khe->qhe", score_grad, key_block, preferred_element_type=jnp.float32)
            * scale
        )
        prob_low = prob.astype(jnp.bfloat16)
        key_grad = (
            jnp.einsum("hqk,qhe->khe", score_grad, query, preferred_element_type=jnp.float32)
            * scale
        )
        value_grad = jnp.einsum(
            "hqk,qhe->khe", prob_low, grad_heads, preferred_element_type=jnp.float32
        )
        return (grad_acc, (key_grad.reshape(size, width), value_grad.reshape(size, width)))

    grad_query, outputs = lax.scan(backward_step, grad_query, (keys, values, seg_blocks))
    grad_acc = grad_query
    key_part = outputs[0].reshape(count, width)
    value_part = outputs[1].reshape(count, width)
    grad_key, grad_value = (
        lax.psum_scatter(
            key_part.astype(jnp.bfloat16), "seq", scatter_dimension=0, tiled=True
        ).astype(jnp.float32),
        lax.psum_scatter(
            value_part.astype(jnp.bfloat16), "seq", scatter_dimension=0, tiled=True
        ).astype(jnp.float32),
    )
    query_back = rotate(grad_acc, -pos_mine).reshape(rows, width)
    key_back = rotate(grad_key.reshape(rows, heads, HEAD), -pos_mine).reshape(rows, width)
    grad_projected_low = jnp.concatenate([query_back, key_back, grad_value], axis=1).astype(
        jnp.bfloat16
    )
    grad_tokens = (grad_first + times_transpose(grad_projected_low, input_weight)).astype(
        jnp.bfloat16
    )
    column_grads = (
        lax.all_to_all(grad_projected_low, "seq", split_axis=1, concat_axis=0, tiled=True),
        lax.all_to_all(grad_branch_low, "seq", split_axis=1, concat_axis=0, tiled=True),
        lax.all_to_all(grad_gate_low, "seq", split_axis=1, concat_axis=0, tiled=True),
        lax.all_to_all(grad_up_low, "seq", split_axis=1, concat_axis=0, tiled=True),
        lax.all_to_all(grad_ff_low, "seq", split_axis=1, concat_axis=0, tiled=True),
    )
    tok_rows = lax.all_gather(tokens, "seq", axis=0, tiled=True)
    normed_rows = lax.all_gather(normed_low, "seq", axis=0, tiled=True)
    attended_rows = lax.all_gather(attended_low, "seq", axis=0, tiled=True)
    hidden_rows = lax.all_gather(hidden_low, "seq", axis=0, tiled=True)
    count = tok_rows.shape[0]
    cols = [member for member in column_grads]
    summed_grads = (
        lax.psum_scatter(
            inner_rows(tok_rows, cols[0]).astype(jnp.bfloat16),
            "dp",
            scatter_dimension=0,
            tiled=True,
        ).astype(jnp.float32),
        lax.psum_scatter(
            inner_rows(attended_rows, cols[1]).astype(jnp.bfloat16),
            "dp",
            scatter_dimension=0,
            tiled=True,
        ).astype(jnp.float32),
        lax.psum_scatter(
            inner_rows(normed_rows, cols[2]).astype(jnp.bfloat16),
            "dp",
            scatter_dimension=0,
            tiled=True,
        ).astype(jnp.float32),
        lax.psum_scatter(
            inner_rows(normed_rows, cols[3]).astype(jnp.bfloat16),
            "dp",
            scatter_dimension=0,
            tiled=True,
        ).astype(jnp.float32),
        lax.psum_scatter(
            inner_rows(hidden_rows, cols[4]).astype(jnp.bfloat16),
            "dp",
            scatter_dimension=0,
            tiled=True,
        ).astype(jnp.float32),
    )
    norm_grads = lax.psum(
        (grad_gain_one, grad_bias_one, grad_gain_two, grad_bias_two), ("dp", "seq")
    )
    return (
        result.astype(jnp.bfloat16),
        grad_tokens,
        summed_grads[0],
        summed_grads[1],
        summed_grads[2],
        summed_grads[3],
        summed_grads[4],
        norm_grads[0],
        norm_grads[1],
        norm_grads[2],
        norm_grads[3],
    )


low = jnp.bfloat16
full = jnp.float32
TILE = 128
MIB = 1024 * 1024


def nn(left, right):
    return lax.dot_general(
        left, right, (((1,), (0,)), ((), ())), preferred_element_type=jnp.float32
    )


def nt(left, right):
    return lax.dot_general(
        left, right, (((1,), (1,)), ((), ())), preferred_element_type=jnp.float32
    )


def tn(left, right):
    return lax.dot_general(
        left, right, (((0,), (0,)), ((), ())), preferred_element_type=jnp.float32
    )


def block(shape, *at):
    at = at or (0,) * len(shape)

    def index(*args):
        return tuple(a(*args[1:]) if callable(a) else a for a in at)

    return pl.BlockSpec(tuple(shape), index)


def shaped(shape, kind):
    return jax.ShapeDtypeStruct(tuple(shape), kind)


SEQ, SIDE, X, LOW, HIGH, PAIR, LONE, OTHER_PAIR, OTHER_LONE, OWN, OTHER, CORE = range(12)

COST = {
    "tables": 1.5, "first_half": 6.9, "second_half": 7.9, "feed_forward": 8.4, "feed_back": 8.6,
    "project_heads": 4, "back_one": 6.5, "back_rest": 7, "column_grads": 7.5, "token_grad": 3,
    "out_grad": 1.2,
}


def took(name):
    return pl.CostEstimate(flops=int(COST.get(name, 0.5) * 10**9), bytes_accessed=1, transcendentals=0)


def still(value):
    return pltpu.with_memory_space_constraint(value, pltpu.HBM)


def call(body, name, scalars, operands, results, scratch=(), mib=16):
    return pl.pallas_call(
        body,
        grid_spec=pltpu.PrefetchScalarGridSpec(
            num_scalar_prefetch=1,
            grid=(1,),
            in_specs=[spec for unused, spec in operands],
            out_specs=[spec for unused, spec in results],
            scratch_shapes=list(scratch),
        ),
        out_shape=[shape for shape, unused in results],
        compiler_params=pltpu.CompilerParams(
            vmem_limit_bytes=mib * MIB, dimension_semantics=("arbitrary",)
        ),
        cost_estimate=took(name),
        name=name,
    )(scalars, *[value for value, unused in operands])


def whole(value):
    return (value, block(value.shape))


def turn(field, cosine, sine):
    lane = lax.broadcasted_iota(jnp.int32, field.shape, 1)
    half = HEAD // 2
    other = jnp.where(
        lane % HEAD < half, pltpu.roll(field, TILE - half, 1), pltpu.roll(field, half, 1)
    )
    return field * cosine + other * sine


def one_head(pair, which):
    lane = lax.broadcasted_iota(jnp.int32, pair.shape, 1)
    return jnp.where((lane // HEAD) == which, pair, jnp.zeros_like(pair))


def rows_at(index, count):
    return pl.ds(pl.multiple_of(index * count, count), count)


def pack(sums):
    high = sums.astype(low)
    return jnp.concatenate([high, (sums - high.astype(jnp.float32)).astype(low)], axis=0)


def unpack(packed):
    wide = packed.astype(jnp.float32)
    return wide[:8] + wide[8:]


def tables(place, lengths, freq, cosine, sine, seg_col, seg_row):
    count = cosine.shape[0]
    rows = count // 4
    lane = lax.broadcasted_iota(jnp.int32, (8, count), 1)
    index = jnp.zeros_like(lane)
    for i in range(1, 4):
        index = index + (lane >= i * rows).astype(jnp.int32)
    spot = (index ^ place[SEQ]) * rows + (lane - index * rows)
    end = jnp.int32(0)
    segment = jnp.zeros_like(lane)
    start = jnp.zeros_like(lane)
    for i in range(lengths.shape[1]):
        length = lengths[0, i]
        end = end + length
        past = (spot >= end).astype(jnp.int32)
        segment = segment + past
        start = start + past * length
    position = (spot - start).astype(jnp.float32)
    angle = freq[:, :1] * position[:1]
    c, s = jnp.cos(angle), jnp.sin(angle)
    cosine[...] = jnp.concatenate([c] * 4, axis=0).T
    sine[...] = jnp.concatenate([-s, s] * 2, axis=0).T
    seg_row[...] = segment
    wide = jnp.broadcast_to(segment[:1].astype(jnp.float32), (TILE, count))
    seg_col[...] = wide.T.astype(jnp.int32)


def put_keys(tokens, wk, wv, cosine, sine, keys, values, start):
    rows = tokens.shape[0]
    projected = nn(tokens, wk)
    for tile in range(projected.shape[1] // TILE):
        cols = slice(tile * TILE, (tile + 1) * TILE)
        keys[start : start + rows, cols] = turn(projected[:, cols], cosine, sine).astype(low)
    values[start : start + rows, :] = nn(tokens, wv).astype(low)


def put_query(tokens, wq, cosine, sine, query):
    scale = 1.0 / math.sqrt(HEAD)
    projected = nn(tokens, wq)
    for tile in range(projected.shape[1] // TILE):
        cols = slice(tile * TILE, (tile + 1) * TILE)
        turned = turn(projected[:, cols], cosine, sine)
        query[:, cols] = (turned.astype(low) * scale).astype(low)


def attend(query, keys, values, bias, take):
    @pl.loop(0, query.shape[1] // TILE, unroll=3)
    def _(tile):
        cols = rows_at(tile, TILE)
        key_pair = keys[:, cols]
        value_pair = values[:, cols]
        query_pair = query[:, cols]
        for which in range(TILE // HEAD):
            scores = nt(key_pair, one_head(query_pair, which)) + bias[...]
            peak = jnp.max(scores, axis=0, keepdims=True)
            weight = jnp.exp(scores - peak)
            total = jnp.sum(weight, axis=0, keepdims=True)
            out = tn(value_pair, weight.astype(low))[which * HEAD : (which + 1) * HEAD]
            take(tile * (TILE // HEAD) + which, out, peak, total)


def first_half(
    place, own, near, wq, wk, wv, cosine, sine, seg_key, seg_query, query, acc, peaks, totals,
    keys, values, bias,
):
    rows = own.shape[0]
    put_query(own[...], wq[...], cosine[:rows, :], sine[:rows, :], query)
    put_keys(own[...], wk[...], wv[...], cosine[:rows, :], sine[:rows, :], keys, values, 0)
    put_keys(near[...], wk[...], wv[...], cosine[rows:, :], sine[rows:, :], keys, values, rows)
    bias[...] = jnp.where(seg_key[:, :1] == seg_query[:1, :], 0.0, masked_value)

    def take(head, out, peak, total):
        acc[rows_at(head, HEAD), :] = out
        peaks[pl.ds(head, 1), :] = peak
        totals[pl.ds(head, 1), :] = total

    attend(query, keys, values, bias, take)


def second_half(
    place, own, far, far_near, wk, wv, wo, cosine, sine, seg_key, seg_query, query, acc, peaks, totals,
    gain, shift, far_wq, attended_low, normed, normed_low, scaled, inverse, keys, values, far_query, logs, bias,
    turned,
):
    rows, width = own.shape
    put_keys(far[...], wk[...], wv[...], cosine[:rows, :], sine[:rows, :], keys, values, 0)
    put_keys(far_near[...], wk[...], wv[...], cosine[rows:, :], sine[rows:, :], keys, values, rows)
    bias[...] = jnp.where(seg_key[:, :1] == seg_query[:1, :], 0.0, masked_value)
    put_query(far[...], far_wq[...], cosine[:rows, :], sine[:rows, :], far_query)
    side_heads = width // HEAD // 2
    logs[...] = jnp.zeros_like(logs)

    def take(head, out, peak, total):
        part = rows_at(head, HEAD)
        before = peaks[pl.ds(head, 1), :]
        best = jnp.maximum(before, peak)
        fade = jnp.exp(before - best)
        grow = jnp.exp(peak - best)
        whole_total = totals[pl.ds(head, 1), :] * fade + total * grow
        logs[pl.ds(head + jnp.where(head >= side_heads, 8 - side_heads, 0), 1), :] = best + jnp.log(whole_total)
        inverse_total = 1.0 / whole_total
        turned[part, :] = acc[part, :] * (fade * inverse_total) + out * (grow * inverse_total)

    attend(query, keys, values, bias, take)
    attended = turned[...].T.astype(low)
    attended_low[...] = attended
    first = own[...].astype(jnp.float32) + nn(attended, wo[...])
    mean = jnp.mean(first, axis=1, keepdims=True)
    centred = first - mean
    spread = lax.rsqrt(jnp.mean(centred * centred, axis=1, keepdims=True) + norm_eps)
    unit = centred * spread
    value = unit * gain[...][None, :] + shift[...][None, :]
    scaled[...] = unit
    inverse[...] = jnp.broadcast_to(spread, (rows, TILE))
    normed[...] = value
    normed_low[...] = value.astype(low)


def halves(place, by_side, by_low, first, second):
    half = first.shape[0]
    first[...] = by_side[:half, :]
    second[...] = by_low[half:, :]


def feed_forward(
    normed, normed_low, wg, wu, wd, cotangent, gain, shift,
    slope_up, slope_gate, result, grad_second, grad_low, sums, acc,
):
    chunk = wg.shape[1] // 4
    acc[...] = normed[...]

    @pl.loop(0, 4, unroll=4)
    def _(step):
        cols = rows_at(step, chunk)
        gate = nn(normed_low[...], wg[:, cols])
        upward = nn(normed_low[...], wu[:, cols])
        sigma = jax.nn.sigmoid(gate)
        active = gate * sigma
        slope_up[:, cols] = active.astype(low)
        slope_gate[:, cols] = (upward * (sigma * (1.0 + gate * (1.0 - sigma)))).astype(low)
        acc[...] += nn((active * upward).astype(low), wd[cols, :])

    if True:
        second = acc[...]
        mean = jnp.mean(second, axis=1, keepdims=True)
        centred = second - mean
        spread = lax.rsqrt(jnp.mean(centred * centred, axis=1, keepdims=True) + norm_eps)
        unit = centred * spread
        result[...] = (unit * gain[...][None, :] + shift[...][None, :]).astype(low)
        grad = cotangent[...].astype(jnp.float32)
        inner = grad * gain[...][None, :]
        back = spread * (
            inner
            - jnp.mean(inner, axis=1, keepdims=True)
            - unit * jnp.mean(inner * unit, axis=1, keepdims=True)
        )
        grad_second[...] = back
        grad_low[...] = back.astype(low)
        sums[0:1, :] = jnp.sum(grad * unit, axis=0, keepdims=True)
        sums[1:2, :] = jnp.sum(grad, axis=0, keepdims=True)


def feed_back(
    place, grad_second, grad_low, slope_up, slope_gate, wg, wu, wd, wo, scaled, inverse, gain, sums_two,
    attended_low, logs, grad_first, branch_low, mine, other, sums, stats, acc,
):
    chunk = wg.shape[1] // 4
    acc[...] = grad_second[...]

    @pl.loop(0, 4, unroll=4)
    def _(step):
        cols = rows_at(step, chunk)
        hidden = nt(grad_low[...], wd[cols, :])
        gate = (hidden * slope_gate[:, cols].astype(jnp.float32)).astype(low)
        upward = (hidden * slope_up[:, cols].astype(jnp.float32)).astype(low)
        acc[...] += nt(gate, wg[:, cols]) + nt(upward, wu[:, cols])

    if True:
        grad = acc[...]
        unit = scaled[...]
        inner = grad * gain[...][None, :]
        back = inverse[:, :1] * (
            inner
            - jnp.mean(inner, axis=1, keepdims=True)
            - unit * jnp.mean(inner * unit, axis=1, keepdims=True)
        )
        grad_first[...] = back
        branch_low[...] = back.astype(low)
        attended_grad = nt(branch_low[...], wo[...]).astype(low)
        group = mine.shape[1]
        height = mine.shape[0]
        left, right = attended_grad[:, :group], attended_grad[:, group:]
        second_side = place[SIDE] > 0
        mine[...] = jnp.where(second_side, right, left)
        other[:height, :] = jnp.where(second_side, left, right)
        sums[...] = jnp.zeros_like(sums)
        sums[0:1, :] = jnp.sum(grad * unit, axis=0, keepdims=True)
        sums[1:2, :] = jnp.sum(grad, axis=0, keepdims=True)
        sums[2:4, :] = sums_two[...]
        for i in range(2):
            part = slice(height + i * 16, height + (i + 1) * 16)
            other[part, :] = pack(sums[:, i * group : (i + 1) * group])
        product = attended_grad.astype(jnp.float32) * attended_low[...].astype(jnp.float32)
        high = product.astype(low)
        rest = (product - high.astype(jnp.float32)).astype(low)
        row = lax.broadcasted_iota(jnp.int32, (16, 2 * group), 0)
        lane = lax.broadcasted_iota(jnp.int32, (16, 2 * group), 1)
        head = lane // HEAD
        ones = (row == head + jnp.where(lane >= group, 8 - group // HEAD, 0)).astype(low)
        deltas = nt(ones, high) + nt(ones, rest)
        left, right = (
            jnp.concatenate([logs[part, :], deltas[part, :]], axis=0) for part in (slice(0, 8), slice(8, 16))
        )
        stats[...] = jnp.where(second_side, right, left)
        rest = jnp.where(second_side, left, right)
        other[height + 32 :, height:] = jnp.zeros((48, group - height), low)
        for i in range(3):
            part = slice(height + 32 + i * 16, height + 48 + i * 16)
            piece = rest.astype(low)
            other[part, :height] = piece
            rest = rest - piece.astype(jnp.float32)


def out_grad(place, branch_low, attended_low, keep, send, turned):
    turned[...] = tn(branch_low[...], attended_low[...])
    quarter = turned.shape[0] // 4
    core = place[CORE]
    for i in range(2):
        to = slice(i * quarter, (i + 1) * quarter)
        keep[to, :] = turned[rows_at(2 * i + core, quarter), :]
        send[to, :] = turned[rows_at(2 * i + 1 - core, quarter), :].astype(low)


def out_halve(place, keep, got, kept, send):
    quarter = keep.shape[0] // 2
    mine, other = rows_at(place[SIDE], quarter), rows_at(1 - place[SIDE], quarter)
    kept[...] = keep[mine, :] + got[mine, :].astype(jnp.float32)
    send[...] = (keep[other, :] + got[other, :].astype(jnp.float32)).astype(low)


def back_tile(key_pair, value_pair, query_pair, grad_pair, bias, logs, deltas):
    scale = 1.0 / math.sqrt(HEAD)
    grad_key = None
    grad_value = None
    pieces = []
    for which in range(TILE // HEAD):
        query_head = one_head(query_pair, which)
        grad_head = one_head(grad_pair, which)
        scores = nt(key_pair, query_head) + bias[...]
        prob = jnp.exp(scores - logs[which])
        prob_grad = nt(value_pair, grad_head)
        score_grad = (prob * (prob_grad - deltas[which])).astype(low)
        value_part = nn(prob.astype(low), grad_head)
        key_part = nn(score_grad, query_head)
        grad_key = key_part if grad_key is None else grad_key + key_part
        grad_value = value_part if grad_value is None else grad_value + value_part
        pieces.append(tn(key_pair, score_grad)[which * HEAD : (which + 1) * HEAD])
    return jnp.concatenate(pieces, axis=0).T * scale, grad_key, grad_value


def back_some(tiles, first, place, *refs):
    own, near, far, far_near = refs[:4]
    pairs = [refs[i : i + 2] for i in range(4, 12, 2)]
    cosine, sine, seg_key, seg_query, stats = refs[12:17]
    far_grad = refs[11]
    rows = own.shape[0]
    blocks = (own, near, far, far_near)
    if first:
        dq, both, grads, bias = refs[17:]
    else:
        before = refs[17:23]
        dq, even, odd_near, odd_far, grads, bias, both = refs[23:]
    group = pairs[0][0].shape[1]
    for index in range(2):
        part = slice(2 * index * rows, (2 * index + 1) * rows)
        to = slice(index * rows, (index + 1) * rows)
        bias[:, to] = jnp.where(seg_key[:, :1] == seg_query[:1, part], 0.0, masked_value)
    far_stats = sum(
        far_grad[rows + 32 + i * 16 : rows + 48 + i * 16, :rows].astype(jnp.float32) for i in range(3)
    )
    both_stats = jnp.concatenate([stats[...], far_stats], axis=1)
    for tile in tiles:
        cols = slice(tile * TILE, (tile + 1) * TILE)
        heads = [tile * (TILE // HEAD) + which for which in range(TILE // HEAD)]
        logs = [both_stats[head : head + 1] for head in heads]
        deltas = [both_stats[8 + head : 9 + head] for head in heads]
        keys, values, queries, outs = (
            jnp.concatenate([one[:, cols], two[: one.shape[0], cols]], axis=0) for one, two in pairs
        )
        grad_query, grad_key, grad_value = back_tile(
            keys, values, queries, outs, bias, logs, deltas
        )
        to = slice(0, TILE) if first else cols
        shifted = slice(TILE, 2 * TILE) if first else slice(group + tile * TILE, group + (tile + 1) * TILE)
        for index in range(2):
            part = slice(index * rows, (index + 1) * rows)
            at = slice(2 * index * rows, (2 * index + 1) * rows)
            dq[part, to] = turn(grad_query[part], cosine[at, :], -sine[at, :]).astype(low)
        both[:, to] = turn(grad_key, cosine[...], -sine[...]).astype(low)
        both[:, shifted] = grad_value.astype(low)
        pair = jnp.concatenate([both[:, to], both[:, shifted]], axis=1)
        total = None
        for index in range(4):
            part = slice(index * rows, (index + 1) * rows)
            product = tn(pair[part], blocks[index][...])
            total = product if total is None else total + product
        query_rows = tn(dq[:rows, to], own[...]) + tn(dq[rows:, to], far[...])
        if first:
            grads[:TILE, :] = query_rows
            grads[TILE:, :] = total
        else:
            grads[tile * TILE : (tile + 1) * TILE, :] = query_rows
            for kind in range(2):
                at = (kind + 1) * group + tile * TILE
                grads[at : at + TILE, :] = total[kind * TILE : (kind + 1) * TILE]
    if first:
        return
    for tile in range(2):
        dq_before, both_before, grads_before = before[3 * tile : 3 * tile + 3]
        dq[:, tile * TILE : (tile + 1) * TILE] = dq_before[...]
        for kind in range(3):
            at = kind * group + tile * TILE
            if kind < 2:
                both[:, at : at + TILE] = both_before[:, kind * TILE : (kind + 1) * TILE]
            grads[at : at + TILE, :] = grads_before[kind * TILE : (kind + 1) * TILE, :]
    for index in range(4):
        part = slice(index * rows, (index + 1) * rows)
        if index % 2:
            (odd_far if index > 1 else odd_near)[...] = both[part, :]
        else:
            even[index // 2 * rows : (index // 2 + 1) * rows, :] = both[part, :]


def fold(place, grads, far_grad, sums, odd_near, odd_far, keep, send, near_send, far_send, kept_sums):
    quarter = keep.shape[0] // 3
    pair, lone, other_pair, other_lone = (place[i] for i in (PAIR, LONE, OTHER_PAIR, OTHER_LONE))
    for i in range(3):
        to = slice(i * quarter, (i + 1) * quarter)
        keep[to, :] = grads[rows_at(pair + i if i < 2 else lone, quarter), :]
        send[to, :] = grads[rows_at(other_pair + i if i < 2 else other_lone, quarter), :].astype(low)
    rows = odd_near.shape[0]
    got = jnp.concatenate(
        [unpack(far_grad[rows : rows + 16, :]), unpack(far_grad[rows + 16 : rows + 32, :])], axis=1
    )
    total = sums[...] + got
    kept_sums[...] = total
    send[3 * quarter :, :] = pack(total)
    near_send[...] = odd_near[...]
    far_send[...] = odd_far[...]


def turn_over(place, keep, got, out_keep, out_got, sums, kept, send, kept_sums, turned):
    height = keep.shape[0]
    turned[:, :height] = (keep[...] + got[:height, :].astype(jnp.float32)).T
    turned[:, height:] = (out_keep[...] + out_got[...].astype(jnp.float32)).T
    bit = place[LOW]
    part = turned.shape[0] // 8
    for i in range(4):
        to = slice(i * part, (i + 1) * part)
        at = 4 * (i // 2) + i % 2
        kept[to, :] = turned[rows_at(at + 2 * bit, part), :]
        send[to, :] = turned[rows_at(at + 2 * (1 - bit), part), :].astype(low)
    both = sums[...] + unpack(got[height:, :])
    kept_sums[...] = both
    send[4 * part :, :] = pack(both)


def halve_x(place, keep, got, sums, kept, send, kept_sums):
    bit = place[X]
    part = keep.shape[0] // 4
    for i in range(2):
        to = slice(i * part, (i + 1) * part)
        for at, out in ((bit, kept), (1 - bit, send)):
            there = rows_at(2 * i + at, part)
            out[to, :] = (keep[there, :] + got[there, :].astype(jnp.float32)).astype(out.dtype)
    both = sums[...] + unpack(got[4 * part :, :])
    kept_sums[...] = both
    send[2 * part :, :] = pack(both)


def halve(place, keep, got, sums, kept, send, kept_sums):
    bit = place[HIGH]
    height = keep.shape[0]
    part = height // 2
    mine, other = rows_at(bit, part), rows_at(1 - bit, part)
    kept[...] = keep[mine, :] + got[mine, :].astype(jnp.float32)
    send[:part, :] = (keep[other, :] + got[other, :].astype(jnp.float32)).astype(low)
    both = sums[...] + unpack(got[height:, :])
    kept_sums[...] = both
    send[part:, :] = pack(both)


def last_sum(place, keep, got, sums, own, send, out, *vectors):
    height = keep.shape[0]
    total = keep[...] + got[:height, :].astype(jnp.float32)
    quarter = out.shape[1]
    own[...] = total[:, : 2 * quarter]
    send[...] = total[:, 2 * quarter : 3 * quarter].astype(low)
    out[...] = total[:, 3 * quarter :]
    both = sums[...] + unpack(got[height:, :])
    for i, vector in enumerate(vectors):
        vector[...] = both[i]


def column_grads(last, place, *refs):
    count = 5
    rows_refs, back_refs = refs[:count], refs[count : 2 * count]
    groups = ((0, 1), (2, 3, 4))
    wg, wu, wd = refs[2 * count : 2 * count + 3]
    rest = refs[2 * count + 3 :]
    if last:
        earlier = (rest[0], rest[-1])
        outs, wgu, acc = rest[1:5], rest[5], rest[6]
    else:
        outs, wgu, acc = rest[:1], rest[1], rest[2]
    half, width = wd.shape
    wgu[:half, :] = wg[...].astype(jnp.float32).T.astype(low)
    wgu[half:, :] = wu[...].astype(jnp.float32).T.astype(low)
    for step, group in enumerate(groups):
        rows, back = (
            jnp.concatenate([v[i][...] for i in group], axis=0) for v in (rows_refs, back_refs)
        )
        both = nt(wgu[...], rows)
        gate, upward = both[:half], both[half:]
        sigma = jax.nn.sigmoid(gate)
        active = gate * sigma
        hidden = (active * upward).astype(low)
        grad_hidden = nt(wd[...], back)
        grad_gate = (grad_hidden * upward * (sigma * (1.0 + gate * (1.0 - sigma)))).astype(low)
        grad_up = (grad_hidden * active).astype(low)
        products = (nn(grad_gate, rows), nn(grad_up, rows), nn(hidden, back))
        for i, product in enumerate(products):
            part = slice(i * half, (i + 1) * half)
            if step == 0:
                acc[part, :] = product
            else:
                acc[part, :] += product
    if last:
        got, total = earlier
        bit = place[X]
        for i in range(3):
            part = slice(i * half, (i + 1) * half)
            total[...] = acc[part, :].T + got[:, part].astype(jnp.float32)
            keep, send, to_cols = (outs[0], outs[2], part) if i < 2 else (outs[1], outs[3], slice(None))
            count = 4 if i < 2 else 2
            cut = width // (2 * count)
            for j in range(count):
                to = slice(j * cut, (j + 1) * cut)
                keep[to, to_cols] = total[rows_at(2 * j + bit, cut), :]
                send[to, to_cols] = total[rows_at(2 * j + 1 - bit, cut), :].astype(low)
    else:
        for i in range(3):
            part = slice(i * half, (i + 1) * half)
            outs[0][:, part] = acc[part, :].T.astype(low)


def second_split(place, keep, got, kept, send):
    bit = place[HIGH]
    part = keep.shape[0] // 2
    mine, other = rows_at(bit, part), rows_at(1 - bit, part)
    kept[...] = keep[mine, :] + got[mine, :].astype(jnp.float32)
    send[...] = (keep[other, :] + got[other, :].astype(jnp.float32)).astype(low)


def pair_sum(place, keep, got, kept, send):
    part = kept.shape[0]
    mine, other = rows_at(place[LOW], part), rows_at(1 - place[LOW], part)
    kept[...] = keep[mine, :] + got[mine, :].astype(jnp.float32)
    send[...] = (keep[other, :] + got[other, :].astype(jnp.float32)).astype(low)


def down_sum(place, keep, got, out):
    out[...] = (keep[...] + got[...].astype(jnp.float32)).astype(low)


def turned_back(place, got, out):
    out[...] = got[...].astype(jnp.float32).T


def in_place(place, own, moved, out):
    got = moved[...].astype(jnp.float32)
    first = jnp.concatenate([own[...], got], axis=1)
    second = jnp.concatenate([got, own[...]], axis=1)
    out[...] = jnp.where(place[CORE] == 0, first, second)


def pair_place(place, kept, got, gate, upward):
    half = kept.shape[1] // 2
    for i, out in enumerate((gate, upward)):
        cols = slice(i * half, (i + 1) * half)
        out[:, rows_at(place[LOW], half)] = kept[:, cols]
        out[:, rows_at(1 - place[LOW], half)] = got[:, cols].astype(jnp.float32)


def far_pack(place, dq, even, got, out):
    rows, group = out.shape[0], dq.shape[1]
    out[:, :group] = dq[rows:, :]
    total = even[rows:, :].astype(jnp.float32) + got[...].astype(jnp.float32)
    out[:, group:] = total.astype(low)


def token_grad(place, grad_first, dq, even, got, far_part, *refs):
    weights, out = refs[:-1], refs[-1]
    rows = grad_first.shape[0]
    kind = len(weights) // 2
    total = grad_first[...]
    key_value = (
        even[:rows, :].astype(jnp.float32) + got[...].astype(jnp.float32)
    ).astype(low)
    group = dq.shape[1]
    for i in range(kind):
        cols = slice(i * group, (i + 1) * group)
        mine = dq[:rows, :] if i == 0 else key_value[:, (i - 1) * group : i * group]
        total = total + nt(mine, weights[i][...]) + nt(far_part[:, cols], weights[kind + i][...])
    out[...] = total.astype(low)


def after(value, *others):
    return lax.optimization_barrier((value,) + others)[0]


def fast(
    tokens,
    cotangent,
    lengths,
    input_weight,
    output_weight,
    gate_weight,
    up_weight,
    down_weight,
    gain_one,
    bias_one,
    gain_two,
    bias_two,
):
    rows, width = tokens.shape
    hidden = gate_weight.shape[1]
    seq = lax.axis_index("seq")
    data = lax.axis_index("dp")
    n_seq, n_data = lax.axis_size("seq"), lax.axis_size("dp")
    core, side = seq % 2, seq // 2
    bit_x, bit_low, bit_high = data % 2, (data // 2) % 2, data // 4
    pairs, lones = (0, 2, 2, 4), (4, 5, 0, 1)
    table = lambda values, i: sum(jnp.where(i == k, v, 0) for k, v in enumerate(values))
    place = jnp.stack(
        [
            jnp.asarray(v, jnp.int32)
            for v in (
                seq, side, bit_x, bit_low, bit_high,
                table(pairs, seq), table(lones, seq), table(pairs, seq ^ 1), table(lones, seq ^ 1),
                2 * seq + bit_low, 2 * (seq ^ 1) + bit_low, core,
            )
        ]
    )

    def swap(value, axis, bit):
        size = n_seq if axis == "seq" else n_data
        return lax.ppermute(value, axis, [(i, i ^ bit) for i in range(size)])

    def core_swap(value):
        return swap(value, "seq", 1)

    def side_swap(value):
        return swap(value, "seq", 2)

    def x_swap(value):
        return swap(value, "dp", 1)

    def low_swap(value):
        return swap(value, "dp", 2)

    def high_swap(value):
        return swap(value, "dp", 4)

    far = side_swap(tokens)
    near = core_swap(tokens)

    window = 4 * rows
    two = 2 * rows
    half = HEAD // 2
    freq = rotary_base ** (-jnp.arange(half, dtype=jnp.float32) * (2.0 / HEAD))
    cosine, sine, seg_col, seg_row = pl.pallas_call(
        tables,
        grid_spec=pltpu.PrefetchScalarGridSpec(
            num_scalar_prefetch=2,
            grid=(1,),
            in_specs=[block((half, TILE))],
            out_specs=[block((window, TILE))] * 3 + [block((8, window))],
        ),
        out_shape=[
            shaped((window, TILE), full), shaped((window, TILE), full),
            shaped((window, TILE), jnp.int32), shaped((8, window), jnp.int32),
        ],
        compiler_params=pltpu.CompilerParams(vmem_limit_bytes=16 * MIB),
        cost_estimate=took("tables"),
        name="tables",
    )(place, lengths, jnp.broadcast_to(freq[:, None], (half, TILE)))

    third = lambda i: (input_weight, block((width, width), 0, i))
    part = lambda v, i: (v, block((two, TILE), i, 0))
    query_row = (seg_row, block((8, rows), 0, 0))
    res = lambda shape, kind: (shaped(shape, kind), block(shape))
    query, acc, peaks, totals, near_keys, near_values = call(
        first_half, "first_half", place,
        [whole(tokens), whole(near), third(0), third(1), third(2),
         part(cosine, 0), part(sine, 0), part(seg_col, 0), query_row],
        [res((rows, width), low), res((width, rows), full), res((16, rows), full), res((16, rows), full),
         res((two, width), low), res((two, width), low)],
        [pltpu.VMEM((two, rows), full)],
        mib=22,
    )
    far_near = core_swap(after(far, peaks))
    attended_low, normed, normed_low, scaled, inverse, far_keys, far_values, far_query, logs = call(
        second_half, "second_half", place,
        [whole(tokens), whole(far), whole(far_near), third(1), third(2), whole(output_weight),
         part(cosine, 1), part(sine, 1), part(seg_col, 1), query_row,
         whole(query), whole(acc), whole(peaks), whole(totals), whole(gain_one), whole(bias_one),
         (input_weight, block((width, width // 2), 0, lambda place: place[SIDE]))],
        [res((rows, width), low), res((rows, width), full), res((rows, width), low),
         res((rows, width), full), res((rows, TILE), full), res((two, width), low),
         res((two, width), low), res((rows, width // 2), low), res((16, rows), full)],
        [pltpu.VMEM((two, rows), full), pltpu.VMEM((width, rows), full)],
        mib=22,
    )

    def spread(value):
        return [value, side_swap(value), low_swap(value)]

    normed_all = spread(normed_low)

    inside = pl.BlockSpec(memory_space=pltpu.VMEM)
    slope_up, slope_gate, result, grad_second, grad_low, sums_two = pl.pallas_call(
        feed_forward,
        grid=(1,),
        in_specs=[
            block((rows, width)), block((rows, width)), inside, inside, inside,
            block((rows, width)), block((width,)), block((width,)),
        ],
        out_specs=[
            block((rows, hidden)), block((rows, hidden)),
            block((rows, width)), block((rows, width)), block((rows, width)), block((2, width)),
        ],
        out_shape=[
            shaped((rows, hidden), low), shaped((rows, hidden), low), shaped((rows, width), low),
            shaped((rows, width), full), shaped((rows, width), low), shaped((2, width), full),
        ],
        scratch_shapes=[pltpu.VMEM((rows, width), full)],
        compiler_params=pltpu.CompilerParams(
            vmem_limit_bytes=14 * MIB, dimension_semantics=("arbitrary",)
        ),
        cost_estimate=took("feed_forward"),
        name="feed_forward",
    )(
        normed, normed_low, gate_weight, up_weight, down_weight, cotangent, gain_two, bias_two,
    )

    def pass_on(rows_there, order):
        by_side, by_low = call(
            halves, "halves", after(place, order), [whole(v) for v in rows_there[1:]],
            [res((rows // 2, width), low)] * 2,
        )
        return [low_swap(by_side), side_swap(by_low)]

    normed_all += pass_on(normed_all, grad_low)
    grad_all = spread(grad_low)
    group = width // 2
    grad_first, branch_low, mine, other, sums, stats = pl.pallas_call(
        feed_back,
        grid_spec=pltpu.PrefetchScalarGridSpec(
            num_scalar_prefetch=1,
            grid=(1,),
            in_specs=[
                block((rows, width)), block((rows, width)),
                inside, inside, inside, inside, inside, block((width, width)),
                block((rows, width)), block((rows, TILE)), block((width,)), block((2, width)), block((rows, width)),
                block((16, rows)),
            ],
            out_specs=[
                block((rows, width)), block((rows, width)), block((rows, group)), block((rows + 80, group)),
                block((8, width)), block((16, rows)),
            ],
            scratch_shapes=[pltpu.VMEM((rows, width), full)],
        ),
        out_shape=[
            shaped((rows, width), full), shaped((rows, width), low), shaped((rows, group), low),
            shaped((rows + 80, group), low), shaped((8, width), full),
            shaped((16, rows), full),
        ],
        compiler_params=pltpu.CompilerParams(
            vmem_limit_bytes=14 * MIB, dimension_semantics=("arbitrary",)
        ),
        cost_estimate=took("feed_back"),
        name="feed_back",
    )(
        place, grad_second, grad_low, slope_up, slope_gate, gate_weight, up_weight, down_weight,
        output_weight, scaled, inverse, gain_one, sums_two, attended_low, logs,
    )
    far_grad = side_swap(other)
    grad_all += pass_on(grad_all, sums)
    quarter = width // 4
    quarter = width // 4
    out_keep, out_send = call(
        out_grad, "out_grad", after(place, sums), [whole(branch_low), whole(attended_low)],
        [res((2 * quarter, width), full), res((2 * quarter, width), low)],
        [pltpu.VMEM((width, width), full)],
    )
    out_got = core_swap(out_send)

    of_side = lambda v: (v, block((v.shape[0], group), 0, lambda place: place[SIDE]))
    heads_of = [
        whole(tokens), whole(near), whole(far), whole(far_near), of_side(near_keys), of_side(far_keys),
        of_side(near_values), of_side(far_values), of_side(query), whole(far_query), whole(mine),
        whole(far_grad), whole(cosine), whole(sine), whole(seg_col), whole(seg_row), whole(stats),
    ]

    def back_one(tile, order):
        return call(
            functools.partial(back_some, (tile,), True), "back_one", order, heads_of,
            [res((two, TILE), low), res((window, 2 * TILE), low), res((3 * TILE, width), full)],
            [pltpu.VMEM((window, two), full)],
            mib=32,
        )

    back_first = back_one(0, after(place, out_keep, grad_all[1], grad_all[2]))
    eighth = hidden // 8

    def columns(owner, order, last, *earlier):
        eight = lambda place: place[owner]
        split = [
            res((width // 2, wide), kind) for kind in (full, low) for wide in (2 * eighth, eighth)
        ]
        return call(
            functools.partial(column_grads, last), "column_grads", order,
            [whole(v) for v in normed_all] + [whole(v) for v in grad_all]
            + [(still(gate_weight), block((width, eighth), 0, eight)),
               (still(up_weight), block((width, eighth), 0, eight)),
               (still(down_weight), block((eighth, width), eight, 0))]
            + [whole(v) for v in earlier],
            split if last else [res((width, 3 * eighth), low)],
            [pltpu.VMEM((2 * eighth, width), low), pltpu.VMEM((3 * eighth, width), full)]
            + ([pltpu.VMEM((width, eighth), full)] if last else []),
            mib=36,
        )

    out_keep, out_send = call(
        out_halve, "out_halve", after(place, back_first[0]), [whole(out_keep), whole(out_got)],
        [res((quarter, width), full), res((quarter, width), low)],
    )
    out_got = side_swap(out_send)
    (col_part,) = columns(OTHER, after(place, out_keep), False)
    col_got = core_swap(col_part)
    back_second = back_one(1, after(place, col_part))
    col_keep, down_keep, col_send, down_send = columns(OWN, after(place, back_second[0]), True, col_got)
    col_got = x_swap(col_send)
    down_got = x_swap(down_send)
    dq, even, odd_near, odd_far, grads = call(
        functools.partial(back_some, (2,), False), "back_rest", after(place, col_keep, out_got),
        heads_of + [whole(v) for v in back_first + back_second],
        [res((two, group), low), res((two, width), low), res((rows, width), low), res((rows, width), low),
         res((3 * group, width), full)],
        [pltpu.VMEM((window, two), full), pltpu.VMEM((window, width), low)],
        mib=36,
    )
    in_keep, in_send, odd_near, odd_far, sums = call(
        fold, "fold", after(place, down_got),
        [whole(grads), whole(far_grad), whole(sums), whole(odd_near), whole(odd_far)],
        [res((3 * quarter, width), full), res((3 * quarter + 16, width), low), res((rows, width), low),
         res((rows, width), low), res((8, width), full)],
    )
    in_got = core_swap(in_send)
    odd_near, odd_far = core_swap(odd_near), core_swap(odd_far)
    down_keep, down_send = call(
        second_split, "second_split", after(place, sums), [whole(down_keep), whole(down_got)],
        [res((width // 4, eighth), full), res((width // 4, eighth), low)],
    )
    down_got = swap(down_send, "dp", 4)

    share = width // n_data
    keep, send, sums = call(
        turn_over, "turn_over", after(place, down_keep),
        [whole(in_keep), whole(in_got), whole(out_keep), whole(out_got), whole(sums)],
        [res((4 * share, width), full), res((4 * share + 16, width), low), res((8, width), full)],
        [pltpu.VMEM((width, width), full)],
        mib=24,
    )
    got = low_swap(send)
    (far_send,) = call(
        far_pack, "far_pack", after(place, sums), [whole(dq), whole(even), whole(odd_far)],
        [res((rows, 3 * group), low)],
    )
    far_part = side_swap(far_send)
    col_keep, col_send = call(
        second_split, "second_split", after(place, far_send), [whole(col_keep), whole(col_got)],
        [res((width // 4, 2 * eighth), full), res((width // 4, 2 * eighth), low)],
    )
    col_got = swap(col_send, "dp", 4)
    keep, send, sums = call(
        halve_x, "halve_x", after(place, col_keep),
        [whole(keep), whole(got), whole(sums)],
        [res((2 * share, width), full), res((2 * share + 16, width), low), res((8, width), full)],
    )
    got = x_swap(send)
    weight_at = lambda i, own: (
        still(input_weight),
        block((width, group), 0, lambda place: 2 * i + (place[SIDE] if own else 1 - place[SIDE])),
    )
    (grad_tokens,) = call(
        token_grad, "token_grad", after(place, sums),
        [whole(grad_first), whole(dq), whole(even), whole(odd_near), whole(far_part)]
        + [weight_at(i, True) for i in range(3)] + [weight_at(i, False) for i in range(3)],
        [res((rows, width), low)],
        mib=24,
    )
    order = []
    for d in range(n_data):
        for s in range(n_seq):
            order.append((d * n_seq + s, (2 * s + d // 2 % 2) * n_seq + d // 4 * 2 + d % 2))
    (down,) = call(
        down_sum, "down_sum", after(place, grad_tokens), [whole(down_keep), whole(down_got)],
        [res((width // 4, eighth), low)],
    )
    down_got = lax.ppermute(down, ("dp", "seq"), order)
    keep, send, sums = call(
        halve, "halve", after(place, down), [whole(keep), whole(got), whole(sums)],
        [res((share, width), full), res((share + 16, width), low), res((8, width), full)],
    )
    got = swap(send, "dp", 4)
    pair_kept, pair_send = call(
        pair_sum, "pair_sum", after(place, sums), [whole(col_keep), whole(col_got)],
        [res((share, 2 * eighth), full), res((share, 2 * eighth), low)],
    )
    pair_got = low_swap(pair_send)
    in_own, in_send, grad_out, *vectors = call(
        last_sum, "last_sum", after(place, pair_send), [whole(keep), whole(got), whole(sums)],
        [res((share, 2 * quarter), full), res((share, quarter), low), res((share, quarter), full)]
        + [res((width,), full)] * 4,
    )
    in_moved = side_swap(in_send)
    grad_gate, grad_up = call(
        pair_place, "pair_place", after(place, in_send), [whole(pair_kept), whole(pair_got)],
        [res((share, 2 * eighth), full), res((share, 2 * eighth), full)],
    )
    (grad_down,) = call(
        turned_back, "turned_back", after(place, grad_gate), [whole(down_got)],
        [res((eighth, quarter), full)],
    )
    (grad_in,) = call(
        in_place, "in_place", after(place, grad_down), [whole(in_own), whole(in_moved)],
        [res((share, 3 * quarter), full)],
    )
    return (
        result,
        grad_tokens,
        grad_in,
        grad_out,
        grad_gate,
        grad_up,
        grad_down,
        *vectors,
    )


def solution(mesh):
    placed = (
        P(("dp", "seq"), None),
        P(("dp", "seq"), None),
        P("dp", None),
        P(),
        P(),
        P(),
        P(),
        P(),
        P(),
        P(),
        P(),
        P(),
    )
    paired = mesh.shape["seq"] == 4 and mesh.shape["dp"] == 8
    return jax.shard_map(
        fast if paired else general,
        mesh=mesh,
        in_specs=placed,
        out_specs=(
            P(("dp", "seq"), None),
            P(("dp", "seq"), None),
            P("dp", "seq"),
            P("dp", "seq"),
            P("dp", "seq"),
            P("dp", "seq"),
            P("dp", "seq"),
            P(),
            P(),
            P(),
            P(),
        ),
        check_vma=False,
    )
```

```python
import functools
import math

import jax
import jax.numpy as jnp
import numpy as np
from jax import lax
from jax.experimental import pallas as pl
from jax.experimental.pallas import tpu as pltpu
from jax.sharding import PartitionSpec as P

HEAD = 64


norm_eps = 1e-05
rotary_base = 1000.0
masked_value = -1e30


def doc_layout(lengths_row, count):
    ends = jnp.cumsum(lengths_row)
    place = jnp.arange(count, dtype=jnp.int32)
    after = (place[:, None] >= ends[None, :]).astype(jnp.int32)
    segment = jnp.sum(after, axis=1)
    start = jnp.sum(after * lengths_row[None, :], axis=1)
    return (segment, place - start)


def rotate(field, position):
    half = field.shape[-1] // 2
    freq = rotary_base ** (-jnp.arange(half, dtype=jnp.float32) * (2.0 / field.shape[-1]))
    angle = position.astype(jnp.float32)[:, None] * freq[None, :]
    cosine = jnp.cos(angle)[:, None, :]
    sine = jnp.sin(angle)[:, None, :]
    first = field[..., :half]
    second = field[..., half:]
    return jnp.concatenate(
        [first * cosine - second * sine, second * cosine + first * sine], axis=-1
    )


def norm_forward(value, gain, shift):
    mean = jnp.mean(value, axis=-1, keepdims=True)
    centred = value - mean
    inverse = lax.rsqrt(jnp.mean(centred * centred, axis=-1, keepdims=True) + norm_eps)
    scaled = centred * inverse
    return (scaled * gain + shift, scaled, inverse)


def norm_backward(grad, scaled, inverse, gain):
    inner = grad * gain
    back = inverse * (
        inner
        - jnp.mean(inner, axis=-1, keepdims=True)
        - scaled * jnp.mean(inner * scaled, axis=-1, keepdims=True)
    )
    return (back, jnp.sum(grad * scaled, axis=0), jnp.sum(grad, axis=0))


def inner_rows(left, right):
    return lax.dot_general(
        left, right, (((0,), (0,)), ((), ())), preferred_element_type=jnp.float32
    )


def times_transpose(left, right):
    return lax.dot_general(
        left, right, (((1,), (1,)), ((), ())), preferred_element_type=jnp.float32
    )


def general(
    tokens,
    cotangent,
    lengths,
    input_weight,
    output_weight,
    gate_weight,
    up_weight,
    down_weight,
    gain_one,
    bias_one,
    gain_two,
    bias_two,
):
    rows, width = tokens.shape
    heads = width // HEAD
    window = rows * lax.axis_size("seq")
    scale = 1.0 / math.sqrt(HEAD)
    segment_all, position_all = doc_layout(lengths[0], window)
    offset = lax.axis_index("seq") * rows
    seg_mine = lax.dynamic_slice_in_dim(segment_all, offset, rows)
    pos_mine = lax.dynamic_slice_in_dim(position_all, offset, rows)
    projected = jnp.dot(tokens, input_weight, preferred_element_type=jnp.float32)
    query = rotate(projected[:, :width].reshape(rows, heads, HEAD), pos_mine).astype(jnp.bfloat16)
    key = (
        rotate(projected[:, width : 2 * width].reshape(rows, heads, HEAD), pos_mine)
        .astype(jnp.bfloat16)
        .reshape(rows, width)
    )
    value = projected[:, 2 * width :].astype(jnp.bfloat16)

    def scores_for(key_block, seg_block):
        scores = (
            jnp.einsum("qhe,khe->hqk", query, key_block, preferred_element_type=jnp.float32) * scale
        )
        same = (seg_mine[:, None] == seg_block[None, :])[None]
        return (jnp.where(same, scores, masked_value), same)

    def split_blocks(piece, segs):
        count = piece[0].shape[0]
        size = math.gcd(count, 512)
        keys = piece[0].reshape(count // size, size, heads, HEAD)
        values = piece[1].reshape(count // size, size, heads, HEAD)
        return (keys, values, segs.reshape(count // size, size), count, size)

    start_state = (
        jnp.zeros((rows, heads, HEAD), jnp.float32),
        jnp.full((heads, rows), masked_value, jnp.float32),
        jnp.zeros((heads, rows), jnp.float32),
    )
    segs = segment_all
    keys, values, seg_blocks, count, size = split_blocks(
        (
            lax.all_gather(key, "seq", axis=0, tiled=True),
            lax.all_gather(value, "seq", axis=0, tiled=True),
        ),
        segs,
    )

    def forward_step(state, item):
        summed, peak, total = state
        key_block, value_block, seg_block = item
        scores, same = scores_for(key_block, seg_block)
        new_peak = jnp.maximum(peak, jnp.max(scores, axis=-1))
        fade = jnp.exp(peak - new_peak)
        weight = jnp.where(same, jnp.exp(scores - new_peak[..., None]), 0.0)
        total = total * fade + jnp.sum(weight, axis=-1)
        summed = summed * fade.T[..., None] + jnp.einsum(
            "hqk,khe->qhe",
            weight.astype(jnp.bfloat16),
            value_block,
            preferred_element_type=jnp.float32,
        )
        return ((summed, new_peak, total), None)

    state, unused = lax.scan(forward_step, start_state, (keys, values, seg_blocks))
    summed, peak, total = state
    attended = (summed / total.T[..., None]).reshape(rows, width)
    attended_low = attended.astype(jnp.bfloat16)
    first = tokens.astype(jnp.float32) + jnp.dot(
        attended_low, output_weight, preferred_element_type=jnp.float32
    )
    normed, scaled_one, inverse_one = norm_forward(first, gain_one, bias_one)
    normed_low = normed.astype(jnp.bfloat16)
    gate = jnp.dot(normed_low, gate_weight, preferred_element_type=jnp.float32)
    upward = jnp.dot(normed_low, up_weight, preferred_element_type=jnp.float32)
    sigma = jax.nn.sigmoid(gate)
    activated = gate * sigma
    hidden_low = (activated * upward).astype(jnp.bfloat16)
    second = normed + jnp.dot(hidden_low, down_weight, preferred_element_type=jnp.float32)
    result, scaled_two, inverse_two = norm_forward(second, gain_two, bias_two)
    grad_second, grad_gain_two, grad_bias_two = norm_backward(
        cotangent.astype(jnp.float32), scaled_two, inverse_two, gain_two
    )
    grad_ff_low = grad_second.astype(jnp.bfloat16)
    grad_hidden = times_transpose(grad_ff_low, down_weight)
    grad_gate_low = (grad_hidden * upward * (sigma * (1.0 + gate * (1.0 - sigma)))).astype(
        jnp.bfloat16
    )
    grad_up_low = (grad_hidden * activated).astype(jnp.bfloat16)
    grad_normed = (
        grad_second
        + times_transpose(grad_gate_low, gate_weight)
        + times_transpose(grad_up_low, up_weight)
    )
    grad_first, grad_gain_one, grad_bias_one = norm_backward(
        grad_normed, scaled_one, inverse_one, gain_one
    )
    grad_branch_low = grad_first.astype(jnp.bfloat16)
    grad_attended_low = times_transpose(grad_branch_low, output_weight).astype(jnp.bfloat16)
    grad_heads = grad_attended_low.reshape(rows, heads, HEAD)
    delta = jnp.sum(
        (grad_attended_low.astype(jnp.float32) * attended).reshape(rows, heads, HEAD), axis=-1
    ).T
    zero_query = jnp.zeros((rows, heads, HEAD), jnp.float32)
    grad_acc = zero_query
    segs = segment_all
    grad_query = grad_acc
    keys, values, seg_blocks, count, size = split_blocks(
        (
            lax.all_gather(key, "seq", axis=0, tiled=True),
            lax.all_gather(value, "seq", axis=0, tiled=True),
        ),
        segs,
    )

    def backward_step(grad_acc, item):
        key_block, value_block, seg_block = item
        scores, same = scores_for(key_block, seg_block)
        prob = jnp.where(same, jnp.exp(scores - peak[..., None]) / total[..., None], 0.0)
        prob_grad = jnp.einsum(
            "qhe,khe->hqk", grad_heads, value_block, preferred_element_type=jnp.float32
        )
        score_grad = (prob * (prob_grad - delta[..., None])).astype(jnp.bfloat16)
        grad_acc = (
            grad_acc
            + jnp.einsum("hqk,khe->qhe", score_grad, key_block, preferred_element_type=jnp.float32)
            * scale
        )
        prob_low = prob.astype(jnp.bfloat16)
        key_grad = (
            jnp.einsum("hqk,qhe->khe", score_grad, query, preferred_element_type=jnp.float32)
            * scale
        )
        value_grad = jnp.einsum(
            "hqk,qhe->khe", prob_low, grad_heads, preferred_element_type=jnp.float32
        )
        return (grad_acc, (key_grad.reshape(size, width), value_grad.reshape(size, width)))

    grad_query, outputs = lax.scan(backward_step, grad_query, (keys, values, seg_blocks))
    grad_acc = grad_query
    key_part = outputs[0].reshape(count, width)
    value_part = outputs[1].reshape(count, width)
    grad_key, grad_value = (
        lax.psum_scatter(
            key_part.astype(jnp.bfloat16), "seq", scatter_dimension=0, tiled=True
        ).astype(jnp.float32),
        lax.psum_scatter(
            value_part.astype(jnp.bfloat16), "seq", scatter_dimension=0, tiled=True
        ).astype(jnp.float32),
    )
    query_back = rotate(grad_acc, -pos_mine).reshape(rows, width)
    key_back = rotate(grad_key.reshape(rows, heads, HEAD), -pos_mine).reshape(rows, width)
    grad_projected_low = jnp.concatenate([query_back, key_back, grad_value], axis=1).astype(
        jnp.bfloat16
    )
    grad_tokens = (grad_first + times_transpose(grad_projected_low, input_weight)).astype(
        jnp.bfloat16
    )
    column_grads = (
        lax.all_to_all(grad_projected_low, "seq", split_axis=1, concat_axis=0, tiled=True),
        lax.all_to_all(grad_branch_low, "seq", split_axis=1, concat_axis=0, tiled=True),
        lax.all_to_all(grad_gate_low, "seq", split_axis=1, concat_axis=0, tiled=True),
        lax.all_to_all(grad_up_low, "seq", split_axis=1, concat_axis=0, tiled=True),
        lax.all_to_all(grad_ff_low, "seq", split_axis=1, concat_axis=0, tiled=True),
    )
    tok_rows = lax.all_gather(tokens, "seq", axis=0, tiled=True)
    normed_rows = lax.all_gather(normed_low, "seq", axis=0, tiled=True)
    attended_rows = lax.all_gather(attended_low, "seq", axis=0, tiled=True)
    hidden_rows = lax.all_gather(hidden_low, "seq", axis=0, tiled=True)
    count = tok_rows.shape[0]
    cols = [member for member in column_grads]
    summed_grads = (
        lax.psum_scatter(
            inner_rows(tok_rows, cols[0]).astype(jnp.bfloat16),
            "dp",
            scatter_dimension=0,
            tiled=True,
        ).astype(jnp.float32),
        lax.psum_scatter(
            inner_rows(attended_rows, cols[1]).astype(jnp.bfloat16),
            "dp",
            scatter_dimension=0,
            tiled=True,
        ).astype(jnp.float32),
        lax.psum_scatter(
            inner_rows(normed_rows, cols[2]).astype(jnp.bfloat16),
            "dp",
            scatter_dimension=0,
            tiled=True,
        ).astype(jnp.float32),
        lax.psum_scatter(
            inner_rows(normed_rows, cols[3]).astype(jnp.bfloat16),
            "dp",
            scatter_dimension=0,
            tiled=True,
        ).astype(jnp.float32),
        lax.psum_scatter(
            inner_rows(hidden_rows, cols[4]).astype(jnp.bfloat16),
            "dp",
            scatter_dimension=0,
            tiled=True,
        ).astype(jnp.float32),
    )
    norm_grads = lax.psum(
        (grad_gain_one, grad_bias_one, grad_gain_two, grad_bias_two), ("dp", "seq")
    )
    return (
        result.astype(jnp.bfloat16),
        grad_tokens,
        summed_grads[0],
        summed_grads[1],
        summed_grads[2],
        summed_grads[3],
        summed_grads[4],
        norm_grads[0],
        norm_grads[1],
        norm_grads[2],
        norm_grads[3],
    )


low = jnp.bfloat16
full = jnp.float32
TILE = 128
MIB = 1024 * 1024


def nn(left, right):
    return lax.dot_general(
        left, right, (((1,), (0,)), ((), ())), preferred_element_type=jnp.float32
    )


def nt(left, right):
    return lax.dot_general(
        left, right, (((1,), (1,)), ((), ())), preferred_element_type=jnp.float32
    )


def tn(left, right):
    return lax.dot_general(
        left, right, (((0,), (0,)), ((), ())), preferred_element_type=jnp.float32
    )


def block(shape, *at):
    at = at or (0,) * len(shape)

    def index(*args):
        return tuple(a(*args[1:]) if callable(a) else a for a in at)

    return pl.BlockSpec(tuple(shape), index)


def shaped(shape, kind):
    return jax.ShapeDtypeStruct(tuple(shape), kind)


SEQ, SIDE, X, LOW, HIGH, PAIR, LONE, OTHER_PAIR, OTHER_LONE, OWN, OTHER, CORE = range(12)

COST = {
    "tables": 1.5, "first_half": 6.9, "second_half": 7.9, "feed_forward": 8.4, "feed_back": 8.6,
    "project_heads": 4, "back_one": 6.5, "back_rest": 7, "column_start": 4, "column_grads": 6, "token_grad": 3,
    "out_grad": 1.2,
}


def took(name):
    return pl.CostEstimate(flops=int(COST.get(name, 0.5) * 10**9), bytes_accessed=1, transcendentals=0)


def still(value):
    return pltpu.with_memory_space_constraint(value, pltpu.HBM)


def call(body, name, scalars, operands, results, scratch=(), mib=16):
    return pl.pallas_call(
        body,
        grid_spec=pltpu.PrefetchScalarGridSpec(
            num_scalar_prefetch=1,
            grid=(1,),
            in_specs=[spec for unused, spec in operands],
            out_specs=[spec for unused, spec in results],
            scratch_shapes=list(scratch),
        ),
        out_shape=[shape for shape, unused in results],
        compiler_params=pltpu.CompilerParams(
            vmem_limit_bytes=mib * MIB, dimension_semantics=("arbitrary",)
        ),
        cost_estimate=took(name),
        name=name,
    )(scalars, *[value for value, unused in operands])


def whole(value):
    return (value, block(value.shape))


def turn(field, cosine, sine):
    lane = lax.broadcasted_iota(jnp.int32, field.shape, 1)
    half = HEAD // 2
    other = jnp.where(
        lane % HEAD < half, pltpu.roll(field, TILE - half, 1), pltpu.roll(field, half, 1)
    )
    return field * cosine + other * sine


def one_head(pair, which):
    lane = lax.broadcasted_iota(jnp.int32, pair.shape, 1)
    return jnp.where((lane // HEAD) == which, pair, jnp.zeros_like(pair))


def rows_at(index, count):
    return pl.ds(pl.multiple_of(index * count, count), count)


def pack(sums):
    high = sums.astype(low)
    return jnp.concatenate([high, (sums - high.astype(jnp.float32)).astype(low)], axis=0)


def unpack(packed):
    wide = packed.astype(jnp.float32)
    return wide[:8] + wide[8:]


def tables(place, lengths, freq, cosine, sine, seg_col, seg_row):
    count = cosine.shape[0]
    rows = count // 4
    lane = lax.broadcasted_iota(jnp.int32, (8, count), 1)
    index = jnp.zeros_like(lane)
    for i in range(1, 4):
        index = index + (lane >= i * rows).astype(jnp.int32)
    spot = (index ^ place[SEQ]) * rows + (lane - index * rows)
    end = jnp.int32(0)
    segment = jnp.zeros_like(lane)
    start = jnp.zeros_like(lane)
    for i in range(lengths.shape[1]):
        length = lengths[0, i]
        end = end + length
        past = (spot >= end).astype(jnp.int32)
        segment = segment + past
        start = start + past * length
    position = (spot - start).astype(jnp.float32)
    angle = freq[:, :1] * position[:1]
    c, s = jnp.cos(angle), jnp.sin(angle)
    cosine[...] = jnp.concatenate([c] * 4, axis=0).T
    sine[...] = jnp.concatenate([-s, s] * 2, axis=0).T
    seg_row[...] = segment
    wide = jnp.broadcast_to(segment[:1].astype(jnp.float32), (TILE, count))
    seg_col[...] = wide.T.astype(jnp.int32)


def put_keys(tokens, wk, wv, cosine, sine, keys, values, start):
    rows = tokens.shape[0]
    projected = nn(tokens, wk)
    for tile in range(projected.shape[1] // TILE):
        cols = slice(tile * TILE, (tile + 1) * TILE)
        keys[start : start + rows, cols] = turn(projected[:, cols], cosine, sine).astype(low)
    values[start : start + rows, :] = nn(tokens, wv).astype(low)


def put_query(tokens, wq, cosine, sine, query):
    scale = 1.0 / math.sqrt(HEAD)
    projected = nn(tokens, wq)
    for tile in range(projected.shape[1] // TILE):
        cols = slice(tile * TILE, (tile + 1) * TILE)
        turned = turn(projected[:, cols], cosine, sine)
        query[:, cols] = (turned.astype(low) * scale).astype(low)


def attend(query, keys, values, bias, take):
    @pl.loop(0, query.shape[1] // TILE, unroll=6)
    def _(tile):
        cols = rows_at(tile, TILE)
        key_pair = keys[:, cols]
        value_pair = values[:, cols]
        query_pair = query[:, cols]
        for which in range(TILE // HEAD):
            scores = nt(key_pair, one_head(query_pair, which)) + bias[...]
            peak = jnp.max(scores, axis=0, keepdims=True)
            weight = jnp.exp(scores - peak)
            total = jnp.sum(weight, axis=0, keepdims=True)
            out = tn(value_pair, weight.astype(low))[which * HEAD : (which + 1) * HEAD]
            take(tile * (TILE // HEAD) + which, out, peak, total)


def first_half(
    place, own, near, wq, wk, wv, cosine, sine, seg_key, seg_query, query, acc, peaks, totals,
    keys, values, bias,
):
    rows = own.shape[0]
    put_query(own[...], wq[...], cosine[:rows, :], sine[:rows, :], query)
    put_keys(own[...], wk[...], wv[...], cosine[:rows, :], sine[:rows, :], keys, values, 0)
    put_keys(near[...], wk[...], wv[...], cosine[rows:, :], sine[rows:, :], keys, values, rows)
    bias[...] = jnp.where(seg_key[:, :1] == seg_query[:1, :], 0.0, masked_value)

    def take(head, out, peak, total):
        acc[rows_at(head, HEAD), :] = out
        peaks[pl.ds(head, 1), :] = peak
        totals[pl.ds(head, 1), :] = total

    attend(query, keys, values, bias, take)


def second_half(
    place, own, far, far_near, wk, wv, wo, cosine, sine, seg_key, seg_query, query, acc, peaks, totals,
    gain, shift, far_wq, attended_low, normed, normed_low, scaled, inverse, keys, values, far_query, logs, bias,
    turned,
):
    rows, width = own.shape
    put_keys(far[...], wk[...], wv[...], cosine[:rows, :], sine[:rows, :], keys, values, 0)
    put_keys(far_near[...], wk[...], wv[...], cosine[rows:, :], sine[rows:, :], keys, values, rows)
    bias[...] = jnp.where(seg_key[:, :1] == seg_query[:1, :], 0.0, masked_value)
    put_query(far[...], far_wq[...], cosine[:rows, :], sine[:rows, :], far_query)
    side_heads = width // HEAD // 2
    logs[...] = jnp.zeros_like(logs)

    def take(head, out, peak, total):
        part = rows_at(head, HEAD)
        before = peaks[pl.ds(head, 1), :]
        best = jnp.maximum(before, peak)
        fade = jnp.exp(before - best)
        grow = jnp.exp(peak - best)
        whole_total = totals[pl.ds(head, 1), :] * fade + total * grow
        logs[pl.ds(head + jnp.where(head >= side_heads, 8 - side_heads, 0), 1), :] = best + jnp.log(whole_total)
        inverse_total = 1.0 / whole_total
        turned[part, :] = acc[part, :] * (fade * inverse_total) + out * (grow * inverse_total)

    attend(query, keys, values, bias, take)
    attended = turned[...].T.astype(low)
    attended_low[...] = attended
    first = own[...].astype(jnp.float32) + nn(attended, wo[...])
    mean = jnp.mean(first, axis=1, keepdims=True)
    centred = first - mean
    spread = lax.rsqrt(jnp.mean(centred * centred, axis=1, keepdims=True) + norm_eps)
    unit = centred * spread
    value = unit * gain[...][None, :] + shift[...][None, :]
    scaled[...] = unit
    inverse[...] = jnp.broadcast_to(spread, (rows, TILE))
    normed[...] = value
    normed_low[...] = value.astype(low)


def halves(place, by_side, by_low, first, second):
    half = first.shape[0]
    first[...] = by_side[:half, :]
    second[...] = by_low[half:, :]


def feed_forward(
    normed, normed_low, wg, wu, wd, cotangent, gain, shift,
    slope_up, slope_gate, result, grad_second, grad_low, sums, acc,
):
    chunk = wg.shape[1] // 4
    acc[...] = normed[...]

    @pl.loop(0, 4, unroll=4)
    def _(step):
        cols = rows_at(step, chunk)
        gate = nn(normed_low[...], wg[:, cols])
        upward = nn(normed_low[...], wu[:, cols])
        sigma = jax.nn.sigmoid(gate)
        active = gate * sigma
        slope_up[:, cols] = active.astype(low)
        slope_gate[:, cols] = (upward * (sigma * (1.0 + gate * (1.0 - sigma)))).astype(low)
        acc[...] += nn((active * upward).astype(low), wd[cols, :])

    if True:
        second = acc[...]
        mean = jnp.mean(second, axis=1, keepdims=True)
        centred = second - mean
        spread = lax.rsqrt(jnp.mean(centred * centred, axis=1, keepdims=True) + norm_eps)
        unit = centred * spread
        result[...] = (unit * gain[...][None, :] + shift[...][None, :]).astype(low)
        grad = cotangent[...].astype(jnp.float32)
        inner = grad * gain[...][None, :]
        back = spread * (
            inner
            - jnp.mean(inner, axis=1, keepdims=True)
            - unit * jnp.mean(inner * unit, axis=1, keepdims=True)
        )
        grad_second[...] = back
        grad_low[...] = back.astype(low)
        sums[0:1, :] = jnp.sum(grad * unit, axis=0, keepdims=True)
        sums[1:2, :] = jnp.sum(grad, axis=0, keepdims=True)


def feed_back(
    place, grad_second, grad_low, slope_up, slope_gate, wg, wu, wd, wo, scaled, inverse, gain, sums_two,
    attended_low, logs, grad_first, branch_low, mine, other, sums, stats, acc,
):
    chunk = wg.shape[1] // 4
    acc[...] = grad_second[...]

    @pl.loop(0, 4, unroll=4)
    def _(step):
        cols = rows_at(step, chunk)
        hidden = nt(grad_low[...], wd[cols, :])
        gate = (hidden * slope_gate[:, cols].astype(jnp.float32)).astype(low)
        upward = (hidden * slope_up[:, cols].astype(jnp.float32)).astype(low)
        acc[...] += nt(gate, wg[:, cols]) + nt(upward, wu[:, cols])

    if True:
        grad = acc[...]
        unit = scaled[...]
        inner = grad * gain[...][None, :]
        back = inverse[:, :1] * (
            inner
            - jnp.mean(inner, axis=1, keepdims=True)
            - unit * jnp.mean(inner * unit, axis=1, keepdims=True)
        )
        grad_first[...] = back
        branch_low[...] = back.astype(low)
        attended_grad = nt(branch_low[...], wo[...]).astype(low)
        group = mine.shape[1]
        height = mine.shape[0]
        left, right = attended_grad[:, :group], attended_grad[:, group:]
        second_side = place[SIDE] > 0
        mine[...] = jnp.where(second_side, right, left)
        other[:height, :] = jnp.where(second_side, left, right)
        sums[...] = jnp.zeros_like(sums)
        sums[0:1, :] = jnp.sum(grad * unit, axis=0, keepdims=True)
        sums[1:2, :] = jnp.sum(grad, axis=0, keepdims=True)
        sums[2:4, :] = sums_two[...]
        for i in range(2):
            part = slice(height + i * 16, height + (i + 1) * 16)
            other[part, :] = pack(sums[:, i * group : (i + 1) * group])
        product = attended_grad.astype(jnp.float32) * attended_low[...].astype(jnp.float32)
        high = product.astype(low)
        rest = (product - high.astype(jnp.float32)).astype(low)
        row = lax.broadcasted_iota(jnp.int32, (16, 2 * group), 0)
        lane = lax.broadcasted_iota(jnp.int32, (16, 2 * group), 1)
        head = lane // HEAD
        ones = (row == head + jnp.where(lane >= group, 8 - group // HEAD, 0)).astype(low)
        deltas = nt(ones, high) + nt(ones, rest)
        left, right = (
            jnp.concatenate([logs[part, :], deltas[part, :]], axis=0) for part in (slice(0, 8), slice(8, 16))
        )
        stats[...] = jnp.where(second_side, right, left)
        rest = jnp.where(second_side, left, right)
        other[height + 32 :, height:] = jnp.zeros((48, group - height), low)
        for i in range(3):
            part = slice(height + 32 + i * 16, height + 48 + i * 16)
            piece = rest.astype(low)
            other[part, :height] = piece
            rest = rest - piece.astype(jnp.float32)


def out_grad(place, branch_low, attended_low, keep, send, turned):
    turned[...] = tn(branch_low[...], attended_low[...])
    quarter = turned.shape[0] // 4
    core = place[CORE]
    for i in range(2):
        to = slice(i * quarter, (i + 1) * quarter)
        keep[to, :] = turned[rows_at(2 * i + core, quarter), :]
        send[to, :] = turned[rows_at(2 * i + 1 - core, quarter), :].astype(low)


def out_halve(place, keep, got, kept, send):
    quarter = keep.shape[0] // 2
    mine, other = rows_at(place[SIDE], quarter), rows_at(1 - place[SIDE], quarter)
    kept[...] = keep[mine, :] + got[mine, :].astype(jnp.float32)
    send[...] = (keep[other, :] + got[other, :].astype(jnp.float32)).astype(low)


def back_tile(key_pair, value_pair, query_pair, grad_pair, bias, logs, deltas):
    scale = 1.0 / math.sqrt(HEAD)
    grad_key = None
    grad_value = None
    pieces = []
    for which in range(TILE // HEAD):
        query_head = one_head(query_pair, which)
        grad_head = one_head(grad_pair, which)
        scores = nt(key_pair, query_head) + bias[...]
        prob = jnp.exp(scores - logs[which])
        prob_grad = nt(value_pair, grad_head)
        score_grad = (prob * (prob_grad - deltas[which])).astype(low)
        value_part = nn(prob.astype(low), grad_head)
        key_part = nn(score_grad, query_head)
        grad_key = key_part if grad_key is None else grad_key + key_part
        grad_value = value_part if grad_value is None else grad_value + value_part
        pieces.append(tn(key_pair, score_grad)[which * HEAD : (which + 1) * HEAD])
    return jnp.concatenate(pieces, axis=0).T * scale, grad_key, grad_value


def back_some(tiles, first, place, *refs):
    own, near, far, far_near = refs[:4]
    pairs = [refs[i : i + 2] for i in range(4, 12, 2)]
    cosine, sine, seg_key, seg_query, stats = refs[12:17]
    far_grad = refs[11]
    rows = own.shape[0]
    blocks = (own, near, far, far_near)
    if first:
        dq, both, grads, bias = refs[17:]
    else:
        before = refs[17:23]
        dq, even, odd_near, odd_far, grads, bias, both = refs[23:]
    group = pairs[0][0].shape[1]
    for index in range(2):
        part = slice(2 * index * rows, (2 * index + 1) * rows)
        to = slice(index * rows, (index + 1) * rows)
        bias[:, to] = jnp.where(seg_key[:, :1] == seg_query[:1, part], 0.0, masked_value)
    far_stats = sum(
        far_grad[rows + 32 + i * 16 : rows + 48 + i * 16, :rows].astype(jnp.float32) for i in range(3)
    )
    both_stats = jnp.concatenate([stats[...], far_stats], axis=1)
    for tile in tiles:
        cols = slice(tile * TILE, (tile + 1) * TILE)
        heads = [tile * (TILE // HEAD) + which for which in range(TILE // HEAD)]
        logs = [both_stats[head : head + 1] for head in heads]
        deltas = [both_stats[8 + head : 9 + head] for head in heads]
        keys, values, queries, outs = (
            jnp.concatenate([one[:, cols], two[: one.shape[0], cols]], axis=0) for one, two in pairs
        )
        grad_query, grad_key, grad_value = back_tile(
            keys, values, queries, outs, bias, logs, deltas
        )
        to = slice(0, TILE) if first else cols
        shifted = slice(TILE, 2 * TILE) if first else slice(group + tile * TILE, group + (tile + 1) * TILE)
        for index in range(2):
            part = slice(index * rows, (index + 1) * rows)
            at = slice(2 * index * rows, (2 * index + 1) * rows)
            dq[part, to] = turn(grad_query[part], cosine[at, :], -sine[at, :]).astype(low)
        both[:, to] = turn(grad_key, cosine[...], -sine[...]).astype(low)
        both[:, shifted] = grad_value.astype(low)
        pair = jnp.concatenate([both[:, to], both[:, shifted]], axis=1)
        total = None
        for index in range(4):
            part = slice(index * rows, (index + 1) * rows)
            product = tn(pair[part], blocks[index][...])
            total = product if total is None else total + product
        query_rows = tn(dq[:rows, to], own[...]) + tn(dq[rows:, to], far[...])
        if first:
            grads[:TILE, :] = query_rows
            grads[TILE:, :] = total
        else:
            grads[tile * TILE : (tile + 1) * TILE, :] = query_rows
            for kind in range(2):
                at = (kind + 1) * group + tile * TILE
                grads[at : at + TILE, :] = total[kind * TILE : (kind + 1) * TILE]
    if first:
        return
    for tile in range(2):
        dq_before, both_before, grads_before = before[3 * tile : 3 * tile + 3]
        dq[:, tile * TILE : (tile + 1) * TILE] = dq_before[...]
        for kind in range(3):
            at = kind * group + tile * TILE
            if kind < 2:
                both[:, at : at + TILE] = both_before[:, kind * TILE : (kind + 1) * TILE]
            grads[at : at + TILE, :] = grads_before[kind * TILE : (kind + 1) * TILE, :]
    for index in range(4):
        part = slice(index * rows, (index + 1) * rows)
        if index % 2:
            (odd_far if index > 1 else odd_near)[...] = both[part, :]
        else:
            even[index // 2 * rows : (index // 2 + 1) * rows, :] = both[part, :]


def fold(place, grads, far_grad, sums, odd_near, odd_far, keep, send, near_send, far_send, kept_sums):
    quarter = keep.shape[0] // 3
    pair, lone, other_pair, other_lone = (place[i] for i in (PAIR, LONE, OTHER_PAIR, OTHER_LONE))
    for i in range(3):
        to = slice(i * quarter, (i + 1) * quarter)
        keep[to, :] = grads[rows_at(pair + i if i < 2 else lone, quarter), :]
        send[to, :] = grads[rows_at(other_pair + i if i < 2 else other_lone, quarter), :].astype(low)
    rows = odd_near.shape[0]
    got = jnp.concatenate(
        [unpack(far_grad[rows : rows + 16, :]), unpack(far_grad[rows + 16 : rows + 32, :])], axis=1
    )
    total = sums[...] + got
    kept_sums[...] = total
    send[3 * quarter :, :] = pack(total)
    near_send[...] = odd_near[...]
    far_send[...] = odd_far[...]


def turn_over(place, keep, got, out_keep, out_got, sums, kept, send, kept_sums, turned):
    height = keep.shape[0]
    turned[:, :height] = (keep[...] + got[:height, :].astype(jnp.float32)).T
    turned[:, height:] = (out_keep[...] + out_got[...].astype(jnp.float32)).T
    bit = place[LOW]
    part = turned.shape[0] // 8
    for i in range(4):
        to = slice(i * part, (i + 1) * part)
        at = 4 * (i // 2) + i % 2
        kept[to, :] = turned[rows_at(at + 2 * bit, part), :]
        send[to, :] = turned[rows_at(at + 2 * (1 - bit), part), :].astype(low)
    both = sums[...] + unpack(got[height:, :])
    kept_sums[...] = both
    send[4 * part :, :] = pack(both)


def halve_x(place, keep, got, sums, kept, send, kept_sums):
    bit = place[X]
    part = keep.shape[0] // 4
    for i in range(2):
        to = slice(i * part, (i + 1) * part)
        for at, out in ((bit, kept), (1 - bit, send)):
            there = rows_at(2 * i + at, part)
            out[to, :] = (keep[there, :] + got[there, :].astype(jnp.float32)).astype(out.dtype)
    both = sums[...] + unpack(got[4 * part :, :])
    kept_sums[...] = both
    send[2 * part :, :] = pack(both)


def halve(place, keep, got, sums, kept, send, kept_sums):
    bit = place[HIGH]
    height = keep.shape[0]
    part = height // 2
    mine, other = rows_at(bit, part), rows_at(1 - bit, part)
    kept[...] = keep[mine, :] + got[mine, :].astype(jnp.float32)
    send[:part, :] = (keep[other, :] + got[other, :].astype(jnp.float32)).astype(low)
    both = sums[...] + unpack(got[height:, :])
    kept_sums[...] = both
    send[part:, :] = pack(both)


def last_sum(place, keep, got, sums, own, send, out, *vectors):
    height = keep.shape[0]
    total = keep[...] + got[:height, :].astype(jnp.float32)
    quarter = out.shape[1]
    own[...] = total[:, : 2 * quarter]
    send[...] = total[:, 2 * quarter : 3 * quarter].astype(low)
    out[...] = total[:, 3 * quarter :]
    both = sums[...] + unpack(got[height:, :])
    for i, vector in enumerate(vectors):
        vector[...] = both[i]


def turn_weights(wg, wu, wgu):
    half = wg.shape[1]
    wgu[:half, :] = wg[...].astype(jnp.float32).T.astype(low)
    wgu[half:, :] = wu[...].astype(jnp.float32).T.astype(low)


def hidden_parts(wgu, rows):
    both = nt(wgu, rows)
    half = both.shape[0] // 2
    gate, upward = both[:half], both[half:]
    sigma = jax.nn.sigmoid(gate)
    active = gate * sigma
    slope = upward * (sigma * (1.0 + gate * (1.0 - sigma)))
    return (active * upward).astype(low), active, slope


def column_start(place, own, by_side, by_low, wg, wu, hidden, active, slope, wgu):
    turn_weights(wg, wu, wgu)
    rows = jnp.concatenate([own[...], by_side[...], by_low[...]], axis=0)
    values = hidden_parts(wgu[...], rows)
    for value, out in zip(values, (hidden, active, slope)):
        out[...] = value.astype(low)


def column_grads(last, place, *refs):
    count = 5
    rows_refs, back_refs = refs[:count], refs[count : 2 * count]
    rows = jnp.concatenate([v[...] for v in rows_refs], axis=0)
    back = jnp.concatenate([v[...] for v in back_refs], axis=0)
    rest = refs[2 * count :]
    if last:
        wg, wu, wd = rest[:3]
        earlier = (rest[3], rest[-1])
        outs, wgu, acc = rest[4:8], rest[8], rest[9]
        turn_weights(wg, wu, wgu)
        hidden, active, slope = hidden_parts(wgu[...], rows)
    else:
        wgu, wd = rest[:2]
        outs, acc = rest[5:6], rest[6]
        late = hidden_parts(wgu[...], rows[-2 * rows_refs[-1].shape[0] :])
        hidden, active, slope = (
            jnp.concatenate([begun[...], value.astype(low)], axis=1) for begun, value in zip(rest[2:5], late)
        )
    half, width = wd.shape
    grad_hidden = nt(wd[...], back)
    grad_gate = (grad_hidden * slope.astype(jnp.float32)).astype(low)
    grad_up = (grad_hidden * active.astype(jnp.float32)).astype(low)
    for i, product in enumerate((nn(grad_gate, rows), nn(grad_up, rows), nn(hidden, back))):
        acc[i * half : (i + 1) * half, :] = product
    if last:
        got, total = earlier
        bit = place[X]
        for i in range(3):
            part = slice(i * half, (i + 1) * half)
            total[...] = acc[part, :].T + got[:, part].astype(jnp.float32)
            keep, send, to_cols = (outs[0], outs[2], part) if i < 2 else (outs[1], outs[3], slice(None))
            count = 4 if i < 2 else 2
            cut = width // (2 * count)
            for j in range(count):
                to = slice(j * cut, (j + 1) * cut)
                keep[to, to_cols] = total[rows_at(2 * j + bit, cut), :]
                send[to, to_cols] = total[rows_at(2 * j + 1 - bit, cut), :].astype(low)
    else:
        for i in range(3):
            part = slice(i * half, (i + 1) * half)
            outs[0][:, part] = acc[part, :].T.astype(low)


def second_split(place, keep, got, kept, send):
    bit = place[HIGH]
    part = keep.shape[0] // 2
    mine, other = rows_at(bit, part), rows_at(1 - bit, part)
    kept[...] = keep[mine, :] + got[mine, :].astype(jnp.float32)
    send[...] = (keep[other, :] + got[other, :].astype(jnp.float32)).astype(low)


def pair_sum(place, keep, got, kept, send):
    part = kept.shape[0]
    mine, other = rows_at(place[LOW], part), rows_at(1 - place[LOW], part)
    kept[...] = keep[mine, :] + got[mine, :].astype(jnp.float32)
    send[...] = (keep[other, :] + got[other, :].astype(jnp.float32)).astype(low)


def down_sum(place, keep, got, out):
    out[...] = (keep[...] + got[...].astype(jnp.float32)).astype(low)


def widened(place, got, out):
    out[...] = got[...].astype(jnp.float32)


def in_place(place, own, moved, out):
    got = moved[...].astype(jnp.float32)
    first = jnp.concatenate([own[...], got], axis=1)
    second = jnp.concatenate([got, own[...]], axis=1)
    out[...] = jnp.where(place[CORE] == 0, first, second)


def pair_place(place, kept, got, gate, upward):
    half = kept.shape[1] // 2
    for i, out in enumerate((gate, upward)):
        cols = slice(i * half, (i + 1) * half)
        out[:, rows_at(place[LOW], half)] = kept[:, cols]
        out[:, rows_at(1 - place[LOW], half)] = got[:, cols].astype(jnp.float32)


def far_pack(place, dq, even, got, out):
    rows, group = out.shape[0], dq.shape[1]
    out[:, :group] = dq[rows:, :]
    total = even[rows:, :].astype(jnp.float32) + got[...].astype(jnp.float32)
    out[:, group:] = total.astype(low)


def token_grad(place, grad_first, dq, even, got, far_part, *refs):
    weights, out = refs[:-1], refs[-1]
    rows = grad_first.shape[0]
    kind = len(weights) // 2
    total = grad_first[...]
    key_value = (
        even[:rows, :].astype(jnp.float32) + got[...].astype(jnp.float32)
    ).astype(low)
    group = dq.shape[1]
    for i in range(kind):
        cols = slice(i * group, (i + 1) * group)
        mine = dq[:rows, :] if i == 0 else key_value[:, (i - 1) * group : i * group]
        total = total + nt(mine, weights[i][...]) + nt(far_part[:, cols], weights[kind + i][...])
    out[...] = total.astype(low)


def after(value, *others):
    return lax.optimization_barrier((value,) + others)[0]


def fast(
    tokens,
    cotangent,
    lengths,
    input_weight,
    output_weight,
    gate_weight,
    up_weight,
    down_weight,
    gain_one,
    bias_one,
    gain_two,
    bias_two,
):
    rows, width = tokens.shape
    hidden = gate_weight.shape[1]
    seq = lax.axis_index("seq")
    data = lax.axis_index("dp")
    n_seq, n_data = lax.axis_size("seq"), lax.axis_size("dp")
    core, side = seq % 2, seq // 2
    bit_x, bit_low, bit_high = data % 2, (data // 2) % 2, data // 4
    pairs, lones = (0, 2, 2, 4), (4, 5, 0, 1)
    table = lambda values, i: sum(jnp.where(i == k, v, 0) for k, v in enumerate(values))
    place = jnp.stack(
        [
            jnp.asarray(v, jnp.int32)
            for v in (
                seq, side, bit_x, bit_low, bit_high,
                table(pairs, seq), table(lones, seq), table(pairs, seq ^ 1), table(lones, seq ^ 1),
                2 * seq + bit_low, 2 * (seq ^ 1) + bit_low, core,
            )
        ]
    )

    def swap(value, axis, bit):
        size = n_seq if axis == "seq" else n_data
        return lax.ppermute(value, axis, [(i, i ^ bit) for i in range(size)])

    def core_swap(value):
        return swap(value, "seq", 1)

    def side_swap(value):
        return swap(value, "seq", 2)

    def x_swap(value):
        return swap(value, "dp", 1)

    def low_swap(value):
        return swap(value, "dp", 2)

    def high_swap(value):
        return swap(value, "dp", 4)

    far = side_swap(tokens)
    near = core_swap(tokens)

    window = 4 * rows
    two = 2 * rows
    half = HEAD // 2
    freq = rotary_base ** (-jnp.arange(half, dtype=jnp.float32) * (2.0 / HEAD))
    cosine, sine, seg_col, seg_row = pl.pallas_call(
        tables,
        grid_spec=pltpu.PrefetchScalarGridSpec(
            num_scalar_prefetch=2,
            grid=(1,),
            in_specs=[block((half, TILE))],
            out_specs=[block((window, TILE))] * 3 + [block((8, window))],
        ),
        out_shape=[
            shaped((window, TILE), full), shaped((window, TILE), full),
            shaped((window, TILE), jnp.int32), shaped((8, window), jnp.int32),
        ],
        compiler_params=pltpu.CompilerParams(vmem_limit_bytes=16 * MIB),
        cost_estimate=took("tables"),
        name="tables",
    )(place, lengths, jnp.broadcast_to(freq[:, None], (half, TILE)))

    third = lambda i: (input_weight, block((width, width), 0, i))
    part = lambda v, i: (v, block((two, TILE), i, 0))
    query_row = (seg_row, block((8, rows), 0, 0))
    res = lambda shape, kind: (shaped(shape, kind), block(shape))
    query, acc, peaks, totals, near_keys, near_values = call(
        first_half, "first_half", place,
        [whole(tokens), whole(near), third(0), third(1), third(2),
         part(cosine, 0), part(sine, 0), part(seg_col, 0), query_row],
        [res((rows, width), low), res((width, rows), full), res((16, rows), full), res((16, rows), full),
         res((two, width), low), res((two, width), low)],
        [pltpu.VMEM((two, rows), full)],
        mib=22,
    )
    far_near = core_swap(after(far, peaks))
    attended_low, normed, normed_low, scaled, inverse, far_keys, far_values, far_query, logs = call(
        second_half, "second_half", place,
        [whole(tokens), whole(far), whole(far_near), third(1), third(2), whole(output_weight),
         part(cosine, 1), part(sine, 1), part(seg_col, 1), query_row,
         whole(query), whole(acc), whole(peaks), whole(totals), whole(gain_one), whole(bias_one),
         (input_weight, block((width, width // 2), 0, lambda place: place[SIDE]))],
        [res((rows, width), low), res((rows, width), full), res((rows, width), low),
         res((rows, width), full), res((rows, TILE), full), res((two, width), low),
         res((two, width), low), res((rows, width // 2), low), res((16, rows), full)],
        [pltpu.VMEM((two, rows), full), pltpu.VMEM((width, rows), full)],
        mib=22,
    )

    def spread(value):
        return [value, side_swap(value), low_swap(value)]

    normed_all = spread(normed_low)

    inside = pl.BlockSpec(memory_space=pltpu.VMEM)
    slope_up, slope_gate, result, grad_second, grad_low, sums_two = pl.pallas_call(
        feed_forward,
        grid=(1,),
        in_specs=[
            block((rows, width)), block((rows, width)), inside, inside, inside,
            block((rows, width)), block((width,)), block((width,)),
        ],
        out_specs=[
            block((rows, hidden)), block((rows, hidden)),
            block((rows, width)), block((rows, width)), block((rows, width)), block((2, width)),
        ],
        out_shape=[
            shaped((rows, hidden), low), shaped((rows, hidden), low), shaped((rows, width), low),
            shaped((rows, width), full), shaped((rows, width), low), shaped((2, width), full),
        ],
        scratch_shapes=[pltpu.VMEM((rows, width), full)],
        compiler_params=pltpu.CompilerParams(
            vmem_limit_bytes=14 * MIB, dimension_semantics=("arbitrary",)
        ),
        cost_estimate=took("feed_forward"),
        name="feed_forward",
    )(
        normed, normed_low, gate_weight, up_weight, down_weight, cotangent, gain_two, bias_two,
    )

    def pass_on(rows_there, order):
        by_side, by_low = call(
            halves, "halves", after(place, order), [whole(v) for v in rows_there[1:]],
            [res((rows // 2, width), low)] * 2,
        )
        return [low_swap(by_side), side_swap(by_low)]

    normed_all += pass_on(normed_all, grad_low)
    grad_all = spread(grad_low)
    group = width // 2
    grad_first, branch_low, mine, other, sums, stats = pl.pallas_call(
        feed_back,
        grid_spec=pltpu.PrefetchScalarGridSpec(
            num_scalar_prefetch=1,
            grid=(1,),
            in_specs=[
                block((rows, width)), block((rows, width)),
                inside, inside, inside, inside, inside, block((width, width)),
                block((rows, width)), block((rows, TILE)), block((width,)), block((2, width)), block((rows, width)),
                block((16, rows)),
            ],
            out_specs=[
                block((rows, width)), block((rows, width)), block((rows, group)), block((rows + 80, group)),
                block((8, width)), block((16, rows)),
            ],
            scratch_shapes=[pltpu.VMEM((rows, width), full)],
        ),
        out_shape=[
            shaped((rows, width), full), shaped((rows, width), low), shaped((rows, group), low),
            shaped((rows + 80, group), low), shaped((8, width), full),
            shaped((16, rows), full),
        ],
        compiler_params=pltpu.CompilerParams(
            vmem_limit_bytes=14 * MIB, dimension_semantics=("arbitrary",)
        ),
        cost_estimate=took("feed_back"),
        name="feed_back",
    )(
        place, grad_second, grad_low, slope_up, slope_gate, gate_weight, up_weight, down_weight,
        output_weight, scaled, inverse, gain_one, sums_two, attended_low, logs,
    )
    far_grad = side_swap(other)
    grad_all += pass_on(grad_all, sums)
    quarter = width // 4
    quarter = width // 4
    out_keep, out_send = call(
        out_grad, "out_grad", after(place, sums), [whole(branch_low), whole(attended_low)],
        [res((2 * quarter, width), full), res((2 * quarter, width), low)],
        [pltpu.VMEM((width, width), full)],
    )
    out_got = core_swap(out_send)

    of_side = lambda v: (v, block((v.shape[0], group), 0, lambda place: place[SIDE]))
    heads_of = [
        whole(tokens), whole(near), whole(far), whole(far_near), of_side(near_keys), of_side(far_keys),
        of_side(near_values), of_side(far_values), of_side(query), whole(far_query), whole(mine),
        whole(far_grad), whole(cosine), whole(sine), whole(seg_col), whole(seg_row), whole(stats),
    ]

    def back_one(tile, order):
        return call(
            functools.partial(back_some, (tile,), True), "back_one", order, heads_of,
            [res((two, TILE), low), res((window, 2 * TILE), low), res((3 * TILE, width), full)],
            [pltpu.VMEM((window, two), full)],
            mib=32,
        )

    eighth = hidden // 8
    eighth_of = lambda value, owner: (
        still(value),
        block((width, eighth), 0, lambda place: place[owner])
        if value.shape[0] == width
        else block((eighth, width), lambda place: place[owner], 0),
    )

    *begun, wgu = call(
        column_start, "column_start", after(place, out_keep),
        [whole(v) for v in normed_all[:3]] + [eighth_of(gate_weight, OTHER), eighth_of(up_weight, OTHER)],
        [res((eighth, 3 * rows), low)] * 3 + [res((2 * eighth, width), low)],
        mib=24,
    )
    back_first = back_one(0, after(place, wgu, grad_all[1], grad_all[2]))

    def columns(owner, order, last, *more):
        half_of = [res((width // 2, wide), kind) for kind in (full, low) for wide in (2 * eighth, eighth)]
        return call(
            functools.partial(column_grads, last), "column_grads", order,
            [whole(v) for v in normed_all] + [whole(v) for v in grad_all] + list(more),
            half_of if last else [res((width, 3 * eighth), low)],
            ([pltpu.VMEM((2 * eighth, width), low)] if last else [])
            + [pltpu.VMEM((3 * eighth, width), full)]
            + ([pltpu.VMEM((width, eighth), full)] if last else []),
            mib=36,
        )

    out_keep, out_send = call(
        out_halve, "out_halve", after(place, back_first[0]), [whole(out_keep), whole(out_got)],
        [res((quarter, width), full), res((quarter, width), low)],
    )
    out_got = side_swap(out_send)
    (col_part,) = columns(
        OTHER, after(place, out_keep), False, whole(wgu), eighth_of(down_weight, OTHER), *[whole(v) for v in begun]
    )
    col_got = core_swap(col_part)
    back_second = back_one(1, after(place, col_part))
    col_keep, down_keep, col_send, down_send = columns(
        OWN, after(place, back_second[0]), True, eighth_of(gate_weight, OWN), eighth_of(up_weight, OWN),
        eighth_of(down_weight, OWN), whole(col_got),
    )
    col_got = x_swap(col_send)
    down_got = x_swap(down_send)
    dq, even, odd_near, odd_far, grads = call(
        functools.partial(back_some, (2,), False), "back_rest", after(place, col_keep, out_got),
        heads_of + [whole(v) for v in back_first + back_second],
        [res((two, group), low), res((two, width), low), res((rows, width), low), res((rows, width), low),
         res((3 * group, width), full)],
        [pltpu.VMEM((window, two), full), pltpu.VMEM((window, width), low)],
        mib=36,
    )
    in_keep, in_send, odd_near, odd_far, sums = call(
        fold, "fold", after(place, down_got),
        [whole(grads), whole(far_grad), whole(sums), whole(odd_near), whole(odd_far)],
        [res((3 * quarter, width), full), res((3 * quarter + 16, width), low), res((rows, width), low),
         res((rows, width), low), res((8, width), full)],
    )
    in_got = core_swap(in_send)
    odd_near, odd_far = core_swap(odd_near), core_swap(odd_far)
    down_keep, down_send = call(
        second_split, "second_split", after(place, sums), [whole(down_keep), whole(down_got)],
        [res((width // 4, eighth), full), res((width // 4, eighth), low)],
    )
    down_got = swap(down_send, "dp", 4)

    share = width // n_data
    keep, send, sums = call(
        turn_over, "turn_over", after(place, down_keep),
        [whole(in_keep), whole(in_got), whole(out_keep), whole(out_got), whole(sums)],
        [res((4 * share, width), full), res((4 * share + 16, width), low), res((8, width), full)],
        [pltpu.VMEM((width, width), full)],
        mib=24,
    )
    got = low_swap(send)
    (far_send,) = call(
        far_pack, "far_pack", after(place, sums), [whole(dq), whole(even), whole(odd_far)],
        [res((rows, 3 * group), low)],
    )
    far_part = side_swap(far_send)
    col_keep, col_send = call(
        second_split, "second_split", after(place, far_send), [whole(col_keep), whole(col_got)],
        [res((width // 4, 2 * eighth), full), res((width // 4, 2 * eighth), low)],
    )
    col_got = swap(col_send, "dp", 4)
    keep, send, sums = call(
        halve_x, "halve_x", after(place, col_keep),
        [whole(keep), whole(got), whole(sums)],
        [res((2 * share, width), full), res((2 * share + 16, width), low), res((8, width), full)],
    )
    got = x_swap(send)
    weight_at = lambda i, own: (
        still(input_weight),
        block((width, group), 0, lambda place: 2 * i + (place[SIDE] if own else 1 - place[SIDE])),
    )
    (grad_tokens,) = call(
        token_grad, "token_grad", after(place, sums),
        [whole(grad_first), whole(dq), whole(even), whole(odd_near), whole(far_part)]
        + [weight_at(i, True) for i in range(3)] + [weight_at(i, False) for i in range(3)],
        [res((rows, width), low)],
        mib=24,
    )
    order = []
    for d in range(n_data):
        for s in range(n_seq):
            order.append((d * n_seq + s, (2 * s + d // 2 % 2) * n_seq + d // 4 * 2 + d % 2))
    (down,) = call(
        down_sum, "down_sum", after(place, grad_tokens), [whole(down_keep), whole(down_got)],
        [res((width // 4, eighth), low)],
    )
    down_got = lax.ppermute(down, ("dp", "seq"), order)
    keep, send, sums = call(
        halve, "halve", after(place, down), [whole(keep), whole(got), whole(sums)],
        [res((share, width), full), res((share + 16, width), low), res((8, width), full)],
    )
    got = swap(send, "dp", 4)
    pair_kept, pair_send = call(
        pair_sum, "pair_sum", after(place, sums), [whole(col_keep), whole(col_got)],
        [res((share, 2 * eighth), full), res((share, 2 * eighth), low)],
    )
    pair_got = low_swap(pair_send)
    in_own, in_send, grad_out, *vectors = call(
        last_sum, "last_sum", after(place, pair_send), [whole(keep), whole(got), whole(sums)],
        [res((share, 2 * quarter), full), res((share, quarter), low), res((share, quarter), full)]
        + [res((width,), full)] * 4,
    )
    in_moved = side_swap(in_send)
    grad_gate, grad_up = call(
        pair_place, "pair_place", after(place, in_send), [whole(pair_kept), whole(pair_got)],
        [res((share, 2 * eighth), full), res((share, 2 * eighth), full)],
    )
    (grad_down,) = call(
        widened, "widened", after(place, grad_gate), [whole(down_got)],
        [res((quarter, eighth), full)],
    )
    (grad_in,) = call(
        in_place, "in_place", after(place, grad_down), [whole(in_own), whole(in_moved)],
        [res((share, 3 * quarter), full)],
    )
    return (
        result,
        grad_tokens,
        grad_in,
        grad_out,
        grad_gate,
        grad_up,
        grad_down.T,
        *vectors,
    )


def solution(mesh):
    placed = (
        P(("dp", "seq"), None),
        P(("dp", "seq"), None),
        P("dp", None),
        P(),
        P(),
        P(),
        P(),
        P(),
        P(),
        P(),
        P(),
        P(),
    )
    paired = mesh.shape["seq"] == 4 and mesh.shape["dp"] == 8
    return jax.shard_map(
        fast if paired else general,
        mesh=mesh,
        in_specs=placed,
        out_specs=(
            P(("dp", "seq"), None),
            P(("dp", "seq"), None),
            P("dp", "seq"),
            P("dp", "seq"),
            P("dp", "seq"),
            P("dp", "seq"),
            P("dp", "seq"),
            P(),
            P(),
            P(),
            P(),
        ),
        check_vma=False,
    )
```

```python
import functools
import math

import jax
import jax.numpy as jnp
import numpy as np
from jax import lax
from jax.experimental import pallas as pl
from jax.experimental.pallas import tpu as pltpu
from jax.sharding import PartitionSpec as P

HEAD = 64


norm_eps = 1e-05
rotary_base = 1000.0
masked_value = -1e30


def doc_layout(lengths_row, count):
    ends = jnp.cumsum(lengths_row)
    place = jnp.arange(count, dtype=jnp.int32)
    after = (place[:, None] >= ends[None, :]).astype(jnp.int32)
    segment = jnp.sum(after, axis=1)
    start = jnp.sum(after * lengths_row[None, :], axis=1)
    return (segment, place - start)


def rotate(field, position):
    half = field.shape[-1] // 2
    freq = rotary_base ** (-jnp.arange(half, dtype=jnp.float32) * (2.0 / field.shape[-1]))
    angle = position.astype(jnp.float32)[:, None] * freq[None, :]
    cosine = jnp.cos(angle)[:, None, :]
    sine = jnp.sin(angle)[:, None, :]
    first = field[..., :half]
    second = field[..., half:]
    return jnp.concatenate(
        [first * cosine - second * sine, second * cosine + first * sine], axis=-1
    )


def norm_forward(value, gain, shift):
    mean = jnp.mean(value, axis=-1, keepdims=True)
    centred = value - mean
    inverse = lax.rsqrt(jnp.mean(centred * centred, axis=-1, keepdims=True) + norm_eps)
    scaled = centred * inverse
    return (scaled * gain + shift, scaled, inverse)


def norm_backward(grad, scaled, inverse, gain):
    inner = grad * gain
    back = inverse * (
        inner
        - jnp.mean(inner, axis=-1, keepdims=True)
        - scaled * jnp.mean(inner * scaled, axis=-1, keepdims=True)
    )
    return (back, jnp.sum(grad * scaled, axis=0), jnp.sum(grad, axis=0))


def inner_rows(left, right):
    return lax.dot_general(
        left, right, (((0,), (0,)), ((), ())), preferred_element_type=jnp.float32
    )


def times_transpose(left, right):
    return lax.dot_general(
        left, right, (((1,), (1,)), ((), ())), preferred_element_type=jnp.float32
    )


def general(
    tokens,
    cotangent,
    lengths,
    input_weight,
    output_weight,
    gate_weight,
    up_weight,
    down_weight,
    gain_one,
    bias_one,
    gain_two,
    bias_two,
):
    rows, width = tokens.shape
    heads = width // HEAD
    window = rows * lax.axis_size("seq")
    scale = 1.0 / math.sqrt(HEAD)
    segment_all, position_all = doc_layout(lengths[0], window)
    offset = lax.axis_index("seq") * rows
    seg_mine = lax.dynamic_slice_in_dim(segment_all, offset, rows)
    pos_mine = lax.dynamic_slice_in_dim(position_all, offset, rows)
    projected = jnp.dot(tokens, input_weight, preferred_element_type=jnp.float32)
    query = rotate(projected[:, :width].reshape(rows, heads, HEAD), pos_mine).astype(jnp.bfloat16)
    key = (
        rotate(projected[:, width : 2 * width].reshape(rows, heads, HEAD), pos_mine)
        .astype(jnp.bfloat16)
        .reshape(rows, width)
    )
    value = projected[:, 2 * width :].astype(jnp.bfloat16)

    def scores_for(key_block, seg_block):
        scores = (
            jnp.einsum("qhe,khe->hqk", query, key_block, preferred_element_type=jnp.float32) * scale
        )
        same = (seg_mine[:, None] == seg_block[None, :])[None]
        return (jnp.where(same, scores, masked_value), same)

    def split_blocks(piece, segs):
        count = piece[0].shape[0]
        size = math.gcd(count, 512)
        keys = piece[0].reshape(count // size, size, heads, HEAD)
        values = piece[1].reshape(count // size, size, heads, HEAD)
        return (keys, values, segs.reshape(count // size, size), count, size)

    start_state = (
        jnp.zeros((rows, heads, HEAD), jnp.float32),
        jnp.full((heads, rows), masked_value, jnp.float32),
        jnp.zeros((heads, rows), jnp.float32),
    )
    segs = segment_all
    keys, values, seg_blocks, count, size = split_blocks(
        (
            lax.all_gather(key, "seq", axis=0, tiled=True),
            lax.all_gather(value, "seq", axis=0, tiled=True),
        ),
        segs,
    )

    def forward_step(state, item):
        summed, peak, total = state
        key_block, value_block, seg_block = item
        scores, same = scores_for(key_block, seg_block)
        new_peak = jnp.maximum(peak, jnp.max(scores, axis=-1))
        fade = jnp.exp(peak - new_peak)
        weight = jnp.where(same, jnp.exp(scores - new_peak[..., None]), 0.0)
        total = total * fade + jnp.sum(weight, axis=-1)
        summed = summed * fade.T[..., None] + jnp.einsum(
            "hqk,khe->qhe",
            weight.astype(jnp.bfloat16),
            value_block,
            preferred_element_type=jnp.float32,
        )
        return ((summed, new_peak, total), None)

    state, unused = lax.scan(forward_step, start_state, (keys, values, seg_blocks))
    summed, peak, total = state
    attended = (summed / total.T[..., None]).reshape(rows, width)
    attended_low = attended.astype(jnp.bfloat16)
    first = tokens.astype(jnp.float32) + jnp.dot(
        attended_low, output_weight, preferred_element_type=jnp.float32
    )
    normed, scaled_one, inverse_one = norm_forward(first, gain_one, bias_one)
    normed_low = normed.astype(jnp.bfloat16)
    gate = jnp.dot(normed_low, gate_weight, preferred_element_type=jnp.float32)
    upward = jnp.dot(normed_low, up_weight, preferred_element_type=jnp.float32)
    sigma = jax.nn.sigmoid(gate)
    activated = gate * sigma
    hidden_low = (activated * upward).astype(jnp.bfloat16)
    second = normed + jnp.dot(hidden_low, down_weight, preferred_element_type=jnp.float32)
    result, scaled_two, inverse_two = norm_forward(second, gain_two, bias_two)
    grad_second, grad_gain_two, grad_bias_two = norm_backward(
        cotangent.astype(jnp.float32), scaled_two, inverse_two, gain_two
    )
    grad_ff_low = grad_second.astype(jnp.bfloat16)
    grad_hidden = times_transpose(grad_ff_low, down_weight)
    grad_gate_low = (grad_hidden * upward * (sigma * (1.0 + gate * (1.0 - sigma)))).astype(
        jnp.bfloat16
    )
    grad_up_low = (grad_hidden * activated).astype(jnp.bfloat16)
    grad_normed = (
        grad_second
        + times_transpose(grad_gate_low, gate_weight)
        + times_transpose(grad_up_low, up_weight)
    )
    grad_first, grad_gain_one, grad_bias_one = norm_backward(
        grad_normed, scaled_one, inverse_one, gain_one
    )
    grad_branch_low = grad_first.astype(jnp.bfloat16)
    grad_attended_low = times_transpose(grad_branch_low, output_weight).astype(jnp.bfloat16)
    grad_heads = grad_attended_low.reshape(rows, heads, HEAD)
    delta = jnp.sum(
        (grad_attended_low.astype(jnp.float32) * attended).reshape(rows, heads, HEAD), axis=-1
    ).T
    zero_query = jnp.zeros((rows, heads, HEAD), jnp.float32)
    grad_acc = zero_query
    segs = segment_all
    grad_query = grad_acc
    keys, values, seg_blocks, count, size = split_blocks(
        (
            lax.all_gather(key, "seq", axis=0, tiled=True),
            lax.all_gather(value, "seq", axis=0, tiled=True),
        ),
        segs,
    )

    def backward_step(grad_acc, item):
        key_block, value_block, seg_block = item
        scores, same = scores_for(key_block, seg_block)
        prob = jnp.where(same, jnp.exp(scores - peak[..., None]) / total[..., None], 0.0)
        prob_grad = jnp.einsum(
            "qhe,khe->hqk", grad_heads, value_block, preferred_element_type=jnp.float32
        )
        score_grad = (prob * (prob_grad - delta[..., None])).astype(jnp.bfloat16)
        grad_acc = (
            grad_acc
            + jnp.einsum("hqk,khe->qhe", score_grad, key_block, preferred_element_type=jnp.float32)
            * scale
        )
        prob_low = prob.astype(jnp.bfloat16)
        key_grad = (
            jnp.einsum("hqk,qhe->khe", score_grad, query, preferred_element_type=jnp.float32)
            * scale
        )
        value_grad = jnp.einsum(
            "hqk,qhe->khe", prob_low, grad_heads, preferred_element_type=jnp.float32
        )
        return (grad_acc, (key_grad.reshape(size, width), value_grad.reshape(size, width)))

    grad_query, outputs = lax.scan(backward_step, grad_query, (keys, values, seg_blocks))
    grad_acc = grad_query
    key_part = outputs[0].reshape(count, width)
    value_part = outputs[1].reshape(count, width)
    grad_key, grad_value = (
        lax.psum_scatter(
            key_part.astype(jnp.bfloat16), "seq", scatter_dimension=0, tiled=True
        ).astype(jnp.float32),
        lax.psum_scatter(
            value_part.astype(jnp.bfloat16), "seq", scatter_dimension=0, tiled=True
        ).astype(jnp.float32),
    )
    query_back = rotate(grad_acc, -pos_mine).reshape(rows, width)
    key_back = rotate(grad_key.reshape(rows, heads, HEAD), -pos_mine).reshape(rows, width)
    grad_projected_low = jnp.concatenate([query_back, key_back, grad_value], axis=1).astype(
        jnp.bfloat16
    )
    grad_tokens = (grad_first + times_transpose(grad_projected_low, input_weight)).astype(
        jnp.bfloat16
    )
    column_grads = (
        lax.all_to_all(grad_projected_low, "seq", split_axis=1, concat_axis=0, tiled=True),
        lax.all_to_all(grad_branch_low, "seq", split_axis=1, concat_axis=0, tiled=True),
        lax.all_to_all(grad_gate_low, "seq", split_axis=1, concat_axis=0, tiled=True),
        lax.all_to_all(grad_up_low, "seq", split_axis=1, concat_axis=0, tiled=True),
        lax.all_to_all(grad_ff_low, "seq", split_axis=1, concat_axis=0, tiled=True),
    )
    tok_rows = lax.all_gather(tokens, "seq", axis=0, tiled=True)
    normed_rows = lax.all_gather(normed_low, "seq", axis=0, tiled=True)
    attended_rows = lax.all_gather(attended_low, "seq", axis=0, tiled=True)
    hidden_rows = lax.all_gather(hidden_low, "seq", axis=0, tiled=True)
    count = tok_rows.shape[0]
    cols = [member for member in column_grads]
    summed_grads = (
        lax.psum_scatter(
            inner_rows(tok_rows, cols[0]).astype(jnp.bfloat16),
            "dp",
            scatter_dimension=0,
            tiled=True,
        ).astype(jnp.float32),
        lax.psum_scatter(
            inner_rows(attended_rows, cols[1]).astype(jnp.bfloat16),
            "dp",
            scatter_dimension=0,
            tiled=True,
        ).astype(jnp.float32),
        lax.psum_scatter(
            inner_rows(normed_rows, cols[2]).astype(jnp.bfloat16),
            "dp",
            scatter_dimension=0,
            tiled=True,
        ).astype(jnp.float32),
        lax.psum_scatter(
            inner_rows(normed_rows, cols[3]).astype(jnp.bfloat16),
            "dp",
            scatter_dimension=0,
            tiled=True,
        ).astype(jnp.float32),
        lax.psum_scatter(
            inner_rows(hidden_rows, cols[4]).astype(jnp.bfloat16),
            "dp",
            scatter_dimension=0,
            tiled=True,
        ).astype(jnp.float32),
    )
    norm_grads = lax.psum(
        (grad_gain_one, grad_bias_one, grad_gain_two, grad_bias_two), ("dp", "seq")
    )
    return (
        result.astype(jnp.bfloat16),
        grad_tokens,
        summed_grads[0],
        summed_grads[1],
        summed_grads[2],
        summed_grads[3],
        summed_grads[4],
        norm_grads[0],
        norm_grads[1],
        norm_grads[2],
        norm_grads[3],
    )


low = jnp.bfloat16
full = jnp.float32
TILE = 128
MIB = 1024 * 1024


def nn(left, right):
    return lax.dot_general(
        left, right, (((1,), (0,)), ((), ())), preferred_element_type=jnp.float32
    )


def nt(left, right):
    return lax.dot_general(
        left, right, (((1,), (1,)), ((), ())), preferred_element_type=jnp.float32
    )


def tn(left, right):
    return lax.dot_general(
        left, right, (((0,), (0,)), ((), ())), preferred_element_type=jnp.float32
    )


def block(shape, *at):
    at = at or (0,) * len(shape)

    def index(*args):
        return tuple(a(*args[1:]) if callable(a) else a for a in at)

    return pl.BlockSpec(tuple(shape), index)


def shaped(shape, kind):
    return jax.ShapeDtypeStruct(tuple(shape), kind)


SEQ, SIDE, X, LOW, HIGH, PAIR, LONE, OTHER_PAIR, OTHER_LONE, OWN, OTHER, CORE = range(12)

COST = {
    "tables": 1.5, "first_half": 6.9, "second_half": 7.9, "feed_forward": 8.4, "feed_back": 8.6,
    "project_heads": 4, "back_one": 6.5, "back_rest": 7, "column_start": 4, "column_grads": 6, "token_grad": 3,
    "out_grad": 1.2,
}


def took(name):
    return pl.CostEstimate(flops=int(COST.get(name, 0.5) * 10**9), bytes_accessed=1, transcendentals=0)


def still(value):
    return pltpu.with_memory_space_constraint(value, pltpu.HBM)


def call(body, name, scalars, operands, results, scratch=(), mib=16):
    return pl.pallas_call(
        body,
        grid_spec=pltpu.PrefetchScalarGridSpec(
            num_scalar_prefetch=1,
            grid=(1,),
            in_specs=[spec for unused, spec in operands],
            out_specs=[spec for unused, spec in results],
            scratch_shapes=list(scratch),
        ),
        out_shape=[shape for shape, unused in results],
        compiler_params=pltpu.CompilerParams(
            vmem_limit_bytes=mib * MIB, dimension_semantics=("arbitrary",)
        ),
        cost_estimate=took(name),
        name=name,
    )(scalars, *[value for value, unused in operands])


def whole(value):
    return (value, block(value.shape))


def turn(field, cosine, sine):
    lane = lax.broadcasted_iota(jnp.int32, field.shape, 1)
    half = HEAD // 2
    other = jnp.where(
        lane % HEAD < half, pltpu.roll(field, TILE - half, 1), pltpu.roll(field, half, 1)
    )
    return field * cosine + other * sine


def one_head(pair, which):
    lane = lax.broadcasted_iota(jnp.int32, pair.shape, 1)
    return jnp.where((lane // HEAD) == which, pair, jnp.zeros_like(pair))


def rows_at(index, count):
    return pl.ds(pl.multiple_of(index * count, count), count)


def pack(sums):
    high = sums.astype(low)
    return jnp.concatenate([high, (sums - high.astype(jnp.float32)).astype(low)], axis=0)


def unpack(packed):
    wide = packed.astype(jnp.float32)
    return wide[:8] + wide[8:]


def tables(place, lengths, freq, cosine, sine, seg_col, seg_row):
    count = cosine.shape[0]
    rows = count // 4
    lane = lax.broadcasted_iota(jnp.int32, (8, count), 1)
    index = jnp.zeros_like(lane)
    for i in range(1, 4):
        index = index + (lane >= i * rows).astype(jnp.int32)
    spot = (index ^ place[SEQ]) * rows + (lane - index * rows)
    end = jnp.int32(0)
    segment = jnp.zeros_like(lane)
    start = jnp.zeros_like(lane)
    for i in range(lengths.shape[1]):
        length = lengths[0, i]
        end = end + length
        past = (spot >= end).astype(jnp.int32)
        segment = segment + past
        start = start + past * length
    position = (spot - start).astype(jnp.float32)
    angle = freq[:, :1] * position[:1]
    c, s = jnp.cos(angle), jnp.sin(angle)
    cosine[...] = jnp.concatenate([c] * 4, axis=0).T
    sine[...] = jnp.concatenate([-s, s] * 2, axis=0).T
    seg_row[...] = segment
    wide = jnp.broadcast_to(segment[:1].astype(jnp.float32), (TILE, count))
    seg_col[...] = wide.T.astype(jnp.int32)


def put_keys(tokens, wk, wv, cosine, sine, keys, values, start):
    rows = tokens.shape[0]
    projected = nn(tokens, wk)
    for tile in range(projected.shape[1] // TILE):
        cols = slice(tile * TILE, (tile + 1) * TILE)
        keys[start : start + rows, cols] = turn(projected[:, cols], cosine, sine).astype(low)
    values[start : start + rows, :] = nn(tokens, wv).astype(low)


def put_query(tokens, wq, cosine, sine, query):
    scale = 1.0 / math.sqrt(HEAD)
    projected = nn(tokens, wq)
    for tile in range(projected.shape[1] // TILE):
        cols = slice(tile * TILE, (tile + 1) * TILE)
        turned = turn(projected[:, cols], cosine, sine)
        query[:, cols] = (turned.astype(low) * scale).astype(low)


def attend(query, keys, values, bias, take):
    @pl.loop(0, query.shape[1] // TILE, unroll=6)
    def _(tile):
        cols = rows_at(tile, TILE)
        key_pair = keys[:, cols]
        value_pair = values[:, cols]
        query_pair = query[:, cols]
        for which in range(TILE // HEAD):
            scores = nt(key_pair, one_head(query_pair, which)) + bias[...]
            peak = jnp.max(scores, axis=0, keepdims=True)
            weight = jnp.exp(scores - peak)
            total = jnp.sum(weight, axis=0, keepdims=True)
            out = tn(value_pair, weight.astype(low))[which * HEAD : (which + 1) * HEAD]
            take(tile * (TILE // HEAD) + which, out, peak, total)


def first_half(
    place, own, near, wq, wk, wv, cosine, sine, seg_key, seg_query, query, acc, peaks, totals,
    keys, values, bias,
):
    rows = own.shape[0]
    put_query(own[...], wq[...], cosine[:rows, :], sine[:rows, :], query)
    put_keys(own[...], wk[...], wv[...], cosine[:rows, :], sine[:rows, :], keys, values, 0)
    put_keys(near[...], wk[...], wv[...], cosine[rows:, :], sine[rows:, :], keys, values, rows)
    bias[...] = jnp.where(seg_key[:, :1] == seg_query[:1, :], 0.0, masked_value)

    def take(head, out, peak, total):
        acc[rows_at(head, HEAD), :] = out
        peaks[pl.ds(head, 1), :] = peak
        totals[pl.ds(head, 1), :] = total

    attend(query, keys, values, bias, take)


def second_half(
    place, own, far, far_near, wk, wv, wo, cosine, sine, seg_key, seg_query, query, acc, peaks, totals,
    gain, shift, far_wq, attended_low, normed, normed_low, scaled, inverse, keys, values, far_query, logs, bias,
    turned,
):
    rows, width = own.shape
    put_keys(far[...], wk[...], wv[...], cosine[:rows, :], sine[:rows, :], keys, values, 0)
    put_keys(far_near[...], wk[...], wv[...], cosine[rows:, :], sine[rows:, :], keys, values, rows)
    bias[...] = jnp.where(seg_key[:, :1] == seg_query[:1, :], 0.0, masked_value)
    put_query(far[...], far_wq[...], cosine[:rows, :], sine[:rows, :], far_query)
    side_heads = width // HEAD // 2
    logs[...] = jnp.zeros_like(logs)

    def take(head, out, peak, total):
        part = rows_at(head, HEAD)
        before = peaks[pl.ds(head, 1), :]
        best = jnp.maximum(before, peak)
        fade = jnp.exp(before - best)
        grow = jnp.exp(peak - best)
        whole_total = totals[pl.ds(head, 1), :] * fade + total * grow
        logs[pl.ds(head + jnp.where(head >= side_heads, 8 - side_heads, 0), 1), :] = best + jnp.log(whole_total)
        inverse_total = 1.0 / whole_total
        turned[part, :] = acc[part, :] * (fade * inverse_total) + out * (grow * inverse_total)

    attend(query, keys, values, bias, take)
    attended = turned[...].T.astype(low)
    attended_low[...] = attended
    first = own[...].astype(jnp.float32) + nn(attended, wo[...])
    mean = jnp.mean(first, axis=1, keepdims=True)
    centred = first - mean
    spread = lax.rsqrt(jnp.mean(centred * centred, axis=1, keepdims=True) + norm_eps)
    unit = centred * spread
    value = unit * gain[...][None, :] + shift[...][None, :]
    scaled[...] = unit
    inverse[...] = jnp.broadcast_to(spread, (rows, TILE))
    normed[...] = value
    normed_low[...] = value.astype(low)


def halves(place, by_side, by_low, first, second):
    half = first.shape[0]
    first[...] = by_side[:half, :]
    second[...] = by_low[half:, :]


def feed_forward(
    normed, normed_low, wg, wu, wd, cotangent, gain, shift,
    slope_up, slope_gate, result, grad_second, grad_low, sums, acc,
):
    chunk = wg.shape[1] // 4
    acc[...] = normed[...]

    @pl.loop(0, 4, unroll=4)
    def _(step):
        cols = rows_at(step, chunk)
        gate = nn(normed_low[...], wg[:, cols])
        upward = nn(normed_low[...], wu[:, cols])
        sigma = jax.nn.sigmoid(gate)
        active = gate * sigma
        slope_up[:, cols] = active.astype(low)
        slope_gate[:, cols] = (upward * (sigma * (1.0 + gate * (1.0 - sigma)))).astype(low)
        acc[...] += nn((active * upward).astype(low), wd[cols, :])

    if True:
        second = acc[...]
        mean = jnp.mean(second, axis=1, keepdims=True)
        centred = second - mean
        spread = lax.rsqrt(jnp.mean(centred * centred, axis=1, keepdims=True) + norm_eps)
        unit = centred * spread
        result[...] = (unit * gain[...][None, :] + shift[...][None, :]).astype(low)
        grad = cotangent[...].astype(jnp.float32)
        inner = grad * gain[...][None, :]
        back = spread * (
            inner
            - jnp.mean(inner, axis=1, keepdims=True)
            - unit * jnp.mean(inner * unit, axis=1, keepdims=True)
        )
        grad_second[...] = back
        grad_low[...] = back.astype(low)
        sums[0:1, :] = jnp.sum(grad * unit, axis=0, keepdims=True)
        sums[1:2, :] = jnp.sum(grad, axis=0, keepdims=True)


def feed_back(
    place, grad_second, grad_low, slope_up, slope_gate, wg, wu, wd, wo, scaled, inverse, gain, sums_two,
    attended_low, logs, grad_first, branch_low, mine, other, sums, stats, acc,
):
    chunk = wg.shape[1] // 4
    acc[...] = grad_second[...]

    @pl.loop(0, 4, unroll=4)
    def _(step):
        cols = rows_at(step, chunk)
        hidden = nt(grad_low[...], wd[cols, :])
        gate = (hidden * slope_gate[:, cols].astype(jnp.float32)).astype(low)
        upward = (hidden * slope_up[:, cols].astype(jnp.float32)).astype(low)
        acc[...] += nt(gate, wg[:, cols]) + nt(upward, wu[:, cols])

    if True:
        grad = acc[...]
        unit = scaled[...]
        inner = grad * gain[...][None, :]
        back = inverse[:, :1] * (
            inner
            - jnp.mean(inner, axis=1, keepdims=True)
            - unit * jnp.mean(inner * unit, axis=1, keepdims=True)
        )
        grad_first[...] = back
        branch_low[...] = back.astype(low)
        attended_grad = nt(branch_low[...], wo[...]).astype(low)
        group = mine.shape[1]
        height = mine.shape[0]
        left, right = attended_grad[:, :group], attended_grad[:, group:]
        second_side = place[SIDE] > 0
        mine[...] = jnp.where(second_side, right, left)
        other[:height, :] = jnp.where(second_side, left, right)
        sums[...] = jnp.zeros_like(sums)
        sums[0:1, :] = jnp.sum(grad * unit, axis=0, keepdims=True)
        sums[1:2, :] = jnp.sum(grad, axis=0, keepdims=True)
        sums[2:4, :] = sums_two[...]
        for i in range(2):
            part = slice(height + i * 16, height + (i + 1) * 16)
            other[part, :] = pack(sums[:, i * group : (i + 1) * group])
        product = attended_grad.astype(jnp.float32) * attended_low[...].astype(jnp.float32)
        high = product.astype(low)
        rest = (product - high.astype(jnp.float32)).astype(low)
        row = lax.broadcasted_iota(jnp.int32, (16, 2 * group), 0)
        lane = lax.broadcasted_iota(jnp.int32, (16, 2 * group), 1)
        head = lane // HEAD
        ones = (row == head + jnp.where(lane >= group, 8 - group // HEAD, 0)).astype(low)
        deltas = nt(ones, high) + nt(ones, rest)
        left, right = (
            jnp.concatenate([logs[part, :], deltas[part, :]], axis=0) for part in (slice(0, 8), slice(8, 16))
        )
        stats[...] = jnp.where(second_side, right, left)
        rest = jnp.where(second_side, left, right)
        other[height + 32 :, height:] = jnp.zeros((48, group - height), low)
        for i in range(3):
            part = slice(height + 32 + i * 16, height + 48 + i * 16)
            piece = rest.astype(low)
            other[part, :height] = piece
            rest = rest - piece.astype(jnp.float32)


def out_grad(place, branch_low, attended_low, keep, send, turned):
    turned[...] = tn(branch_low[...], attended_low[...])
    quarter = turned.shape[0] // 4
    core = place[CORE]
    for i in range(2):
        to = slice(i * quarter, (i + 1) * quarter)
        keep[to, :] = turned[rows_at(2 * i + core, quarter), :]
        send[to, :] = turned[rows_at(2 * i + 1 - core, quarter), :].astype(low)


def out_halve(place, keep, got, kept, send):
    quarter = keep.shape[0] // 2
    mine, other = rows_at(place[SIDE], quarter), rows_at(1 - place[SIDE], quarter)
    kept[...] = keep[mine, :] + got[mine, :].astype(jnp.float32)
    send[...] = (keep[other, :] + got[other, :].astype(jnp.float32)).astype(low)


def back_tile(key_pair, value_pair, query_pair, grad_pair, bias, logs, deltas):
    scale = 1.0 / math.sqrt(HEAD)
    grad_key = None
    grad_value = None
    pieces = []
    for which in range(TILE // HEAD):
        query_head = one_head(query_pair, which)
        grad_head = one_head(grad_pair, which)
        scores = nt(key_pair, query_head) + bias[...]
        prob = jnp.exp(scores - logs[which])
        prob_grad = nt(value_pair, grad_head)
        score_grad = (prob * (prob_grad - deltas[which])).astype(low)
        value_part = nn(prob.astype(low), grad_head)
        key_part = nn(score_grad, query_head)
        grad_key = key_part if grad_key is None else grad_key + key_part
        grad_value = value_part if grad_value is None else grad_value + value_part
        pieces.append(tn(key_pair, score_grad)[which * HEAD : (which + 1) * HEAD])
    return jnp.concatenate(pieces, axis=0).T * scale, grad_key, grad_value


def back_some(tiles, first, place, *refs):
    own, near, far, far_near = refs[:4]
    pairs = [refs[i : i + 2] for i in range(4, 12, 2)]
    cosine, sine, seg_key, seg_query, stats = refs[12:17]
    far_grad = refs[11]
    rows = own.shape[0]
    blocks = (own, near, far, far_near)
    if first:
        dq, both, grads, bias = refs[17:]
    else:
        before = refs[17:23]
        dq, even, odd_near, odd_far, grads, bias, both = refs[23:]
    group = pairs[0][0].shape[1]
    for index in range(2):
        part = slice(2 * index * rows, (2 * index + 1) * rows)
        to = slice(index * rows, (index + 1) * rows)
        bias[:, to] = jnp.where(seg_key[:, :1] == seg_query[:1, part], 0.0, masked_value)
    far_stats = sum(
        far_grad[rows + 32 + i * 16 : rows + 48 + i * 16, :rows].astype(jnp.float32) for i in range(3)
    )
    both_stats = jnp.concatenate([stats[...], far_stats], axis=1)
    for tile in tiles:
        cols = slice(tile * TILE, (tile + 1) * TILE)
        heads = [tile * (TILE // HEAD) + which for which in range(TILE // HEAD)]
        logs = [both_stats[head : head + 1] for head in heads]
        deltas = [both_stats[8 + head : 9 + head] for head in heads]
        keys, values, queries, outs = (
            jnp.concatenate([one[:, cols], two[: one.shape[0], cols]], axis=0) for one, two in pairs
        )
        grad_query, grad_key, grad_value = back_tile(
            keys, values, queries, outs, bias, logs, deltas
        )
        to = slice(0, TILE) if first else cols
        shifted = slice(TILE, 2 * TILE) if first else slice(group + tile * TILE, group + (tile + 1) * TILE)
        for index in range(2):
            part = slice(index * rows, (index + 1) * rows)
            at = slice(2 * index * rows, (2 * index + 1) * rows)
            dq[part, to] = turn(grad_query[part], cosine[at, :], -sine[at, :]).astype(low)
        both[:, to] = turn(grad_key, cosine[...], -sine[...]).astype(low)
        both[:, shifted] = grad_value.astype(low)
        pair = jnp.concatenate([both[:, to], both[:, shifted]], axis=1)
        total = None
        for index in range(4):
            part = slice(index * rows, (index + 1) * rows)
            product = tn(pair[part], blocks[index][...])
            total = product if total is None else total + product
        query_rows = tn(dq[:rows, to], own[...]) + tn(dq[rows:, to], far[...])
        if first:
            grads[:TILE, :] = query_rows
            grads[TILE:, :] = total
        else:
            grads[tile * TILE : (tile + 1) * TILE, :] = query_rows
            for kind in range(2):
                at = (kind + 1) * group + tile * TILE
                grads[at : at + TILE, :] = total[kind * TILE : (kind + 1) * TILE]
    if first:
        return
    for tile in range(2):
        dq_before, both_before, grads_before = before[3 * tile : 3 * tile + 3]
        dq[:, tile * TILE : (tile + 1) * TILE] = dq_before[...]
        for kind in range(3):
            at = kind * group + tile * TILE
            if kind < 2:
                both[:, at : at + TILE] = both_before[:, kind * TILE : (kind + 1) * TILE]
            grads[at : at + TILE, :] = grads_before[kind * TILE : (kind + 1) * TILE, :]
    for index in range(4):
        part = slice(index * rows, (index + 1) * rows)
        if index % 2:
            (odd_far if index > 1 else odd_near)[...] = both[part, :]
        else:
            even[index // 2 * rows : (index // 2 + 1) * rows, :] = both[part, :]


def fold(place, grads, far_grad, sums, odd_near, odd_far, keep, send, near_send, far_send, kept_sums):
    quarter = keep.shape[0] // 3
    pair, lone, other_pair, other_lone = (place[i] for i in (PAIR, LONE, OTHER_PAIR, OTHER_LONE))
    for i in range(3):
        to = slice(i * quarter, (i + 1) * quarter)
        keep[to, :] = grads[rows_at(pair + i if i < 2 else lone, quarter), :]
        send[to, :] = grads[rows_at(other_pair + i if i < 2 else other_lone, quarter), :].astype(low)
    rows = odd_near.shape[0]
    got = jnp.concatenate(
        [unpack(far_grad[rows : rows + 16, :]), unpack(far_grad[rows + 16 : rows + 32, :])], axis=1
    )
    total = sums[...] + got
    kept_sums[...] = total
    send[3 * quarter :, :] = pack(total)
    near_send[...] = odd_near[...]
    far_send[...] = odd_far[...]


def turn_over(place, keep, got, out_keep, out_got, sums, kept, send, kept_sums, turned):
    height = keep.shape[0]
    turned[:, :height] = (keep[...] + got[:height, :].astype(jnp.float32)).T
    turned[:, height:] = (out_keep[...] + out_got[...].astype(jnp.float32)).T
    bit = place[LOW]
    part = turned.shape[0] // 8
    for i in range(4):
        to = slice(i * part, (i + 1) * part)
        at = 4 * (i // 2) + i % 2
        kept[to, :] = turned[rows_at(at + 2 * bit, part), :]
        send[to, :] = turned[rows_at(at + 2 * (1 - bit), part), :].astype(low)
    both = sums[...] + unpack(got[height:, :])
    kept_sums[...] = both
    send[4 * part :, :] = pack(both)


def halve_x(place, keep, got, sums, kept, send, kept_sums):
    bit = place[X]
    part = keep.shape[0] // 4
    for i in range(2):
        to = slice(i * part, (i + 1) * part)
        for at, out in ((bit, kept), (1 - bit, send)):
            there = rows_at(2 * i + at, part)
            out[to, :] = (keep[there, :] + got[there, :].astype(jnp.float32)).astype(out.dtype)
    both = sums[...] + unpack(got[4 * part :, :])
    kept_sums[...] = both
    send[2 * part :, :] = pack(both)


def halve(place, keep, got, sums, kept, send, kept_sums):
    bit = place[HIGH]
    height = keep.shape[0]
    part = height // 2
    mine, other = rows_at(bit, part), rows_at(1 - bit, part)
    kept[...] = keep[mine, :] + got[mine, :].astype(jnp.float32)
    send[:part, :] = (keep[other, :] + got[other, :].astype(jnp.float32)).astype(low)
    both = sums[...] + unpack(got[height:, :])
    kept_sums[...] = both
    send[part:, :] = pack(both)


def last_sum(place, keep, got, sums, own, send, out, *vectors):
    height = keep.shape[0]
    total = keep[...] + got[:height, :].astype(jnp.float32)
    quarter = out.shape[1]
    own[...] = total[:, : 2 * quarter]
    send[...] = total[:, 2 * quarter : 3 * quarter].astype(low)
    out[...] = total[:, 3 * quarter :]
    both = sums[...] + unpack(got[height:, :])
    for i, vector in enumerate(vectors):
        vector[...] = both[i]


def turn_weights(wg, wu, wgu):
    half = wg.shape[1]
    wgu[:half, :] = wg[...].astype(jnp.float32).T.astype(low)
    wgu[half:, :] = wu[...].astype(jnp.float32).T.astype(low)


def hidden_parts(wgu, rows):
    both = nt(wgu, rows)
    half = both.shape[0] // 2
    gate, upward = both[:half], both[half:]
    sigma = jax.nn.sigmoid(gate)
    active = gate * sigma
    slope = upward * (sigma * (1.0 + gate * (1.0 - sigma)))
    return (active * upward).astype(low), active, slope


def column_start(place, own, by_side, by_low, wg, wu, hidden, active, slope, wgu):
    turn_weights(wg, wu, wgu)
    rows = jnp.concatenate([own[...], by_side[...], by_low[...]], axis=0)
    values = hidden_parts(wgu[...], rows)
    for value, out in zip(values, (hidden, active, slope)):
        out[...] = value.astype(low)


def column_grads(last, place, *refs):
    count = 5
    rows_refs, back_refs = refs[:count], refs[count : 2 * count]
    rows = jnp.concatenate([v[...] for v in rows_refs], axis=0)
    back = jnp.concatenate([v[...] for v in back_refs], axis=0)
    rest = refs[2 * count :]
    if last:
        wg, wu, wd = rest[:3]
        earlier = (rest[3], rest[-1])
        outs, wgu, acc = rest[4:8], rest[8], rest[9]
        turn_weights(wg, wu, wgu)
        hidden, active, slope = hidden_parts(wgu[...], rows)
    else:
        wgu, wd = rest[:2]
        outs, acc = rest[5:6], rest[6]
        late = hidden_parts(wgu[...], rows[-2 * rows_refs[-1].shape[0] :])
        hidden, active, slope = (
            jnp.concatenate([begun[...], value.astype(low)], axis=1) for begun, value in zip(rest[2:5], late)
        )
    half, width = wd.shape
    grad_hidden = nt(wd[...], back)
    grad_gate = (grad_hidden * slope.astype(jnp.float32)).astype(low)
    grad_up = (grad_hidden * active.astype(jnp.float32)).astype(low)
    for i, product in enumerate((nn(grad_gate, rows), nn(grad_up, rows), nn(hidden, back))):
        acc[i * half : (i + 1) * half, :] = product
    if last:
        got, total = earlier
        bit = place[X]
        for i in range(3):
            part = slice(i * half, (i + 1) * half)
            total[...] = acc[part, :].T + got[:, part].astype(jnp.float32)
            keep, send, to_cols = (outs[0], outs[2], part) if i < 2 else (outs[1], outs[3], slice(None))
            count = 4 if i < 2 else 2
            cut = width // (2 * count)
            for j in range(count):
                to = slice(j * cut, (j + 1) * cut)
                keep[to, to_cols] = total[rows_at(2 * j + bit, cut), :]
                send[to, to_cols] = total[rows_at(2 * j + 1 - bit, cut), :].astype(low)
    else:
        for i in range(3):
            part = slice(i * half, (i + 1) * half)
            outs[0][:, part] = acc[part, :].T.astype(low)


def second_split(place, keep, got, kept, send):
    bit = place[HIGH]
    part = keep.shape[0] // 2
    mine, other = rows_at(bit, part), rows_at(1 - bit, part)
    kept[...] = keep[mine, :] + got[mine, :].astype(jnp.float32)
    send[...] = (keep[other, :] + got[other, :].astype(jnp.float32)).astype(low)


def pair_sum(place, keep, got, kept, send):
    part = kept.shape[0]
    mine, other = rows_at(place[LOW], part), rows_at(1 - place[LOW], part)
    kept[...] = keep[mine, :] + got[mine, :].astype(jnp.float32)
    send[...] = (keep[other, :] + got[other, :].astype(jnp.float32)).astype(low)


def down_sum(place, keep, got, out):
    out[...] = (keep[...] + got[...].astype(jnp.float32)).astype(low)


def in_place(place, own, moved, out):
    got = moved[...].astype(jnp.float32)
    first = jnp.concatenate([own[...], got], axis=1)
    second = jnp.concatenate([got, own[...]], axis=1)
    out[...] = jnp.where(place[CORE] == 0, first, second)


def pair_place(place, kept, got, gate, upward):
    half = kept.shape[1] // 2
    for i, out in enumerate((gate, upward)):
        cols = slice(i * half, (i + 1) * half)
        out[:, rows_at(place[LOW], half)] = kept[:, cols]
        out[:, rows_at(1 - place[LOW], half)] = got[:, cols].astype(jnp.float32)


def far_pack(place, dq, even, got, out):
    rows, group = out.shape[0], dq.shape[1]
    out[:, :group] = dq[rows:, :]
    total = even[rows:, :].astype(jnp.float32) + got[...].astype(jnp.float32)
    out[:, group:] = total.astype(low)


def token_grad(place, grad_first, dq, even, got, far_part, *refs):
    weights, out = refs[:-1], refs[-1]
    rows = grad_first.shape[0]
    kind = len(weights) // 2
    total = grad_first[...]
    key_value = (
        even[:rows, :].astype(jnp.float32) + got[...].astype(jnp.float32)
    ).astype(low)
    group = dq.shape[1]
    for i in range(kind):
        cols = slice(i * group, (i + 1) * group)
        mine = dq[:rows, :] if i == 0 else key_value[:, (i - 1) * group : i * group]
        total = total + nt(mine, weights[i][...]) + nt(far_part[:, cols], weights[kind + i][...])
    out[...] = total.astype(low)


def after(value, *others):
    return lax.optimization_barrier((value,) + others)[0]


def fast(
    tokens,
    cotangent,
    lengths,
    input_weight,
    output_weight,
    gate_weight,
    up_weight,
    down_weight,
    gain_one,
    bias_one,
    gain_two,
    bias_two,
):
    rows, width = tokens.shape
    hidden = gate_weight.shape[1]
    seq = lax.axis_index("seq")
    data = lax.axis_index("dp")
    n_seq, n_data = lax.axis_size("seq"), lax.axis_size("dp")
    core, side = seq % 2, seq // 2
    bit_x, bit_low, bit_high = data % 2, (data // 2) % 2, data // 4
    pairs, lones = (0, 2, 2, 4), (4, 5, 0, 1)
    table = lambda values, i: sum(jnp.where(i == k, v, 0) for k, v in enumerate(values))
    place = jnp.stack(
        [
            jnp.asarray(v, jnp.int32)
            for v in (
                seq, side, bit_x, bit_low, bit_high,
                table(pairs, seq), table(lones, seq), table(pairs, seq ^ 1), table(lones, seq ^ 1),
                2 * seq + bit_low, 2 * (seq ^ 1) + bit_low, core,
            )
        ]
    )

    def swap(value, axis, bit):
        size = n_seq if axis == "seq" else n_data
        return lax.ppermute(value, axis, [(i, i ^ bit) for i in range(size)])

    def core_swap(value):
        return swap(value, "seq", 1)

    def side_swap(value):
        return swap(value, "seq", 2)

    def x_swap(value):
        return swap(value, "dp", 1)

    def low_swap(value):
        return swap(value, "dp", 2)

    def high_swap(value):
        return swap(value, "dp", 4)

    far = side_swap(tokens)
    near = core_swap(tokens)

    window = 4 * rows
    two = 2 * rows
    half = HEAD // 2
    freq = rotary_base ** (-jnp.arange(half, dtype=jnp.float32) * (2.0 / HEAD))
    cosine, sine, seg_col, seg_row = pl.pallas_call(
        tables,
        grid_spec=pltpu.PrefetchScalarGridSpec(
            num_scalar_prefetch=2,
            grid=(1,),
            in_specs=[block((half, TILE))],
            out_specs=[block((window, TILE))] * 3 + [block((8, window))],
        ),
        out_shape=[
            shaped((window, TILE), full), shaped((window, TILE), full),
            shaped((window, TILE), jnp.int32), shaped((8, window), jnp.int32),
        ],
        compiler_params=pltpu.CompilerParams(vmem_limit_bytes=16 * MIB),
        cost_estimate=took("tables"),
        name="tables",
    )(place, lengths, jnp.broadcast_to(freq[:, None], (half, TILE)))

    third = lambda i: (input_weight, block((width, width), 0, i))
    part = lambda v, i: (v, block((two, TILE), i, 0))
    query_row = (seg_row, block((8, rows), 0, 0))
    res = lambda shape, kind: (shaped(shape, kind), block(shape))
    query, acc, peaks, totals, near_keys, near_values = call(
        first_half, "first_half", place,
        [whole(tokens), whole(near), third(0), third(1), third(2),
         part(cosine, 0), part(sine, 0), part(seg_col, 0), query_row],
        [res((rows, width), low), res((width, rows), full), res((16, rows), full), res((16, rows), full),
         res((two, width), low), res((two, width), low)],
        [pltpu.VMEM((two, rows), full)],
        mib=22,
    )
    far_near = core_swap(after(far, peaks))
    attended_low, normed, normed_low, scaled, inverse, far_keys, far_values, far_query, logs = call(
        second_half, "second_half", place,
        [whole(tokens), whole(far), whole(far_near), third(1), third(2), whole(output_weight),
         part(cosine, 1), part(sine, 1), part(seg_col, 1), query_row,
         whole(query), whole(acc), whole(peaks), whole(totals), whole(gain_one), whole(bias_one),
         (input_weight, block((width, width // 2), 0, lambda place: place[SIDE]))],
        [res((rows, width), low), res((rows, width), full), res((rows, width), low),
         res((rows, width), full), res((rows, TILE), full), res((two, width), low),
         res((two, width), low), res((rows, width // 2), low), res((16, rows), full)],
        [pltpu.VMEM((two, rows), full), pltpu.VMEM((width, rows), full)],
        mib=22,
    )

    def spread(value):
        return [value, side_swap(value), low_swap(value)]

    normed_all = spread(normed_low)

    inside = pl.BlockSpec(memory_space=pltpu.VMEM)
    slope_up, slope_gate, result, grad_second, grad_low, sums_two = pl.pallas_call(
        feed_forward,
        grid=(1,),
        in_specs=[
            block((rows, width)), block((rows, width)), inside, inside, inside,
            block((rows, width)), block((width,)), block((width,)),
        ],
        out_specs=[
            block((rows, hidden)), block((rows, hidden)),
            block((rows, width)), block((rows, width)), block((rows, width)), block((2, width)),
        ],
        out_shape=[
            shaped((rows, hidden), low), shaped((rows, hidden), low), shaped((rows, width), low),
            shaped((rows, width), full), shaped((rows, width), low), shaped((2, width), full),
        ],
        scratch_shapes=[pltpu.VMEM((rows, width), full)],
        compiler_params=pltpu.CompilerParams(
            vmem_limit_bytes=14 * MIB, dimension_semantics=("arbitrary",)
        ),
        cost_estimate=took("feed_forward"),
        name="feed_forward",
    )(
        normed, normed_low, gate_weight, up_weight, down_weight, cotangent, gain_two, bias_two,
    )

    def pass_on(rows_there, order):
        by_side, by_low = call(
            halves, "halves", after(place, order), [whole(v) for v in rows_there[1:]],
            [res((rows // 2, width), low)] * 2,
        )
        return [low_swap(by_side), side_swap(by_low)]

    normed_all += pass_on(normed_all, grad_low)
    grad_all = spread(grad_low)
    group = width // 2
    grad_first, branch_low, mine, other, sums, stats = pl.pallas_call(
        feed_back,
        grid_spec=pltpu.PrefetchScalarGridSpec(
            num_scalar_prefetch=1,
            grid=(1,),
            in_specs=[
                block((rows, width)), block((rows, width)),
                inside, inside, inside, inside, inside, block((width, width)),
                block((rows, width)), block((rows, TILE)), block((width,)), block((2, width)), block((rows, width)),
                block((16, rows)),
            ],
            out_specs=[
                block((rows, width)), block((rows, width)), block((rows, group)), block((rows + 80, group)),
                block((8, width)), block((16, rows)),
            ],
            scratch_shapes=[pltpu.VMEM((rows, width), full)],
        ),
        out_shape=[
            shaped((rows, width), full), shaped((rows, width), low), shaped((rows, group), low),
            shaped((rows + 80, group), low), shaped((8, width), full),
            shaped((16, rows), full),
        ],
        compiler_params=pltpu.CompilerParams(
            vmem_limit_bytes=14 * MIB, dimension_semantics=("arbitrary",)
        ),
        cost_estimate=took("feed_back"),
        name="feed_back",
    )(
        place, grad_second, grad_low, slope_up, slope_gate, gate_weight, up_weight, down_weight,
        output_weight, scaled, inverse, gain_one, sums_two, attended_low, logs,
    )
    far_grad = side_swap(other)
    grad_all += pass_on(grad_all, sums)
    quarter = width // 4
    quarter = width // 4
    out_keep, out_send = call(
        out_grad, "out_grad", after(place, sums), [whole(branch_low), whole(attended_low)],
        [res((2 * quarter, width), full), res((2 * quarter, width), low)],
        [pltpu.VMEM((width, width), full)],
    )
    out_got = core_swap(out_send)

    of_side = lambda v: (v, block((v.shape[0], group), 0, lambda place: place[SIDE]))
    heads_of = [
        whole(tokens), whole(near), whole(far), whole(far_near), of_side(near_keys), of_side(far_keys),
        of_side(near_values), of_side(far_values), of_side(query), whole(far_query), whole(mine),
        whole(far_grad), whole(cosine), whole(sine), whole(seg_col), whole(seg_row), whole(stats),
    ]

    def back_one(tile, order):
        return call(
            functools.partial(back_some, (tile,), True), "back_one", order, heads_of,
            [res((two, TILE), low), res((window, 2 * TILE), low), res((3 * TILE, width), full)],
            [pltpu.VMEM((window, two), full)],
            mib=32,
        )

    eighth = hidden // 8
    eighth_of = lambda value, owner: (
        still(value),
        block((width, eighth), 0, lambda place: place[owner])
        if value.shape[0] == width
        else block((eighth, width), lambda place: place[owner], 0),
    )

    *begun, wgu = call(
        column_start, "column_start", after(place, out_keep),
        [whole(v) for v in normed_all[:3]] + [eighth_of(gate_weight, OTHER), eighth_of(up_weight, OTHER)],
        [res((eighth, 3 * rows), low)] * 3 + [res((2 * eighth, width), low)],
        mib=24,
    )
    back_first = back_one(0, after(place, wgu, grad_all[1], grad_all[2]))

    def columns(owner, order, last, *more):
        half_of = [res((width // 2, wide), kind) for kind in (full, low) for wide in (2 * eighth, eighth)]
        return call(
            functools.partial(column_grads, last), "column_grads", order,
            [whole(v) for v in normed_all] + [whole(v) for v in grad_all] + list(more),
            half_of if last else [res((width, 3 * eighth), low)],
            ([pltpu.VMEM((2 * eighth, width), low)] if last else [])
            + [pltpu.VMEM((3 * eighth, width), full)]
            + ([pltpu.VMEM((width, eighth), full)] if last else []),
            mib=36,
        )

    out_keep, out_send = call(
        out_halve, "out_halve", after(place, back_first[0]), [whole(out_keep), whole(out_got)],
        [res((quarter, width), full), res((quarter, width), low)],
    )
    out_got = side_swap(out_send)
    (col_part,) = columns(
        OTHER, after(place, out_keep), False, whole(wgu), eighth_of(down_weight, OTHER), *[whole(v) for v in begun]
    )
    col_got = core_swap(col_part)
    back_second = back_one(1, after(place, col_part))
    col_keep, down_keep, col_send, down_send = columns(
        OWN, after(place, back_second[0]), True, eighth_of(gate_weight, OWN), eighth_of(up_weight, OWN),
        eighth_of(down_weight, OWN), whole(col_got),
    )
    col_got = x_swap(col_send)
    down_got = x_swap(down_send)
    dq, even, odd_near, odd_far, grads = call(
        functools.partial(back_some, (2,), False), "back_rest", after(place, col_keep, out_got),
        heads_of + [whole(v) for v in back_first + back_second],
        [res((two, group), low), res((two, width), low), res((rows, width), low), res((rows, width), low),
         res((3 * group, width), full)],
        [pltpu.VMEM((window, two), full), pltpu.VMEM((window, width), low)],
        mib=36,
    )
    in_keep, in_send, odd_near, odd_far, sums = call(
        fold, "fold", after(place, down_got),
        [whole(grads), whole(far_grad), whole(sums), whole(odd_near), whole(odd_far)],
        [res((3 * quarter, width), full), res((3 * quarter + 16, width), low), res((rows, width), low),
         res((rows, width), low), res((8, width), full)],
    )
    in_got = core_swap(in_send)
    odd_near, odd_far = core_swap(odd_near), core_swap(odd_far)
    down_keep, down_send = call(
        second_split, "second_split", after(place, sums), [whole(down_keep), whole(down_got)],
        [res((width // 4, eighth), full), res((width // 4, eighth), low)],
    )
    down_got = swap(down_send, "dp", 4)

    share = width // n_data
    keep, send, sums = call(
        turn_over, "turn_over", after(place, down_keep),
        [whole(in_keep), whole(in_got), whole(out_keep), whole(out_got), whole(sums)],
        [res((4 * share, width), full), res((4 * share + 16, width), low), res((8, width), full)],
        [pltpu.VMEM((width, width), full)],
        mib=24,
    )
    got = low_swap(send)
    (far_send,) = call(
        far_pack, "far_pack", after(place, sums), [whole(dq), whole(even), whole(odd_far)],
        [res((rows, 3 * group), low)],
    )
    far_part = side_swap(far_send)
    col_keep, col_send = call(
        second_split, "second_split", after(place, far_send), [whole(col_keep), whole(col_got)],
        [res((width // 4, 2 * eighth), full), res((width // 4, 2 * eighth), low)],
    )
    col_got = swap(col_send, "dp", 4)
    keep, send, sums = call(
        halve_x, "halve_x", after(place, col_keep),
        [whole(keep), whole(got), whole(sums)],
        [res((2 * share, width), full), res((2 * share + 16, width), low), res((8, width), full)],
    )
    got = x_swap(send)
    weight_at = lambda i, own: (
        still(input_weight),
        block((width, group), 0, lambda place: 2 * i + (place[SIDE] if own else 1 - place[SIDE])),
    )
    (grad_tokens,) = call(
        token_grad, "token_grad", after(place, sums),
        [whole(grad_first), whole(dq), whole(even), whole(odd_near), whole(far_part)]
        + [weight_at(i, True) for i in range(3)] + [weight_at(i, False) for i in range(3)],
        [res((rows, width), low)],
        mib=24,
    )
    order = []
    for d in range(n_data):
        for s in range(n_seq):
            order.append((d * n_seq + s, (2 * s + d // 2 % 2) * n_seq + d // 4 * 2 + d % 2))
    (down,) = call(
        down_sum, "down_sum", after(place, grad_tokens), [whole(down_keep), whole(down_got)],
        [res((width // 4, eighth), low)],
    )
    down_got = lax.ppermute(down, ("dp", "seq"), order)
    keep, send, sums = call(
        halve, "halve", after(place, down), [whole(keep), whole(got), whole(sums)],
        [res((share, width), full), res((share + 16, width), low), res((8, width), full)],
    )
    got = swap(send, "dp", 4)
    pair_kept, pair_send = call(
        pair_sum, "pair_sum", after(place, sums), [whole(col_keep), whole(col_got)],
        [res((share, 2 * eighth), full), res((share, 2 * eighth), low)],
    )
    pair_got = low_swap(pair_send)
    in_own, in_send, grad_out, *vectors = call(
        last_sum, "last_sum", after(place, pair_send), [whole(keep), whole(got), whole(sums)],
        [res((share, 2 * quarter), full), res((share, quarter), low), res((share, quarter), full)]
        + [res((width,), full)] * 4,
    )
    in_moved = side_swap(in_send)
    grad_gate, grad_up = call(
        pair_place, "pair_place", after(place, in_send), [whole(pair_kept), whole(pair_got)],
        [res((share, 2 * eighth), full), res((share, 2 * eighth), full)],
    )
    (grad_in,) = call(
        in_place, "in_place", after(place, grad_gate), [whole(in_own), whole(in_moved)],
        [res((share, 3 * quarter), full)],
    )
    return (
        result,
        grad_tokens,
        grad_in,
        grad_out,
        grad_gate,
        grad_up,
        down_got.astype(full).T,
        *vectors,
    )


def solution(mesh):
    placed = (
        P(("dp", "seq"), None),
        P(("dp", "seq"), None),
        P("dp", None),
        P(),
        P(),
        P(),
        P(),
        P(),
        P(),
        P(),
        P(),
        P(),
    )
    paired = mesh.shape["seq"] == 4 and mesh.shape["dp"] == 8
    return jax.shard_map(
        fast if paired else general,
        mesh=mesh,
        in_specs=placed,
        out_specs=(
            P(("dp", "seq"), None),
            P(("dp", "seq"), None),
            P("dp", "seq"),
            P("dp", "seq"),
            P("dp", "seq"),
            P("dp", "seq"),
            P("dp", "seq"),
            P(),
            P(),
            P(),
            P(),
        ),
        check_vma=False,
    )
```
